32 devices in a mesh: ctx: 8 (over y, x, core), fsdp: 4 (over z).
Axes of the slice: x: 2, y: 2, z: 4, core: 2. Of those that a mesh axis runs over, the one named last changes fastest.
Arguments:
- inputs: bfloat16 [8, 1024, 2048], P('fsdp', 'ctx'), may hold values from -6 to 6
- positions: int32 [8, 1024], P('fsdp'), may hold values from 0 to 1023, as said below
- first_gain: float32 [2048], replicated, may hold values from 0.5 to 1.5
- attention_weight: bfloat16 [2048, 6144], P('fsdp'), may hold values from -0.125 to 0.125
- output_weight: bfloat16 [2048, 2048], P('fsdp'), may hold values from -2 to 2
- second_gain: float32 [2048], replicated, may hold values from 0.5 to 1.5
- gate_up_weight: bfloat16 [2048, 16384], P('fsdp'), may hold values from -0.125 to 0.125
- down_weight: bfloat16 [2048, 8192], P('fsdp'), may hold values from -0.0625 to 0.0625
- cotangent: bfloat16 [8, 1024, 2048], P('fsdp', 'ctx'), may hold values from -6 to 6
Outputs:
- output: float32 [8, 1024, 2048], P('fsdp', 'ctx')
- grad_input: float32 [8, 1024, 2048], P('fsdp', 'ctx')
- grad_attention: float32 [2048, 6144], P(('ctx', 'fsdp'))
- grad_output_weight: float32 [2048, 2048], P(('ctx', 'fsdp'))
- grad_gate_up: float32 [2048, 16384], P(('ctx', 'fsdp'))
- grad_down: float32 [2048, 8192], P(('ctx', 'fsdp'))
- grad_first_gain: float32 [2048], P(('ctx', 'fsdp'))
- grad_second_gain: float32 [2048], P(('ctx', 'fsdp'))
The draws below stay inside these ranges and needn't reach their ends.
Inputs may be any that keep to these rules, and one draw needn't show every extreme that they name: Each row holds every position of its sequence once. Entries [c * 2 * 64, (c + 1) * 2 * 64) of a row hold two runs of 64 consecutive positions, blocks b and 15 - b (block b starts at b * 64), in either order; which pair lies where is drawn for each sequence.
All inputs are finite; a program needn't handle non-finite values.
Results may differ from the reference program's by a relative error of at most 0.015.
Values may be sent and summed in bfloat16 or wider, within the bound.
A program may use at most 896 MiB of HBM per device.

```python
import jax
import jax.numpy as jnp
from jax import lax

D = 2048
HEADS = 32
HEAD_DIM = 64
FF = 8192
BLOCK = 64
LENGTH = 1024
SEQS_ALL = 8


def draw_positions(key, part):
    key = jax.random.fold_in(key, 7)
    pairs = LENGTH // (2 * BLOCK)
    first_key, second_key = jax.random.split(key)
    orders = jax.vmap(lambda single: jax.random.permutation(single, pairs))(jax.random.split(first_key, SEQS_ALL))
    flips = jax.random.randint(second_key, (SEQS_ALL, pairs), 0, 2)
    mirrored = 2 * pairs - 1 - orders
    leading = jnp.where(flips == 1, mirrored, orders)
    trailing = 2 * pairs - 1 - leading
    blocks = jnp.stack([leading, trailing], axis=-1).reshape(SEQS_ALL, 2 * pairs)
    places = blocks[:, :, None] * BLOCK + jnp.arange(BLOCK, dtype=jnp.int32)[None, None, :]
    return places.reshape(SEQS_ALL, LENGTH).astype(jnp.int32)


def strengthened(array, own_key, source, target, blocks, factor):
    owner, partner = [(jnp.arange(array.shape[position]) // (array.shape[position] // blocks)).reshape([-1 if axis == position else 1 for axis in range(array.ndim)]) for position in (source, target)]
    chosen = jax.random.permutation(own_key, blocks)[partner]
    strong = (owner == chosen) | (owner == (partner + blocks // 2) % blocks)
    return jnp.where(strong, factor * array, array)


def levels(own_key, extent, pieces, least, top_value):
    loudness = 1.0
    for position, shards_of in pieces:
        heights = jax.random.uniform(jax.random.fold_in(jax.random.fold_in(own_key, 6), position), (shards_of,), jnp.float32, least / len(pieces), top_value / len(pieces))
        loudness = loudness * jnp.repeat(jnp.exp(heights), extent[position] // shards_of).reshape((-1,) + (1,) * (len(extent) - 1 - position))
    return loudness


def centred(own_key, extent, width, bound, cuts=(), kind=jnp.bfloat16):
    array = jax.random.normal(own_key, extent, jnp.float32) * width
    if len(cuts) > 0:
        array = levels(own_key, extent, cuts, -0.22, 0.18) * array
    return jnp.clip(array, min=-bound, max=bound).astype(kind)


def bell_draw_with(key, shape, spread, limit, cuts, heavy, kind=jnp.bfloat16):
    array = spread * jax.random.normal(key, shape, jnp.float32)
    if cuts:
        array = array * levels(key, shape, cuts, -0.22, 0.18)
    return jnp.clip(strengthened(array, jax.random.fold_in(key, 3), *heavy), -limit, limit).astype(kind)


def setup_inputs(seed: int = 0) -> dict:
    seeds = jax.random.split(jax.random.key(seed), 10)
    return {
        "inputs": bell_draw_with(seeds[0], (SEQS_ALL, LENGTH, D), 1.0, 6.0, ((0, 4), (1, 8)), (1, 2, 8, 2.0)),
        "positions": draw_positions(jax.random.fold_in(seeds[9], 71), 0),
        "first_gain": jnp.clip(1.0 + 0.1 * jax.random.normal(seeds[2], (D,), jnp.float32), 0.5, 1.5),
        "attention_weight": centred(seeds[3], (D, 3 * D), D ** -0.5, 0.125, ((0, 4),)),
        "output_weight": centred(seeds[4], (D, D), (max(1, D // 256)) ** -0.5, 2.0, ((0, 4),)),
        "second_gain": jnp.clip(1.0 + 0.1 * jax.random.normal(seeds[5], (D,), jnp.float32), 0.5, 1.5),
        "gate_up_weight": centred(seeds[6], (D, 2 * FF), D ** -0.5, 0.125, ((0, 4),)),
        "down_weight": centred(seeds[7], (D, FF), FF ** -0.5, 0.0625, ((0, 4),)),
        "cotangent": bell_draw_with(seeds[8], (SEQS_ALL, LENGTH, D), 1.0, 6.0, ((0, 4), (1, 8)), (1, 2, 8, 2.0)),
    }


precise = lax.Precision.HIGHEST
epsilon = 1e-05
rope_base = 130000.0

@jax.custom_vjp
def low(v):
    return lax.optimization_barrier(v.astype(jnp.bfloat16)).astype(jnp.float32)

@jax.custom_vjp
def low_back(v):
    return v

def low_keep(v):
    return (low(v), None)

def low_pass(kept, grad):
    return (grad,)

def back_keep(v):
    return (v, None)

def back_low(kept, grad):
    return (low(grad),)
low.defvjp(low_keep, low_pass)
low_back.defvjp(back_keep, back_low)

def rms_scale(values):
    return lax.rsqrt(lax.optimization_barrier(jnp.mean(values * values, axis=-1, keepdims=True)) + epsilon)

def rope_tables(places, head_size):
    halves = jnp.arange(head_size // 2, dtype=jnp.float32)
    inverse = jnp.exp(-(2.0 * halves / head_size) * jnp.log(jnp.float32(rope_base)))
    angles = places.astype(jnp.float32)[..., None] * inverse
    angles = jnp.concatenate([angles, angles], axis=-1)
    return (jnp.cos(angles), jnp.sin(angles))

def rotate(values, cosine_table, sine_table):
    half_size = values.shape[-1] // 2
    turned = jnp.concatenate([-values[..., half_size:], values[..., :half_size]], axis=-1)
    return values * cosine_table + turned * sine_table

def attend_sequence(operands):
    queries, key_rows, value_rows, places = operands
    length = queries.shape[0]
    block_rows = min(512, length)
    score_scale = queries.shape[-1] ** (-0.5)

    def one_block(block_index):
        offset = (block_index * block_rows).astype(jnp.int32)
        query_part = lax.dynamic_slice_in_dim(queries, offset, block_rows, 0)
        query_place = lax.dynamic_slice_in_dim(places, offset, block_rows, 0)
        scores = low_back(jnp.einsum('qhd,khd->hqk', query_part, key_rows, precision=precise) * score_scale)
        allowed = places[None, None, :] <= query_place[None, :, None]
        masked = jnp.where(allowed, scores, -1e+30)
        log_total = jax.nn.logsumexp(masked, axis=-1, keepdims=True)
        probs_low = low(jnp.where(allowed, jnp.exp(masked - log_total), 0.0))
        return jnp.einsum('hqk,khd->qhd', probs_low, value_rows, precision=precise)
    blocks = lax.map(jax.checkpoint(one_block), jnp.arange(length // block_rows, dtype=jnp.int32))
    return blocks.reshape(queries.shape)

def apply_layer(inputs, first_gain, attention_weight, output_weight, second_gain, gate_up_weight, down_weight, places):
    sequences, length, model_width = inputs.shape
    flattened = inputs.reshape(-1, model_width)
    normed_low = low(flattened * rms_scale(flattened) * first_gain)
    projected = low_back(jnp.dot(normed_low, attention_weight, precision=precise))
    cosine_table, sine_table = rope_tables(places, HEAD_DIM)
    cosine_table = cosine_table[:, :, None, :]
    sine_table = sine_table[:, :, None, :]

    def part_heads(index_part):
        return projected[:, index_part * model_width:(index_part + 1) * model_width].reshape(sequences, length, HEADS, HEAD_DIM)
    queries = low(rotate(part_heads(0), cosine_table, sine_table))
    key_rows = low(rotate(part_heads(1), cosine_table, sine_table))
    value_rows = low(part_heads(2))
    attended = lax.map(jax.checkpoint(attend_sequence), (queries, key_rows, value_rows, places))
    attended_low = low(low_back(attended.reshape(-1, model_width)))
    residual = flattened + low_back(jnp.dot(attended_low, output_weight, precision=precise))
    second_low = low(residual * rms_scale(residual) * second_gain)
    gate_up = low_back(jnp.dot(second_low, gate_up_weight, precision=precise))
    hidden = low(jax.nn.silu(gate_up[:, :FF]) * gate_up[:, FF:])
    output = residual + jnp.dot(hidden, down_weight.T, precision=precise)
    return output.reshape(sequences, length, model_width)

def reference(inputs, positions, first_gain, attention_weight, output_weight, second_gain, gate_up_weight, down_weight, cotangent):

    def layer_of(*weights):
        return apply_layer(*weights, positions)
    output, pullback = jax.vjp(layer_of, inputs.astype(jnp.float32), first_gain.astype(jnp.float32), attention_weight.astype(jnp.float32), output_weight.astype(jnp.float32), second_gain.astype(jnp.float32), gate_up_weight.astype(jnp.float32), down_weight.astype(jnp.float32))
    gradient = pullback(cotangent.astype(jnp.float32))
    return (output, gradient[0], gradient[2], gradient[3], gradient[5], gradient[6], gradient[1], gradient[4])
```

```python
import functools

import jax
import jax.numpy as jnp
from jax import lax
from jax.experimental import pallas as pl
from jax.experimental.pallas import tpu as pltpu
from jax.sharding import PartitionSpec as P

HEAD_SIZE = 64
EPSILON = 1e-05
ROPE_BASE = 130000.0
CHUNKS = 4

f32 = jnp.float32
bf16 = jnp.bfloat16


def rms_scale(values):
    return lax.rsqrt(jnp.mean(values * values, axis=-1, keepdims=True) + EPSILON)


def dot(left, right):
    return jnp.dot(left, right, preferred_element_type=f32)


def dot_rows(left, right):
    return lax.dot_general(left, right, (((1,), (1,)), ((), ())), preferred_element_type=f32)


def dot_tokens(left, right):
    return lax.dot_general(left, right, (((0,), (0,)), ((), ())), preferred_element_type=f32)


def rope_tables(places, lanes):
    half = HEAD_SIZE // 2
    halves = jnp.arange(half, dtype=f32)
    inverse = jnp.exp(-(2.0 * halves / HEAD_SIZE) * jnp.log(f32(ROPE_BASE)))
    angles = places.astype(f32)[..., None] * inverse
    copies = lanes // half
    return jnp.tile(jnp.cos(angles), copies), jnp.tile(jnp.sin(angles), copies)


def first_half(lanes):
    return (jnp.arange(lanes) % HEAD_SIZE) < HEAD_SIZE // 2


def rotate(values, cosine, sine):
    half = HEAD_SIZE // 2
    turned = jnp.where(
        first_half(values.shape[-1]), -jnp.roll(values, -half, -1), jnp.roll(values, half, -1)
    )
    return values * cosine + turned * sine


def rotate_back(gradient, cosine, sine):
    half = HEAD_SIZE // 2
    scaled = gradient * sine
    turned = jnp.where(
        first_half(gradient.shape[-1]), jnp.roll(scaled, -half, -1), -jnp.roll(scaled, half, -1)
    )
    return gradient * cosine + turned


class Plane:
    def __init__(self, size):
        self.size = size
        self.relative = size == 8

    def swap(self, value, bits):
        return lax.ppermute(value, "ctx", [(i, i ^ bits) for i in range(self.size)])

    def gather(self, own):
        if not self.relative:
            whole = lax.all_gather(own, "ctx", axis=1, tiled=False)
            s, n, r, d = whole.shape
            return whole.reshape(s, n // 2, 2, r, d).transpose(2, 0, 1, 3, 4)
        by_x, by_y = self.swap(own, 2), self.swap(own, 4)
        half = own.shape[0] // 2
        far_one, far_two = self.swap(by_x[:half], 4), self.swap(by_y[half:], 2)
        even = [own, by_x, by_y, jnp.concatenate([far_one, far_two], axis=0)]
        odd = [self.swap(part, 1) for part in even]
        return jnp.stack([jnp.stack(even, axis=1), jnp.stack(odd, axis=1)])

    def scatter(self, odd, even):
        if not self.relative:
            both = jnp.stack([even, odd], axis=2)
            s, q, p, r, d = both.shape
            return lax.psum_scatter(
                both.reshape(s, q * p, r, d), "ctx", scatter_dimension=1, tiled=False
            ).astype(f32)
        half = odd.shape[0] // 2
        came = self.swap(odd, 1)
        both = (even.astype(f32) + came.astype(f32)).astype(bf16)
        far_x, far_y = self.swap(both[:half, 3], 2), self.swap(both[half:, 3], 4)
        direct_x, direct_y = self.swap(both[:half, 1], 2), self.swap(both[half:, 2], 4)
        to_x = (both[half:, 1].astype(f32) + far_y.astype(f32)).astype(bf16)
        to_y = (both[:half, 2].astype(f32) + far_x.astype(f32)).astype(bf16)
        later_x, later_y = self.swap(to_x, 2), self.swap(to_y, 4)
        from_x = jnp.concatenate([direct_x, later_x], axis=0).astype(f32)
        from_y = jnp.concatenate([later_y, direct_y], axis=0).astype(f32)
        return both[:, 0].astype(f32) + from_x + from_y

    def order(self, places):
        s, n, r = places.shape
        if self.relative:
            me = lax.axis_index("ctx")
            bits = places.reshape(s, 2, 2, 2, r)
            for axis, bit in ((1, 4), (2, 2), (3, 1)):
                bits = jnp.where((me & bit) != 0, jnp.flip(bits, axis), bits)
            places = bits.reshape(s, n, r)
        return places.reshape(s, n // 2, 2, r).transpose(2, 0, 1, 3)

    def gather_columns(self, own, rows):
        if not self.relative:
            return lax.all_gather(own, "ctx", axis=1, tiled=True)
        tokens, width = own.shape
        me = lax.axis_index("ctx")
        half = tokens // 2

        def swap(part, bits):
            part = self.swap(part, bits)
            laid = part.reshape(-1, 4 * rows // 2, width) if bits == 4 else part.reshape(-1, rows, width)
            if bits == 1:
                return jnp.concatenate([part[half:], part[:half]], axis=0)
            laid = laid.reshape(-1, 2, laid.shape[1], width)
            return jnp.stack([laid[:, 1], laid[:, 0]], axis=1).reshape(part.shape)

        by_x, by_y = swap(own, 2), swap(own, 4)
        far_one, far_two = swap(by_x[:half], 4), swap(by_y[half:], 2)
        even = [own, by_x, by_y, jnp.concatenate([far_one, far_two], axis=0)]
        odd = [swap(part, 1) for part in even]
        whole = jnp.zeros((tokens, self.size * width), own.dtype)
        for place, part in enumerate(even):
            whole = lax.dynamic_update_slice(whole, part, (0, (me ^ (2 * place)) * width))
        for place, part in enumerate(odd):
            whole = lax.dynamic_update_slice(whole, part, (0, (me ^ (2 * place + 1)) * width))
        return whole


def gather_rows(own):
    z = lax.axis_index("fsdp")
    one = lax.ppermute(own, "fsdp", [(i, (i + 1) % 4) for i in range(4)])
    three = lax.ppermute(own, "fsdp", [(i, (i + 3) % 4) for i in range(4)])
    sent = jnp.where(z == 2, one, jnp.where(z == 1, three, own))
    two = lax.ppermute(sent, "fsdp", [(0, 2), (3, 1), (2, 3), (1, 0)])
    rows = own.shape[0]
    whole = jnp.zeros((4 * rows, own.shape[1]), own.dtype)
    for shift, part in enumerate((own, one, two, three)):
        whole = lax.dynamic_update_slice(whole, part, (((z - shift) % 4) * rows, 0))
    return whole


def sum_rows(partial, plane):
    depth, columns = partial.shape
    n = plane.size
    rows = depth // (4 * n)
    laid = partial.astype(bf16).reshape(n, 4, rows, columns).transpose(1, 0, 2, 3)
    mine = lax.psum_scatter(
        laid.reshape(depth, columns), "fsdp", scatter_dimension=0, tiled=True
    ).reshape(n, rows, columns)
    return lax.all_to_all(mine, "ctx", split_axis=0, concat_axis=0, tiled=True)


def head_lanes(shape, head):
    lane = lax.broadcasted_iota(jnp.int32, shape, 1)
    return (lane >= head * HEAD_SIZE) & (lane < (head + 1) * HEAD_SIZE)


def only(values, head, heads):
    if heads == 1:
        return values
    return jnp.where(head_lanes(values.shape, head), values, jnp.zeros_like(values))


def forward_kernel(heads, q_spot, k_spot, q_ref, k_ref, v_ref, out_ref, low_ref, total_ref):
    lanes = q_ref.shape[-1]
    queries = q_ref[0, 0] * bf16(HEAD_SIZE**-0.5)
    keys = k_ref[:, 0].reshape(-1, lanes)
    values = v_ref[:, 0].reshape(-1, lanes)
    allowed = k_spot[0] <= q_spot[0, 0]
    attended = jnp.zeros(queries.shape, f32)
    for head in range(heads):
        scores = dot_rows(keys, only(queries, head, heads))
        scores = jnp.where(allowed, scores, -1e30)
        highest = jnp.max(scores, axis=0, keepdims=True)
        raised = jnp.exp(scores - highest)
        summed = jnp.sum(raised, axis=0, keepdims=True)
        probs = (raised * (1.0 / summed)).astype(bf16)
        total_ref[0, 0, head : head + 1, :] = highest + jnp.log(summed)
        attended += dot_tokens(probs, only(values, head, heads))
    out_ref[0, 0] = attended
    low_ref[0, 0] = attended.astype(bf16)


def backward_kernel(
    heads, q_spot, k_spot, q_ref, k_ref, v_ref, grad_ref, total_ref, delta_ref, dq_ref, dk_ref, dv_ref
):
    lanes = q_ref.shape[-1]
    scale = HEAD_SIZE**-0.5

    @pl.when((pl.program_id(1) == 0) & (pl.program_id(2) == 0))
    def _():
        dk_ref[...] = jnp.zeros_like(dk_ref)
        dv_ref[...] = jnp.zeros_like(dv_ref)

    queries = q_ref[0, 0] * bf16(scale)
    grads = grad_ref[0, 0]
    keys = k_ref[:, 0].reshape(-1, lanes)
    values = v_ref[:, 0].reshape(-1, lanes)
    allowed = k_spot[0] <= q_spot[0, 0]
    grad_q = jnp.zeros(queries.shape, f32)
    grad_k = jnp.zeros(keys.shape, f32)
    grad_v = jnp.zeros(keys.shape, f32)
    for head in range(heads):
        query = only(queries, head, heads)
        grad = only(grads, head, heads)
        scores = jnp.where(allowed, dot_rows(keys, query), -1e30)
        probs = jnp.exp(scores - total_ref[0, 0, head : head + 1, :])
        grad_v += dot(probs.astype(bf16), grad)
        grad_probs = dot_rows(values, grad)
        grad_scores = (probs * (grad_probs - delta_ref[0, 0, head : head + 1, :])).astype(bf16)
        grad_k += dot(grad_scores, query)
        grad_q += dot_tokens(grad_scores, only(keys, head, heads))
    dq_ref[0, 0] = grad_q * scale
    shape = dk_ref.shape
    dk_ref[...] += grad_k.reshape(shape)
    dv_ref[...] += grad_v.reshape(shape)


def attention_specs(shape, heads):
    p, s, rows, lanes = shape
    tile = min(256, rows)
    one = pl.BlockSpec((1, 1, tile, lanes), lambda i, j, t: (j, i, t, 0))
    side = pl.BlockSpec((p, 1, rows, lanes), lambda i, j, t: (0, i, 0, 0))
    stat = pl.BlockSpec((1, 1, heads, tile), lambda i, j, t: (j, i, 0, t))
    q_spot = pl.BlockSpec((1, 1, 1, tile), lambda i, j, t: (j, i, 0, t))
    k_spot = pl.BlockSpec((1, p * rows, 1), lambda i, j, t: (i, 0, 0))
    return (s, p, rows // tile), one, side, stat, q_spot, k_spot


PARAMS = pltpu.CompilerParams(vmem_limit_bytes=48 * 1024 * 1024)


def attend(q_spot, k_spot, queries, keys, values):
    p, s, rows, lanes = queries.shape
    heads = lanes // HEAD_SIZE
    grid, one, side, stat, q_spec, k_spec = attention_specs(queries.shape, heads)
    pairs = p * rows * s * p * rows
    return pl.pallas_call(
        functools.partial(forward_kernel, heads),
        grid=grid,
        in_specs=[q_spec, k_spec, one, side, side],
        out_specs=[one, one, stat],
        out_shape=[
            jax.ShapeDtypeStruct(queries.shape, f32),
            jax.ShapeDtypeStruct(queries.shape, bf16),
            jax.ShapeDtypeStruct((p, s, heads, rows), f32),
        ],
        compiler_params=PARAMS,
        cost_estimate=pl.CostEstimate(
            flops=pairs * heads * 1024, bytes_accessed=queries.size * 14, transcendentals=pairs * heads
        ),
    )(q_spot, k_spot, queries, keys, values)


def attend_back(q_spot, k_spot, queries, keys, values, grads, totals, deltas):
    p, s, rows, lanes = queries.shape
    heads = lanes // HEAD_SIZE
    grid, one, side, stat, q_spec, k_spec = attention_specs(queries.shape, heads)
    pairs = p * rows * s * p * rows
    return pl.pallas_call(
        functools.partial(backward_kernel, heads),
        grid=grid,
        in_specs=[q_spec, k_spec, one, side, side, one, stat, stat],
        out_specs=[one, side, side],
        out_shape=[jax.ShapeDtypeStruct(queries.shape, f32)] * 3,
        compiler_params=PARAMS,
        cost_estimate=pl.CostEstimate(
            flops=pairs * heads * 2560, bytes_accessed=queries.size * 20, transcendentals=pairs * heads
        ),
    )(q_spot, k_spot, queries, keys, values, grads, totals, deltas)


def on_device(
    plane,
    inputs,
    positions,
    first_gain,
    attention_weight,
    output_weight,
    second_gain,
    gate_up_weight,
    down_weight,
    cotangent,
):
    s, r, d = inputs.shape
    n = plane.size
    ff = down_weight.shape[1]
    me = lax.axis_index("ctx")
    lanes = d // n
    mine = ff // n
    tokens = s * r * n
    group = (2, s, n // 2 * r)

    def columns(weight, start, width):
        return lax.dynamic_slice_in_dim(weight, start, width, 1)

    qkv = jnp.concatenate(
        [columns(attention_weight, part * d + me * lanes, lanes) for part in range(3)], axis=1
    )
    qkv_whole = gather_rows(qkv)
    out_whole = lax.all_gather(
        gather_rows(columns(output_weight, me * lanes, lanes)), "ctx", axis=1, tiled=True
    )
    step = mine // CHUNKS
    ffn = []
    for chunk in range(CHUNKS):
        start = me * mine + chunk * step
        ffn.append(
            gather_rows(
                jnp.concatenate(
                    [
                        columns(gate_up_weight, start, step),
                        columns(gate_up_weight, ff + start, step),
                        columns(down_weight, start, step),
                    ],
                    axis=1,
                )
            )
        )

    whole_inputs = plane.gather(inputs).reshape(tokens, d)
    flat_inputs = whole_inputs.astype(f32)
    normed_low = (flat_inputs * rms_scale(flat_inputs) * first_gain).astype(bf16)
    projected = dot(normed_low, qkv_whole)
    places = plane.order(positions.reshape(s, n, r)).reshape(group)
    q_spot = places[:, :, None, :]
    k_spot = places.transpose(1, 0, 2).reshape(s, n * r, 1)
    cosine, sine = rope_tables(places.reshape(tokens), lanes)
    queries = rotate(projected[:, :lanes], cosine, sine).astype(bf16).reshape(*group, lanes)
    keys = rotate(projected[:, lanes : 2 * lanes], cosine, sine).astype(bf16).reshape(*group, lanes)
    values = projected[:, 2 * lanes :].astype(bf16).reshape(*group, lanes)
    attended, attended_low, totals = attend(q_spot, k_spot, queries, keys, values)
    attended_low = attended_low.reshape(tokens, lanes)
    attended_whole = plane.gather_columns(attended_low, r)
    residual_whole = flat_inputs + dot(attended_whole, out_whole)
    second_low = (residual_whole * rms_scale(residual_whole) * second_gain).astype(bf16)
    residual = residual_whole.reshape(2, s, n // 2, r, d)
    if plane.relative:
        residual = residual[0, :, 0]
    else:
        residual = lax.dynamic_index_in_dim(
            lax.dynamic_index_in_dim(residual, me % 2, 0, keepdims=False), me // 2, 1, keepdims=False
        )

    cot = plane.gather(cotangent).reshape(tokens, d)
    hiddens, grads, sums = [], [], []
    for weight in ffn:
        gate_up = dot(second_low, weight[:, : 2 * step])
        grad_hidden = dot(cot, weight[:, 2 * step :])
        gate, upward = gate_up[:, :step], gate_up[:, step:]
        sigmoid = jax.nn.sigmoid(gate)
        hidden = (gate * sigmoid * upward).astype(bf16)
        grad_gate_up = jnp.concatenate(
            [
                grad_hidden * upward * sigmoid * (1.0 + gate * (1.0 - sigmoid)),
                grad_hidden * gate * sigmoid,
            ],
            axis=1,
        ).astype(bf16)
        hiddens.append(hidden)
        grads.append(grad_gate_up)
        partial = jnp.concatenate(
            [dot_tokens(second_low, grad_gate_up), dot_tokens(cot, hidden)], axis=1
        )
        sums.append(sum_rows(partial, plane))

    def by_parity(lefts, rights):
        left = jnp.concatenate(lefts, axis=1)
        right = jnp.concatenate(rights, axis=1)
        half = tokens // 2
        odd = dot_rows(left[half:], right).astype(bf16)
        even = dot_rows(left[:half], right).astype(bf16)
        shape = (s, n // 2, r, d)
        return plane.scatter(odd.reshape(shape), even.reshape(shape))

    grad_second = by_parity(grads, [weight[:, : 2 * step] for weight in ffn])
    output = residual + by_parity(hiddens, [weight[:, 2 * step :] for weight in ffn])

    scale_two = rms_scale(residual)
    weighted = second_gain * grad_second
    second_gain_part = jnp.sum(grad_second * residual * scale_two, axis=(0, 1))
    grad_residual = (
        cotangent.astype(f32)
        + scale_two * weighted
        - residual
        * (scale_two * scale_two * scale_two)
        * jnp.mean(weighted * residual, axis=-1, keepdims=True)
    )
    grad_low = plane.gather(grad_residual.astype(bf16)).reshape(tokens, d)

    out_rows = lax.dynamic_slice_in_dim(out_whole, me * lanes, lanes, 0)
    grad_attended = dot_rows(grad_low, out_rows).astype(bf16)
    out_part = dot_tokens(attended_low, grad_low).astype(bf16)
    grad_output_weight = lax.psum_scatter(out_part, "fsdp", scatter_dimension=0, tiled=True)
    deltas = jnp.sum(
        (grad_attended.astype(f32) * attended.reshape(tokens, lanes)).reshape(
            *group, lanes // HEAD_SIZE, HEAD_SIZE
        ),
        axis=-1,
    ).transpose(0, 1, 3, 2)
    dq, dk, dv = attend_back(
        q_spot, k_spot, queries, keys, values, grad_attended.reshape(*group, lanes), totals, deltas
    )
    grad_projected = jnp.concatenate(
        [
            rotate_back(dq.reshape(tokens, lanes), cosine, sine),
            rotate_back(dk.reshape(tokens, lanes), cosine, sine),
            dv.reshape(tokens, lanes),
        ],
        axis=1,
    ).astype(bf16)
    grad_first = by_parity([grad_projected], [qkv_whole])
    attention_sums = sum_rows(dot_tokens(normed_low, grad_projected), plane)

    own = inputs.astype(f32)
    scale_one = rms_scale(own)
    weighted = first_gain * grad_first
    first_gain_part = jnp.sum(grad_first * own * scale_one, axis=(0, 1))
    grad_input = (
        grad_residual
        + scale_one * weighted
        - own
        * (scale_one * scale_one * scale_one)
        * jnp.mean(weighted * own, axis=-1, keepdims=True)
    )
    gains = lax.psum_scatter(
        jnp.stack([first_gain_part, second_gain_part], axis=1),
        ("ctx", "fsdp"),
        scatter_dimension=0,
        tiled=True,
    )

    rows = d // (4 * n)
    grad_attention = (
        attention_sums.reshape(n, rows, 3, lanes).transpose(1, 2, 0, 3).reshape(rows, 3 * d)
    )
    gate_up_parts = jnp.stack([part.reshape(n, rows, 3, step) for part in sums], axis=3)
    gate_up_parts = gate_up_parts.transpose(1, 2, 0, 3, 4).reshape(rows, 3, ff)
    return (
        output,
        grad_input,
        grad_attention.astype(f32),
        grad_output_weight.astype(f32),
        gate_up_parts[:, :2].reshape(rows, 2 * ff).astype(f32),
        gate_up_parts[:, 2].astype(f32),
        gains[:, 0],
        gains[:, 1],
    )


def solution(mesh):
    plane = Plane(mesh.shape["ctx"])
    return jax.shard_map(
        functools.partial(on_device, plane),
        mesh=mesh,
        in_specs=(
            P("fsdp", "ctx", None),
            P("fsdp", None),
            P(),
            P("fsdp", None),
            P("fsdp", None),
            P(),
            P("fsdp", None),
            P("fsdp", None),
            P("fsdp", "ctx", None),
        ),
        out_specs=(
            P("fsdp", "ctx", None),
            P("fsdp", "ctx", None),
            P(("ctx", "fsdp"), None),
            P(("ctx", "fsdp"), None),
            P(("ctx", "fsdp"), None),
            P(("ctx", "fsdp"), None),
            P(("ctx", "fsdp")),
            P(("ctx", "fsdp")),
        ),
        check_vma=False,
    )
```

```python
import functools

import jax
import jax.numpy as jnp
from jax import lax
from jax.experimental import pallas as pl
from jax.experimental.pallas import tpu as pltpu
from jax.sharding import PartitionSpec as P

HEAD_SIZE = 64
EPSILON = 1e-05
ROPE_BASE = 130000.0
CHUNKS = 4

f32 = jnp.float32
bf16 = jnp.bfloat16


def rms_scale(values):
    return lax.rsqrt(jnp.mean(values * values, axis=-1, keepdims=True) + EPSILON)


def dot(left, right):
    return jnp.dot(left, right, preferred_element_type=f32)


def dot_rows(left, right):
    return lax.dot_general(left, right, (((1,), (1,)), ((), ())), preferred_element_type=f32)


def dot_tokens(left, right):
    return lax.dot_general(left, right, (((0,), (0,)), ((), ())), preferred_element_type=f32)


def tables_kernel(places_ref, cos_ref, sin_ref):
    half = HEAD_SIZE // 2
    width = cos_ref.shape[1]
    narrow = min(width, 128)
    lane = lax.broadcasted_iota(jnp.int32, (1, narrow), 1) % half
    inverse = jnp.exp(-(2.0 * lane.astype(f32) / HEAD_SIZE) * jnp.log(f32(ROPE_BASE)))
    angles = places_ref[...].astype(f32) * inverse
    cosine, sine = jnp.cos(angles), jnp.sin(angles)
    for start in range(0, width, narrow):
        cos_ref[:, start : start + narrow] = cosine
        sin_ref[:, start : start + narrow] = sine


def rope_tables(places, lanes):
    tokens = places.shape[0]
    tile = min(256, tokens)
    return pl.pallas_call(
        tables_kernel,
        grid=(tokens // tile,),
        in_specs=[pl.BlockSpec((tile, 1), lambda i: (i, 0))],
        out_specs=[pl.BlockSpec((tile, lanes), lambda i: (i, 0))] * 2,
        out_shape=[jax.ShapeDtypeStruct((tokens, lanes), f32)] * 2,
        cost_estimate=pl.CostEstimate(
            flops=100 * tokens * lanes, bytes_accessed=8 * tokens * lanes, transcendentals=0
        ),
    )(places.reshape(tokens, 1))


def other_half(values):
    half = HEAD_SIZE // 2
    lanes = values.shape[-1]
    if lanes == HEAD_SIZE:
        return jnp.concatenate([-values[:, half:], values[:, :half]], axis=1)
    lane = lax.broadcasted_iota(jnp.int32, values.shape, 1)
    return jnp.where(
        lane % HEAD_SIZE < half,
        -pltpu.roll(values, lanes - half, 1),
        pltpu.roll(values, half, 1),
    )


def rotate(values, cosine, sine):
    return values * cosine + other_half(values) * sine


def rotate_back(gradient, cosine, sine):
    return gradient * cosine - other_half(gradient * sine)


MESH = pl.DeviceIdType.MESH


def greet(partners):
    barrier = pltpu.get_barrier_semaphore()
    for partner in partners:
        pl.semaphore_signal(barrier, inc=1, device_id={"ctx": partner}, device_id_type=MESH)
    pl.semaphore_wait(barrier, len(partners))


def flipped(place, bits):
    for bit in (1, 2, 4):
        if bits & bit:
            place = place + bit - 2 * bit * ((place // bit) % 2)
    return place


def neighbours():
    me = lax.axis_index("ctx")
    return [flipped(me, bit) for bit in (1, 2, 4)]


class Gather:
    SEMAPHORES = (
        pltpu.SemaphoreType.DMA((2,)),
        pltpu.SemaphoreType.DMA((14,)),
        pltpu.SemaphoreType.DMA((14,)),
    )

    def __init__(self, own, out, local, sent, came):
        self.partners = sibling, by_x, by_y = neighbours()
        routes = [
            (by_x, own.at[0], out.at[0, 0, 1]),
            (by_y, own.at[1], out.at[0, 1, 2]),
            (by_x, own.at[1], out.at[0, 1, 1]),
            (by_y, own.at[0], out.at[0, 0, 2]),
            (by_y, out.at[0, 0, 1], out.at[0, 0, 3]),
            (by_x, out.at[0, 1, 2], out.at[0, 1, 3]),
        ]
        for h in range(2):
            routes.append((sibling, own.at[h], out.at[1, h, 0]))
        for h, q in ((0, 1), (1, 2), (1, 1), (0, 2), (0, 3), (1, 3)):
            routes.append((sibling, out.at[0, h, q], out.at[1, h, q]))
        self.copies = [
            pltpu.make_async_remote_copy(
                src_ref=source,
                dst_ref=target,
                send_sem=sent.at[index],
                recv_sem=came.at[index],
                device_id={"ctx": partner},
                device_id_type=MESH,
            )
            for index, (partner, source, target) in enumerate(routes)
        ]
        self.kept = [
            pltpu.make_async_copy(own.at[h], out.at[0, h, 0], local.at[h]) for h in range(2)
        ]

    def start(self):
        greet(self.partners)
        for index in (0, 1, 2, 3, 6, 7):
            self.copies[index].start()
        for copy in self.kept:
            copy.start()

    def pass_on(self):
        self.copies[0].wait_recv()
        self.copies[4].start()
        self.copies[8].start()
        self.copies[1].wait_recv()
        self.copies[5].start()
        self.copies[9].start()

    def pass_seconds(self):
        self.copies[2].wait_recv()
        self.copies[10].start()
        self.copies[3].wait_recv()
        self.copies[11].start()

    def finish(self):
        self.copies[4].wait_recv()
        self.copies[12].start()
        self.copies[5].wait_recv()
        self.copies[13].start()
        for copy in self.copies[6:]:
            copy.wait_recv()
        for copy in self.copies:
            copy.wait_send()
        for copy in self.kept:
            copy.wait()

    def ride(self, step, steps):
        for turn, phase in ((0, self.start), (steps // 2, self.pass_on), (steps - 1, self.pass_seconds)):
            pl.when(step == turn)(phase)


def gathered_shape(own):
    return jax.ShapeDtypeStruct((2, 2, 4) + own.shape[1:], own.dtype)


ANYWHERE = pl.BlockSpec(memory_space=pl.ANY)


def talking(identity):
    return pltpu.CompilerParams(
        collective_id=identity, has_side_effects=True, vmem_limit_bytes=56 * 1024 * 1024
    )


def gather_kernel(count, own_ref, *refs):
    gather = Gather(own_ref, *refs[count:])
    gather.start()
    gather.pass_on()
    gather.pass_seconds()
    gather.finish()


def gather_in_plane(own, identity, earlier=()):
    size = own.size * own.dtype.itemsize
    return pl.pallas_call(
        functools.partial(gather_kernel, len(earlier)),
        in_specs=[ANYWHERE] * (1 + len(earlier)),
        out_specs=ANYWHERE,
        out_shape=gathered_shape(own),
        scratch_shapes=list(Gather.SEMAPHORES),
        compiler_params=talking(identity),
        cost_estimate=pl.CostEstimate(
            flops=0, bytes_accessed=16 * size, transcendentals=0, remote_bytes_transferred=7 * size
        ),
    )(own, *earlier)


class Plane:
    def __init__(self, size):
        self.size = size
        self.relative = size == 8

    def swap(self, value, bits):
        return lax.ppermute(value, "ctx", [(i, i ^ bits) for i in range(self.size)])

    def gather(self, own, identity, earlier=()):
        if self.relative:
            return gather_in_plane(own, identity, earlier)
        whole = lax.all_gather(own, "ctx", axis=1, tiled=False)
        s, n, r, d = whole.shape
        return whole.reshape(s, n // 2, 2, r, d).transpose(2, 0, 1, 3, 4)

    def scatter(self, odd, even):
        if not self.relative:
            both = jnp.stack([even, odd], axis=2)
            s, q, p, r, d = both.shape
            return lax.psum_scatter(
                both.reshape(s, q * p, r, d), "ctx", scatter_dimension=1, tiled=False
            ).astype(f32)
        half = odd.shape[0] // 2
        came = self.swap(odd, 1)
        both = (even.astype(f32) + came.astype(f32)).astype(bf16)
        far_x, far_y = self.swap(both[:half, 3], 2), self.swap(both[half:, 3], 4)
        direct_x, direct_y = self.swap(both[:half, 1], 2), self.swap(both[half:, 2], 4)
        to_x = (both[half:, 1].astype(f32) + far_y.astype(f32)).astype(bf16)
        to_y = (both[:half, 2].astype(f32) + far_x.astype(f32)).astype(bf16)
        later_x, later_y = self.swap(to_x, 2), self.swap(to_y, 4)
        from_x = jnp.concatenate([direct_x, later_x], axis=0).astype(f32)
        from_y = jnp.concatenate([later_y, direct_y], axis=0).astype(f32)
        return both[:, 0].astype(f32) + from_x + from_y

    def order(self, places):
        s, n, r = places.shape
        if self.relative:
            me = lax.axis_index("ctx")
            bits = places.reshape(s, 2, 2, 2, r)
            for axis, bit in ((1, 4), (2, 2), (3, 1)):
                bits = jnp.where((me & bit) != 0, jnp.flip(bits, axis), bits)
            places = bits.reshape(s, n, r)
        return places.reshape(s, n // 2, 2, r).transpose(2, 0, 1, 3)


def zero_of(value):
    first = lax.slice(value, (0,) * value.ndim, (1,) * value.ndim).reshape(()).astype(f32)
    return (first != first).astype(jnp.int32)


def after(value, earlier):
    return jnp.where(zero_of(earlier) == 0, value, jnp.zeros_like(value))


def gather_rows(own):
    return lax.all_gather(own, "fsdp", axis=0, tiled=True)


def by_owners(partial, n, rows):
    depth, columns = partial.shape
    return partial.astype(bf16).reshape(n, depth // (n * rows), rows, columns).transpose(1, 0, 2, 3)


def sum_rows(laid):
    groups, n, rows, columns = laid.shape
    return lax.psum_scatter(
        laid.reshape(groups * n * rows, columns), "fsdp", scatter_dimension=0, tiled=True
    ).reshape(n, rows, columns)


def to_owners(sums):
    return lax.all_to_all(sums, "ctx", split_axis=0, concat_axis=0, tiled=True)


PARAMS = pltpu.CompilerParams(vmem_limit_bytes=56 * 1024 * 1024)


def whole_spec(shape):
    return pl.BlockSpec(shape, lambda i: (0,) * len(shape), pipeline_mode=pl.Buffered(1))


def tile_spec(tile, width):
    return pl.BlockSpec((tile, width), lambda i: (i, 0))


def project_kernel(x_ref, gain_ref, cos_ref, sin_ref, w_ref, low_ref, q_ref, k_ref, v_ref):
    x = x_ref[...].astype(f32)
    low = (x * rms_scale(x) * gain_ref[...]).astype(bf16)
    low_ref[...] = low
    lanes = q_ref.shape[-1]
    projected = dot(low, w_ref[...])
    cosine, sine = cos_ref[...], sin_ref[...]
    q_ref[...] = rotate(projected[:, :lanes], cosine, sine).astype(bf16)
    k_ref[...] = rotate(projected[:, lanes : 2 * lanes], cosine, sine).astype(bf16)
    v_ref[...] = projected[:, 2 * lanes :].astype(bf16)


def project(x, gain, cosine, sine, weight):
    tokens, d = x.shape
    lanes = cosine.shape[1]
    tile = min(256, tokens)
    return pl.pallas_call(
        project_kernel,
        grid=(tokens // tile,),
        in_specs=[tile_spec(tile, d), whole_spec((1, d))]
        + [tile_spec(tile, lanes)] * 2
        + [whole_spec(weight.shape)],
        out_specs=[tile_spec(tile, d)] + [tile_spec(tile, lanes)] * 3,
        out_shape=[jax.ShapeDtypeStruct((tokens, d), bf16)]
        + [jax.ShapeDtypeStruct((tokens, lanes), bf16)] * 3,
        compiler_params=PARAMS,
        cost_estimate=pl.CostEstimate(
            flops=6 * tokens * d * lanes, bytes_accessed=6 * tokens * d, transcendentals=0
        ),
    )(x, gain.reshape(1, d), cosine, sine, weight)


def residual_kernel(x_ref, att_ref, gain_ref, w_ref, low_ref, res_ref):
    n, _, width = w_ref.shape
    for c in range(n):
        columns = slice(c * width, (c + 1) * width)
        res_ref[:, columns] = x_ref[:, columns].astype(f32) + dot(att_ref[...], w_ref[c])
    residual = res_ref[...]
    low_ref[...] = (residual * rms_scale(residual) * gain_ref[...]).astype(bf16)


def residuals(x, attended, gain, out_blocks):
    tokens, d = x.shape
    tile = min(256, tokens)
    return pl.pallas_call(
        residual_kernel,
        grid=(tokens // tile,),
        in_specs=[tile_spec(tile, d), tile_spec(tile, d), whole_spec((1, d)), whole_spec(out_blocks.shape)],
        out_specs=[tile_spec(tile, d), tile_spec(tile, d)],
        out_shape=[jax.ShapeDtypeStruct((tokens, d), bf16), jax.ShapeDtypeStruct((tokens, d), f32)],
        compiler_params=PARAMS,
        cost_estimate=pl.CostEstimate(
            flops=2 * tokens * d * d, bytes_accessed=10 * tokens * d, transcendentals=0
        ),
    )(x, attended, gain.reshape(1, d), out_blocks)


def gathered_residual_kernel(x_ref, gain_ref, w_ref, *refs):
    parts, (own_ref, low_ref, res_ref, all_ref, att, total) = refs[:8], refs[8:14]
    gather = Gather(own_ref, all_ref, *refs[14:])
    step, steps = pl.program_id(0) * pl.num_programs(1) + pl.program_id(1), 8
    gather.ride(step, steps)
    width = w_ref.shape[-1]
    shape = low_ref.shape

    def columns(index):
        return pl.ds(pl.multiple_of(flipped(lax.axis_index("ctx"), index) * width, width), width)

    for index, part in enumerate(parts):
        att[:, columns(index)] = part[...].reshape(-1, width)
    attended = att[...]
    for index in range(8):
        total[:, columns(index)] = dot(attended, w_ref[index % 2, :, index // 2].reshape(-1, width))
    residual = total[...] + x_ref[...].reshape(attended.shape).astype(f32)
    res_ref[...] = residual.reshape(shape)
    low_ref[...] = (residual * rms_scale(residual) * gain_ref[...]).astype(bf16).reshape(shape)
    pl.when(step == steps - 1)(gather.finish)


def gathered_residuals(x, attended, gain, out_blocks, own, identity):
    _, s, q, r, d = x.shape
    width = attended.shape[-1]
    tile = pl.BlockSpec((1, s, 1, r, d), lambda p, t: (p, 0, t, 0, 0))

    def sent(index):
        odd, other = index % 2, index // 2
        return pl.BlockSpec(
            (1, 1, 1, s, 1, r, width),
            lambda p, t: (odd, (p + odd) % 2, other, 0, flipped(t, other), 0, 0),
        )

    def fixed(shape):
        return pl.BlockSpec(shape, lambda p, t: (0,) * len(shape), pipeline_mode=pl.Buffered(1))

    return pl.pallas_call(
        gathered_residual_kernel,
        grid=(2, q),
        in_specs=[tile, fixed((1, d)), fixed(out_blocks.shape)]
        + [sent(i) for i in range(8)]
        + [ANYWHERE],
        out_specs=[tile, tile, ANYWHERE],
        out_shape=[
            jax.ShapeDtypeStruct(x.shape, bf16),
            jax.ShapeDtypeStruct(x.shape, f32),
            gathered_shape(own),
        ],
        scratch_shapes=[
            pltpu.VMEM((s * r, d), bf16),
            pltpu.VMEM((s * r, d), f32),
            *Gather.SEMAPHORES,
        ],
        compiler_params=talking(identity),
        cost_estimate=pl.CostEstimate(
            flops=2 * x.size * d, bytes_accessed=10 * x.size, transcendentals=0
        ),
    )(x, gain.reshape(1, d), out_blocks, *[attended] * 8, own)


def hidden_kernel(low_ref, cot_ref, w_ref, *refs):
    hidden_ref, grad_ref = refs[-2:]
    step = hidden_ref.shape[-1]
    gate_up = dot(low_ref[...], w_ref[:, : 2 * step])
    grad_hidden = dot(cot_ref[...], w_ref[:, 2 * step :])
    gate, upward = gate_up[:, :step], gate_up[:, step:]
    sigmoid = jax.nn.sigmoid(gate)
    hidden_ref[...] = (gate * sigmoid * upward).astype(bf16)
    grad_ref[:, :step] = (grad_hidden * upward * sigmoid * (1.0 + gate * (1.0 - sigmoid))).astype(bf16)
    grad_ref[:, step:] = (grad_hidden * gate * sigmoid).astype(bf16)


def hidden_part(second_low, cot, weight, earlier=()):
    tokens, d = second_low.shape
    step = weight.shape[1] // 3
    tile = min(256, tokens)
    return pl.pallas_call(
        hidden_kernel,
        grid=(tokens // tile,),
        in_specs=[tile_spec(tile, d)] * 2 + [whole_spec(weight.shape)] + [ANYWHERE] * len(earlier),
        out_specs=[tile_spec(tile, step), tile_spec(tile, 2 * step)],
        out_shape=[
            jax.ShapeDtypeStruct((tokens, step), bf16),
            jax.ShapeDtypeStruct((tokens, 2 * step), bf16),
        ],
        compiler_params=PARAMS,
        cost_estimate=pl.CostEstimate(
            flops=6 * tokens * d * step, bytes_accessed=4 * tokens * d, transcendentals=tokens * step
        ),
    )(second_low, cot, weight, *earlier)


def back_kernel(count, *refs):
    lefts, weights = refs[:count], refs[count : 2 * count]
    total = None
    for left, weight in zip(lefts, weights):
        part = dot_rows(left[...], weight[...])
        total = part if total is None else total + part
    if len(refs) == 2 * count + 1:
        refs[2 * count][...] = total.astype(bf16)
        return
    low_ref, out_ref, sum_ref = refs[2 * count :]

    @pl.when(pl.program_id(0) == 0)
    def _():
        sum_ref[...] = jnp.zeros_like(sum_ref)

    out_ref[...] = total.astype(bf16)
    sum_ref[...] += jnp.sum(total * low_ref[...].astype(f32), axis=0, keepdims=True)


def picked(weights, picks, width):
    if width % 128:
        weights = [
            lax.slice_in_dim(weight, pick * width, (pick + 1) * width, axis=1)
            for weight, pick in zip(weights, picks)
        ]
        picks = [0] * len(weights)
    return weights, picks


def back(lefts, weights, picks, first, tokens, low=None):
    d = weights[0].shape[0]
    tile = min(256, tokens)
    start = first // tile
    width = lefts[0].shape[1]
    weights, picks = picked(weights, picks, width)

    def shifted(wide):
        return pl.BlockSpec((tile, wide), lambda i: (i + start, 0))

    def columns(pick):
        return pl.BlockSpec((d, width), lambda i: (0, pick), pipeline_mode=pl.Buffered(1))

    out_specs = [tile_spec(tile, d)]
    out_shape = [jax.ShapeDtypeStruct((tokens, d), bf16)]
    if low is not None:
        out_specs.append(pl.BlockSpec((1, d), lambda i: (0, 0)))
        out_shape.append(jax.ShapeDtypeStruct((1, d), f32))
    return pl.pallas_call(
        functools.partial(back_kernel, len(lefts)),
        grid=(tokens // tile,),
        in_specs=[shifted(width)] * len(lefts)
        + [columns(pick) for pick in picks]
        + ([shifted(d)] if low is not None else []),
        out_specs=out_specs,
        out_shape=out_shape,
        compiler_params=PARAMS,
        cost_estimate=pl.CostEstimate(
            flops=2 * tokens * d * width * len(lefts), bytes_accessed=4 * tokens * d, transcendentals=0
        ),
    )(*lefts, *weights, *([low] if low is not None else []))


FAR, BY_X, BY_Y, OWN = 3, 1, 2, 0
TURNS = ((1, FAR), (1, BY_X), (0, FAR), (1, BY_Y), (0, BY_X), (1, OWN), (0, BY_Y), (0, OWN))
PARITIES = sum(p << t for t, (p, _) in enumerate(TURNS))
PLACES = sum(q << (2 * t) for t, (_, q) in enumerate(TURNS))


def back_scatter_kernel(count, with_low, skipped, *refs):
    lefts, weights, refs = refs[:count], refs[count : 2 * count], refs[2 * count + skipped :]
    if with_low:
        low_ref, out_ref, sum_ref, refs = refs[0], refs[1], refs[2], refs[3:]
        sum_ref[...] = jnp.zeros_like(sum_ref)
    else:
        out_ref, refs = refs[0], refs[1:]
    given, got, sums, own, far, from_x, from_y, send_odd, came_odd, sent, came = refs
    sibling, by_x, by_y = neighbours()
    greet((sibling, by_x, by_y))
    s, r, d = own.shape
    half = s // 2

    def move(partner, source, target, send_sem, recv_sem):
        return pltpu.make_async_remote_copy(
            src_ref=source,
            dst_ref=target,
            send_sem=send_sem,
            recv_sem=recv_sem,
            device_id={"ctx": partner},
            device_id_type=MESH,
        )

    def odd_copy(q):
        return move(sibling, given.at[q], got.at[q], send_odd.at[q], came_odd.at[q])

    low_half, high_half = pl.ds(0, half), pl.ds(half, half)
    far_x = move(by_x, sums.at[FAR, low_half], far.at[low_half], sent.at[0], came.at[0])
    far_y = move(by_y, sums.at[FAR, high_half], far.at[high_half], sent.at[1], came.at[1])
    first_x = move(by_x, sums.at[BY_X, low_half], from_x.at[low_half], sent.at[2], came.at[2])
    first_y = move(by_y, sums.at[BY_Y, high_half], from_y.at[high_half], sent.at[3], came.at[3])
    last_x = move(by_x, sums.at[BY_X, high_half], from_x.at[high_half], sent.at[4], came.at[4])
    last_y = move(by_y, sums.at[BY_Y, low_half], from_y.at[low_half], sent.at[5], came.at[5])

    def turn(t, _):
        p = lax.shift_right_logical(jnp.int32(PARITIES), t) % 2
        q = lax.shift_right_logical(jnp.int32(PLACES), 2 * t) % 4
        total = None
        for left, weight in zip(lefts, weights):
            width = left.shape[-1]
            part = dot_rows(left[p, :, q].reshape(s * r, width), weight[...])
            total = part if total is None else total + part
        if with_low:
            low = low_ref[p, :, q].reshape(s * r, d).astype(f32)
            sum_ref[...] += jnp.sum(total * low, axis=0, keepdims=True)
        total = total.reshape(s, r, d)

        @pl.when(p == 1)
        def _():
            given[q] = total.astype(bf16)
            odd_copy(q).start()

        @pl.when(p == 0)
        def _():
            odd_copy(q).wait_recv()
            both = total + got[q].astype(f32)

            @pl.when(q == OWN)
            def _():
                own[...] = both

            @pl.when(q != OWN)
            def _():
                sums[q] = both.astype(bf16)

            @pl.when(q == FAR)
            def _():
                far_x.start()
                far_y.start()

            @pl.when(q == BY_X)
            def _():
                first_x.start()

            @pl.when(q == BY_Y)
            def _():
                first_y.start()

        return 0

    lax.fori_loop(0, len(TURNS), turn, 0)
    far_x.wait_recv()
    sums[BY_Y, low_half] = (sums[BY_Y, low_half].astype(f32) + far[low_half].astype(f32)).astype(bf16)
    last_y.start()
    far_y.wait_recv()
    sums[BY_X, high_half] = (sums[BY_X, high_half].astype(f32) + far[high_half].astype(f32)).astype(bf16)
    last_x.start()
    first_x.wait_recv()
    first_y.wait_recv()
    out_ref[low_half] = own[low_half] + from_x[low_half].astype(f32)
    out_ref[high_half] = own[high_half] + from_y[high_half].astype(f32)
    last_y.wait_recv()
    out_ref[low_half] += from_y[low_half].astype(f32)
    last_x.wait_recv()
    out_ref[high_half] += from_x[high_half].astype(f32)
    for copy in (far_x, far_y, first_x, first_y, last_x, last_y):
        copy.wait_send()
    for q in range(4):
        odd_copy(q).wait_send()


def back_scatter(lefts, weights, picks, shape, identity, low=None, earlier=()):
    s, q, r, d = shape
    width = lefts[0].shape[-1]
    weights, picks = picked(weights, picks, width)
    lefts = [left.reshape(2, s, q, r, width) for left in lefts]

    def fixed(whole):
        return pl.BlockSpec(whole, lambda i: (0,) * len(whole), pipeline_mode=pl.Buffered(1))

    def columns(pick):
        return pl.BlockSpec((d, width), lambda i: (0, pick), pipeline_mode=pl.Buffered(1))

    operands = [*lefts, *weights, *earlier]
    in_specs = [fixed(left.shape) for left in lefts] + [columns(pick) for pick in picks]
    in_specs += [ANYWHERE] * len(earlier)
    out_specs = [fixed((s, r, d))]
    out_shape = [jax.ShapeDtypeStruct((s, r, d), f32)]
    if low is not None:
        low = low.reshape(2, s, q, r, d)
        operands.append(low)
        in_specs.append(fixed(low.shape))
        out_specs.append(fixed((1, d)))
        out_shape.append(jax.ShapeDtypeStruct((1, d), f32))
    dma = pltpu.SemaphoreType.DMA
    return pl.pallas_call(
        functools.partial(back_scatter_kernel, len(lefts), low is not None, len(earlier)),
        grid=(1,),
        in_specs=in_specs,
        out_specs=out_specs,
        out_shape=out_shape,
        scratch_shapes=[
            pltpu.VMEM((4, s, r, d), bf16),
            pltpu.VMEM((4, s, r, d), bf16),
            pltpu.VMEM((4, s, r, d), bf16),
            pltpu.VMEM((s, r, d), f32),
            pltpu.VMEM((s, r, d), bf16),
            pltpu.VMEM((s, r, d), bf16),
            pltpu.VMEM((s, r, d), bf16),
            dma((4,)),
            dma((4,)),
            dma((6,)),
            dma((6,)),
        ],
        compiler_params=talking(identity),
        cost_estimate=pl.CostEstimate(
            flops=16 * s * r * d * width * len(lefts),
            bytes_accessed=16 * s * r * d,
            transcendentals=0,
            remote_bytes_transferred=14 * s * r * d,
        ),
    )(*operands)


def token_sums_kernel(counts, *refs):
    out_ref = refs[-1]
    refs = list(refs)
    start = 0
    for count in counts:
        left, rights, refs = refs[0], refs[1 : 1 + count], refs[1 + count :]
        for right in rights:
            width = right.shape[1]
            part = dot_tokens(left[...], right[...]).astype(bf16)
            out_ref[:, :, :, start : start + width] = part.reshape(out_ref.shape[:3] + (width,))
            start += width


def token_sums(pairs, n, rows):
    groups = pairs[0][0].shape[1] // (n * rows)
    operands, in_specs, width = [], [], 0
    for left, rights in pairs:
        operands += [left, *rights]
        in_specs.append(pl.BlockSpec((left.shape[0], groups * rows), lambda i: (0, i)))
        in_specs += [whole_spec(right.shape) for right in rights]
        width += sum(right.shape[1] for right in rights)
    tokens, d = pairs[0][0].shape
    return pl.pallas_call(
        functools.partial(token_sums_kernel, [len(rights) for _, rights in pairs]),
        grid=(n,),
        in_specs=in_specs,
        out_specs=pl.BlockSpec((groups, 1, rows, width), lambda i: (0, i, 0, 0)),
        out_shape=jax.ShapeDtypeStruct((groups, n, rows, width), bf16),
        compiler_params=PARAMS,
        cost_estimate=pl.CostEstimate(
            flops=2 * tokens * d * width, bytes_accessed=4 * tokens * d, transcendentals=0
        ),
    )(*operands)


def output_back_kernel(low_ref, att_ref, w_ref, *refs):
    grad_ref, sum_ref, total = refs[-3:]

    @pl.when(pl.program_id(0) == 0)
    def _():
        total[...] = jnp.zeros_like(total)

    low = low_ref[...]
    grad_ref[...] = dot_rows(low, w_ref[...]).astype(bf16)
    total[...] += dot_tokens(att_ref[...], low)

    @pl.when(pl.program_id(0) == pl.num_programs(0) - 1)
    def _():
        sum_ref[...] = total[...].astype(bf16)


def output_back(grad_low, attended_low, out_rows, earlier=()):
    tokens, d = grad_low.shape
    lanes = attended_low.shape[1]
    tile = min(256, tokens)
    return pl.pallas_call(
        output_back_kernel,
        grid=(tokens // tile,),
        in_specs=[tile_spec(tile, d), tile_spec(tile, lanes), whole_spec((lanes, d))]
        + [ANYWHERE] * len(earlier),
        out_specs=[tile_spec(tile, lanes), pl.BlockSpec((lanes, d), lambda i: (0, 0))],
        out_shape=[
            jax.ShapeDtypeStruct((tokens, lanes), bf16),
            jax.ShapeDtypeStruct((lanes, d), bf16),
        ],
        scratch_shapes=[pltpu.VMEM((lanes, d), f32)],
        compiler_params=PARAMS,
        cost_estimate=pl.CostEstimate(
            flops=4 * tokens * d * lanes, bytes_accessed=2 * tokens * d, transcendentals=0
        ),
    )(grad_low, attended_low, out_rows, *earlier)


def gather_and_sum_kernel(hiddens, skipped, low_ref, grad_ref, cot_ref, *refs):
    lefts, weights = refs[:hiddens], refs[hiddens : 2 * hiddens]
    refs = refs[2 * hiddens :]
    own_ref, refs = refs[0], refs[1 + skipped :]
    sum_ref, out_ref, all_ref = refs[:3]
    gather = Gather(own_ref, all_ref, *refs[3:])
    step, steps = pl.program_id(0), 8
    gather.ride(step, steps)
    tile = lefts[0].shape[0] // steps
    token_sums_kernel([1, 1], low_ref, grad_ref, cot_ref, lefts[-1], sum_ref)
    rows = pl.ds(pl.multiple_of(step * tile, tile), tile)
    total = None
    for left, weight in zip(lefts, weights):
        part = dot_rows(left[rows, :], weight[...])
        total = part if total is None else total + part
    out_ref[...] = total.astype(bf16)
    pl.when(step == steps - 1)(gather.finish)


def gather_and_sum(own, second_low, grad, cot, hiddens, weights, rows, identity, earlier=()):
    tokens, d = second_low.shape
    step = hiddens[0].shape[1]
    groups = d // (8 * rows)
    column = pl.BlockSpec((tokens, groups * rows), lambda i: (0, i))
    return pl.pallas_call(
        functools.partial(gather_and_sum_kernel, len(hiddens), len(earlier)),
        grid=(8,),
        in_specs=[column, whole_spec(grad.shape), column]
        + [whole_spec(hidden.shape) for hidden in hiddens]
        + [
            pl.BlockSpec((d, step), lambda i: (0, 2), pipeline_mode=pl.Buffered(1)) for _ in weights
        ]
        + [ANYWHERE] * (1 + len(earlier)),
        out_specs=[
            pl.BlockSpec((groups, 1, rows, 3 * step), lambda i: (0, i, 0, 0)),
            tile_spec(tokens // 8, d),
            ANYWHERE,
        ],
        out_shape=[
            jax.ShapeDtypeStruct((groups, 8, rows, 3 * step), bf16),
            jax.ShapeDtypeStruct((tokens, d), bf16),
            gathered_shape(own),
        ],
        scratch_shapes=list(Gather.SEMAPHORES),
        compiler_params=talking(identity),
        cost_estimate=pl.CostEstimate(
            flops=14 * tokens * d * step, bytes_accessed=12 * tokens * d, transcendentals=0
        ),
    )(second_low, grad, cot, *hiddens, *weights, own, *earlier)


def only(values, head, heads):
    if heads == 1:
        return values
    lane = lax.broadcasted_iota(jnp.int32, values.shape, 1)
    inside = (lane >= head * HEAD_SIZE) & (lane < (head + 1) * HEAD_SIZE)
    return jnp.where(inside, values, jnp.zeros_like(values))


def forward_kernel(heads, q_spot, k_spot, q_ref, k_ref, v_ref, *refs):
    if len(refs) > 2:
        own_ref, low_ref, total_ref, all_ref = refs[:4]
        gather = Gather(own_ref, all_ref, *refs[4:])
        steps = pl.num_programs(0) * pl.num_programs(1) * pl.num_programs(2)
        step = (pl.program_id(0) * pl.num_programs(1) + pl.program_id(1)) * pl.num_programs(2)
        step += pl.program_id(2)
        gather.ride(step, steps)
    else:
        low_ref, total_ref = refs
    lanes = q_ref.shape[-1]
    queries = q_ref[0, 0] * bf16(HEAD_SIZE**-0.5)
    keys = k_ref[:, 0].reshape(-1, lanes)
    values = v_ref[:, 0].reshape(-1, lanes)
    allowed = k_spot[0] <= q_spot[0, 0]
    attended = jnp.zeros(queries.shape, f32)
    for head in range(heads):
        scores = dot_rows(keys, only(queries, head, heads))
        scores = jnp.where(allowed, scores, -1e30)
        highest = jnp.max(scores, axis=0, keepdims=True)
        raised = jnp.exp(scores - highest)
        summed = jnp.sum(raised, axis=0, keepdims=True)
        probs = (raised * (1.0 / summed)).astype(bf16)
        total_ref[0, 0, head : head + 1, :] = highest + jnp.log(summed)
        attended += dot_tokens(probs, only(values, head, heads))
    low_ref[0, 0] = attended.astype(bf16)
    if len(refs) > 2:
        pl.when(step == steps - 1)(gather.finish)


def backward_kernel(
    heads, q_spot, k_spot, q_ref, k_ref, v_ref, grad_ref, total_ref, qc_ref, qs_ref, kc_ref, ks_ref, *refs
):
    dq_ref, dk_ref, dv_ref, dk_sum, dv_sum = refs[-5:]
    lanes = q_ref.shape[-1]
    scale = HEAD_SIZE**-0.5
    step = pl.program_id(1) * pl.num_programs(2) + pl.program_id(2)

    @pl.when(step == 0)
    def _():
        dk_sum[...] = jnp.zeros_like(dk_sum)
        dv_sum[...] = jnp.zeros_like(dv_sum)

    queries = q_ref[0, 0] * bf16(scale)
    grads = grad_ref[0, 0]
    keys = k_ref[:, 0].reshape(-1, lanes)
    values = v_ref[:, 0].reshape(-1, lanes)
    allowed = k_spot[0] <= q_spot[0, 0]
    grad_q = jnp.zeros(queries.shape, f32)
    for head in range(heads):
        query = only(queries, head, heads)
        grad = only(grads, head, heads)
        scores = jnp.where(allowed, dot_rows(keys, query), -1e30)
        probs = jnp.exp(scores - total_ref[0, 0, head : head + 1, :])
        dv_sum[...] += dot(probs.astype(bf16), grad)
        weighted = probs * dot_rows(values, grad)
        delta = jnp.sum(weighted, axis=0, keepdims=True)
        grad_scores = (weighted - probs * delta).astype(bf16)
        dk_sum[...] += dot(grad_scores, query)
        grad_q += dot_tokens(grad_scores, only(keys, head, heads))
    dq_ref[0, 0] = rotate_back(grad_q * scale, qc_ref[0, 0], qs_ref[0, 0]).astype(bf16)

    @pl.when(step == pl.num_programs(1) * pl.num_programs(2) - 1)
    def _():
        shape = (dk_ref.shape[0],) + dk_ref.shape[2:]
        cosine = kc_ref[:, 0].reshape(-1, lanes)
        sine = ks_ref[:, 0].reshape(-1, lanes)
        dk_ref[:, 0] = rotate_back(dk_sum[...], cosine, sine).astype(bf16).reshape(shape)
        dv_ref[:, 0] = dv_sum[...].astype(bf16).reshape(shape)


def attention_specs(shape, heads):
    p, s, rows, lanes = shape
    tile = min(256, rows)
    one = pl.BlockSpec((1, 1, tile, lanes), lambda i, j, t: (j, i, t, 0))
    side = pl.BlockSpec((p, 1, rows, lanes), lambda i, j, t: (0, i, 0, 0))
    stat = pl.BlockSpec((1, 1, heads, tile), lambda i, j, t: (j, i, 0, t))
    q_spot = pl.BlockSpec((1, 1, 1, tile), lambda i, j, t: (j, i, 0, t))
    k_spot = pl.BlockSpec((1, p * rows, 1), lambda i, j, t: (i, 0, 0))
    return (s, p, rows // tile), one, side, stat, q_spot, k_spot


def attend(q_spot, k_spot, queries, keys, values, own=None, identity=None):
    p, s, rows, lanes = queries.shape
    heads = lanes // HEAD_SIZE
    grid, one, side, stat, q_spec, k_spec = attention_specs(queries.shape, heads)
    pairs = p * rows * s * p * rows
    out_shape = [
        jax.ShapeDtypeStruct(queries.shape, bf16),
        jax.ShapeDtypeStruct((p, s, heads, rows), f32),
    ]
    riding = own is not None
    return pl.pallas_call(
        functools.partial(forward_kernel, heads),
        grid=grid,
        in_specs=[q_spec, k_spec, one, side, side] + [ANYWHERE] * riding,
        out_specs=[one, stat] + [ANYWHERE] * riding,
        out_shape=out_shape + ([gathered_shape(own)] if riding else []),
        scratch_shapes=list(Gather.SEMAPHORES) if riding else [],
        compiler_params=talking(identity) if riding else PARAMS,
        cost_estimate=pl.CostEstimate(
            flops=pairs * heads * 2048, bytes_accessed=queries.size * 14, transcendentals=pairs * heads
        ),
    )(q_spot, k_spot, queries, keys, values, *([own] if riding else []))


def attend_back(q_spot, k_spot, queries, keys, values, grads, totals, cosine, sine, earlier=()):
    p, s, rows, lanes = queries.shape
    heads = lanes // HEAD_SIZE
    grid, one, side, stat, q_spec, k_spec = attention_specs(queries.shape, heads)
    pairs = p * rows * s * p * rows
    return pl.pallas_call(
        functools.partial(backward_kernel, heads),
        grid=grid,
        in_specs=[q_spec, k_spec, one, side, side, one, stat, one, one, side, side]
        + [ANYWHERE] * len(earlier),
        out_specs=[one, side, side],
        out_shape=[jax.ShapeDtypeStruct(queries.shape, bf16)] * 3,
        scratch_shapes=[pltpu.VMEM((p * rows, lanes), f32)] * 2,
        compiler_params=PARAMS,
        cost_estimate=pl.CostEstimate(
            flops=pairs * heads * 5120, bytes_accessed=queries.size * 20, transcendentals=pairs * heads
        ),
    )(q_spot, k_spot, queries, keys, values, grads, totals, cosine, sine, cosine, sine, *earlier)


def on_device(
    plane,
    inputs,
    positions,
    first_gain,
    attention_weight,
    output_weight,
    second_gain,
    gate_up_weight,
    down_weight,
    cotangent,
):
    s, r, d = inputs.shape
    n = plane.size
    ff = down_weight.shape[1]
    me = lax.axis_index("ctx")
    lanes = d // n
    mine = ff // n
    step = mine // CHUNKS
    tokens = s * r * n
    rows = d // (n * lax.axis_size("fsdp"))
    half = tokens // 2
    group = (2, s, n // 2 * r)
    blocks = (s, n // 2, r, d)

    def columns(weight, start, width):
        return lax.dynamic_slice_in_dim(weight, start, width, 1)

    qkv = gather_rows(
        jnp.concatenate(
            [columns(attention_weight, part * d + me * lanes, lanes) for part in range(3)], axis=1
        )
    )
    out_own = gather_rows(columns(output_weight, me * lanes, lanes))
    ffn = []
    for chunk in range(CHUNKS):
        start = me * mine + chunk * step
        ffn.append(
            gather_rows(
                jnp.concatenate(
                    [
                        columns(gate_up_weight, start, step),
                        columns(gate_up_weight, ff + start, step),
                        columns(down_weight, start, step),
                    ],
                    axis=1,
                )
            )
        )
    whole_inputs = plane.gather(inputs, 1)

    places = plane.order(positions.reshape(s, n, r)).reshape(group)
    q_spot = places[:, :, None, :]
    k_spot = places.transpose(1, 0, 2).reshape(s, n * r, 1)
    cosine, sine = rope_tables(places.reshape(tokens), lanes)
    normed_low, queries, keys, values = project(
        whole_inputs.reshape(tokens, d), first_gain, cosine, sine, qkv
    )
    queries, keys, values, cosine, sine = (
        part.reshape(*group, lanes) for part in (queries, keys, values, cosine, sine)
    )
    if plane.relative:
        attended_low, totals, out_blocks = attend(
            q_spot, k_spot, queries, keys, values, out_own.reshape(2, d // 2, lanes), 2
        )
        attended_whole = plane.gather(attended_low.reshape(2, half, lanes), 3)
        second_low, residual, cot = gathered_residuals(
            whole_inputs,
            attended_whole.reshape(2, 2, 4, s, 4, r, lanes),
            second_gain,
            out_blocks,
            cotangent,
            4,
        )
        second_low = second_low.reshape(tokens, d)
        residual = residual[0, :, 0]
    else:
        attended_low, totals = attend(q_spot, k_spot, queries, keys, values)
        out_blocks = lax.all_gather(out_own, "ctx", axis=0, tiled=False)
        attended_whole = lax.all_gather(
            attended_low.reshape(tokens, lanes), "ctx", axis=1, tiled=True
        )
        second_low, residual = residuals(
            whole_inputs.reshape(tokens, d), attended_whole, second_gain, out_blocks
        )
        residual = lax.dynamic_index_in_dim(residual.reshape(2, *blocks), me % 2, 0, keepdims=False)
        residual = lax.dynamic_index_in_dim(residual, me // 2, 1, keepdims=False)
        cot = plane.gather(cotangent, 4)
    cot = cot.reshape(tokens, d)
    attended_low = attended_low.reshape(tokens, lanes)

    def summed(pairs):
        if plane.relative:
            return token_sums(pairs, n, rows)
        partial = [dot_tokens(left, right) for left, rights in pairs for right in rights]
        return by_owners(jnp.concatenate(partial, axis=1), n, rows)

    hiddens, grads, partials, sums = [], [], [], []
    for chunk, weight in enumerate(ffn):
        hidden, grad_gate_up = hidden_part(second_low, cot, weight, partials[-1:])
        hiddens.append(hidden)
        grads.append(grad_gate_up)
        if chunk < CHUNKS - 1 or not plane.relative:
            partials.append(summed([(second_low, [grad_gate_up]), (cot, [hidden])]))
            sums.append(sum_rows(partials[-1]))

    def apart(lefts, weights, picks, low=None):
        odd = back(lefts, weights, picks, half, half, low)
        even = back(lefts, weights, picks, 0, half, low)
        total = plane.scatter(odd[0].reshape(blocks), even[0].reshape(blocks))
        return (total,) if low is None else (total, odd[1] + even[1])

    def together(identity, lefts, weights, picks, low=None, earlier=()):
        if not plane.relative:
            return apart(lefts, weights, picks, low)
        return back_scatter(lefts, weights, picks, blocks, identity, low, earlier)

    owned = [to_owners(part) for part in sums]
    (grad_second,) = together(5, grads, ffn, [0] * CHUNKS, earlier=partials[-1:])

    scale_two = rms_scale(residual)
    weighted = second_gain * grad_second
    second_gain_part = jnp.sum(grad_second * residual * scale_two, axis=(0, 1))
    grad_residual = (
        cotangent.astype(f32)
        + scale_two * weighted
        - residual
        * (scale_two * scale_two * scale_two)
        * jnp.mean(weighted * residual, axis=-1, keepdims=True)
    )
    if plane.relative:
        last, output_parts, grad_low = gather_and_sum(
            grad_residual.astype(bf16), second_low, grads[-1], cot, hiddens, ffn, rows, 6
        )
        owned.append(to_owners(sum_rows(last)))
        output_parts = output_parts.reshape(2, *blocks)
        output = residual + plane.scatter(output_parts[1], output_parts[0])
    else:
        grad_low = plane.gather(grad_residual.astype(bf16), 6)
        output = residual + apart(hiddens, ffn, [2] * CHUNKS)[0]
    grad_low = grad_low.reshape(tokens, d)

    if plane.relative:
        out_rows = lax.dynamic_slice(
            out_blocks, (0, me // 4, 0, (me % 4) * lanes, 0), (2, 1, 4, lanes, lanes)
        ).reshape(2, 2, 2, lanes, lanes)
        for axis, bit in ((0, 1), (1, 4), (2, 2)):
            out_rows = jnp.where((me & bit) != 0, jnp.flip(out_rows, axis), out_rows)
        out_rows = out_rows.transpose(3, 1, 2, 0, 4).reshape(lanes, d)
    else:
        out_rows = lax.dynamic_slice_in_dim(out_blocks, me * lanes, lanes, 1)
        out_rows = out_rows.transpose(1, 0, 2).reshape(lanes, d)
    grad_attended, out_part = output_back(
        grad_low, attended_low, out_rows, owned[:1]
    )
    grad_projected = attend_back(
        q_spot, k_spot, queries, keys, values, grad_attended.reshape(*group, lanes), totals, cosine, sine
    )
    grad_projected = [part.reshape(tokens, lanes) for part in grad_projected]
    attention_parts = summed([(normed_low, grad_projected)])
    attention_sums = sum_rows(attention_parts)
    grad_output_weight = lax.psum_scatter(
        after(out_part, attention_parts), "fsdp", scatter_dimension=0, tiled=True
    )
    grad_first, gain_sum = together(
        7, grad_projected, [qkv] * 3, [0, 1, 2], normed_low, [attention_parts]
    )
    gains = jnp.stack([gain_sum.reshape(d) / first_gain, second_gain_part])
    gains = gains.reshape(2, d // rows, rows).transpose(1, 0, 2)
    gains = jnp.sum(
        lax.all_to_all(gains, ("ctx", "fsdp"), split_axis=0, concat_axis=0, tiled=True), axis=0
    )

    own = inputs.astype(f32)
    scale_one = rms_scale(own)
    weighted = first_gain * grad_first
    grad_input = (
        grad_residual
        + scale_one * weighted
        - own
        * (scale_one * scale_one * scale_one)
        * jnp.mean(weighted * own, axis=-1, keepdims=True)
    )

    attention_sums = to_owners(attention_sums)
    grad_attention = (
        attention_sums.reshape(n, rows, 3, lanes).transpose(1, 2, 0, 3).reshape(rows, 3 * d)
    )
    sums = jnp.stack([part.reshape(n, rows, 3, step) for part in owned], axis=3)
    sums = sums.transpose(1, 2, 0, 3, 4).reshape(rows, 3, ff)
    return (
        output,
        grad_input,
        grad_attention.astype(f32),
        grad_output_weight.astype(f32),
        sums[:, :2].reshape(rows, 2 * ff).astype(f32),
        sums[:, 2].astype(f32),
        gains[0],
        gains[1],
    )


def solution(mesh):
    plane = Plane(mesh.shape["ctx"])
    return jax.shard_map(
        functools.partial(on_device, plane),
        mesh=mesh,
        in_specs=(
            P("fsdp", "ctx", None),
            P("fsdp", None),
            P(),
            P("fsdp", None),
            P("fsdp", None),
            P(),
            P("fsdp", None),
            P("fsdp", None),
            P("fsdp", "ctx", None),
        ),
        out_specs=(
            P("fsdp", "ctx", None),
            P("fsdp", "ctx", None),
            P(("ctx", "fsdp"), None),
            P(("ctx", "fsdp"), None),
            P(("ctx", "fsdp"), None),
            P(("ctx", "fsdp"), None),
            P(("ctx", "fsdp")),
            P(("ctx", "fsdp")),
        ),
        check_vma=False,
    )
```

```python
import functools

import jax
import jax.numpy as jnp
from jax import lax
from jax.experimental import pallas as pl
from jax.experimental.pallas import tpu as pltpu
from jax.sharding import PartitionSpec as P

HEAD_SIZE = 64
EPSILON = 1e-05
ROPE_BASE = 130000.0
CHUNKS = 4
RIDING = 0
PERMUTED = 0

f32 = jnp.float32
bf16 = jnp.bfloat16


def rms_scale(values):
    return lax.rsqrt(jnp.mean(values * values, axis=-1, keepdims=True) + EPSILON)


def dot(left, right):
    return jnp.dot(left, right, preferred_element_type=f32)


def dot_rows(left, right):
    return lax.dot_general(left, right, (((1,), (1,)), ((), ())), preferred_element_type=f32)


def dot_tokens(left, right):
    return lax.dot_general(left, right, (((0,), (0,)), ((), ())), preferred_element_type=f32)


def tables_kernel(places_ref, cos_ref, sin_ref):
    half = HEAD_SIZE // 2
    width = cos_ref.shape[1]
    narrow = min(width, 128)
    lane = lax.broadcasted_iota(jnp.int32, (1, narrow), 1) % half
    inverse = jnp.exp(-(2.0 * lane.astype(f32) / HEAD_SIZE) * jnp.log(f32(ROPE_BASE)))
    angles = places_ref[...].astype(f32) * inverse
    cosine, sine = jnp.cos(angles), jnp.sin(angles)
    for start in range(0, width, narrow):
        cos_ref[:, start : start + narrow] = cosine
        sin_ref[:, start : start + narrow] = sine


def rope_tables(places, lanes):
    tokens = places.shape[0]
    tile = min(512, tokens)
    return pl.pallas_call(
        tables_kernel,
        grid=(tokens // tile,),
        in_specs=[pl.BlockSpec((tile, 1), lambda i: (i, 0))],
        out_specs=[pl.BlockSpec((tile, lanes), lambda i: (i, 0))] * 2,
        out_shape=[jax.ShapeDtypeStruct((tokens, lanes), f32)] * 2,
        cost_estimate=pl.CostEstimate(
            flops=100 * tokens * lanes, bytes_accessed=8 * tokens * lanes, transcendentals=0
        ),
    )(places.reshape(tokens, 1))


def other_half(values):
    half = HEAD_SIZE // 2
    lanes = values.shape[-1]
    if lanes == HEAD_SIZE:
        return jnp.concatenate([-values[:, half:], values[:, :half]], axis=1)
    lane = lax.broadcasted_iota(jnp.int32, values.shape, 1)
    return jnp.where(
        lane % HEAD_SIZE < half,
        -pltpu.roll(values, lanes - half, 1),
        pltpu.roll(values, half, 1),
    )


def rotate(values, cosine, sine):
    return values * cosine + other_half(values) * sine


def rotate_back(gradient, cosine, sine):
    return gradient * cosine - other_half(gradient * sine)


MESH = pl.DeviceIdType.MESH


def greet(partners, axis="ctx"):
    barrier = pltpu.get_barrier_semaphore()
    for partner in partners:
        pl.semaphore_signal(barrier, inc=1, device_id={axis: partner}, device_id_type=MESH)
    pl.semaphore_wait(barrier, len(partners))


def flipped(place, bits):
    for bit in (1, 2, 4):
        if bits & bit:
            place = place + bit - 2 * bit * ((place // bit) % 2)
    return place


def neighbours():
    me = lax.axis_index("ctx")
    return [flipped(me, bit) for bit in (1, 2, 4)]


class Gather:
    SEMAPHORES = (
        pltpu.SemaphoreType.DMA((2,)),
        pltpu.SemaphoreType.DMA((14,)),
        pltpu.SemaphoreType.DMA((14,)),
    )

    def __init__(self, own, out, local, sent, came):
        self.partners = sibling, by_x, by_y = neighbours()
        routes = [
            (by_x, own.at[0], out.at[0, 0, 1]),
            (by_y, own.at[1], out.at[0, 1, 2]),
            (by_x, own.at[1], out.at[0, 1, 1]),
            (by_y, own.at[0], out.at[0, 0, 2]),
            (by_y, out.at[0, 0, 1], out.at[0, 0, 3]),
            (by_x, out.at[0, 1, 2], out.at[0, 1, 3]),
        ]
        for h in range(2):
            routes.append((sibling, own.at[h], out.at[1, h, 0]))
        for h, q in ((0, 1), (1, 2), (1, 1), (0, 2), (0, 3), (1, 3)):
            routes.append((sibling, out.at[0, h, q], out.at[1, h, q]))
        self.copies = [
            pltpu.make_async_remote_copy(
                src_ref=source,
                dst_ref=target,
                send_sem=sent.at[index],
                recv_sem=came.at[index],
                device_id={"ctx": partner},
                device_id_type=MESH,
            )
            for index, (partner, source, target) in enumerate(routes)
        ]
        self.kept = [
            pltpu.make_async_copy(own.at[h], out.at[0, h, 0], local.at[h]) for h in range(2)
        ]

    def start(self):
        greet(self.partners)
        self.send()

    def send(self):
        for index in (0, 1, 2, 3, 6, 7):
            self.copies[index].start()
        for copy in self.kept:
            copy.start()

    def pass_on(self):
        self.copies[0].wait_recv()
        self.copies[4].start()
        self.copies[8].start()
        self.copies[1].wait_recv()
        self.copies[5].start()
        self.copies[9].start()

    def pass_seconds(self):
        self.copies[2].wait_recv()
        self.copies[10].start()
        self.copies[3].wait_recv()
        self.copies[11].start()

    def finish(self):
        self.copies[4].wait_recv()
        self.copies[12].start()
        self.copies[5].wait_recv()
        self.copies[13].start()
        for copy in self.copies[6:]:
            copy.wait_recv()
        for copy in self.copies:
            copy.wait_send()
        for copy in self.kept:
            copy.wait()

    def ride(self, step, steps):
        for turn, phase in ((0, self.start), (steps // 2, self.pass_on), (steps - 1, self.pass_seconds)):
            pl.when(step == turn)(phase)


class LineGather:
    SEMAPHORES = (
        pltpu.SemaphoreType.DMA((1,)),
        pltpu.SemaphoreType.DMA((3,)),
        pltpu.SemaphoreType.DMA((3,)),
    )

    def __init__(self, own, out, local, sent, came):
        z = lax.axis_index("fsdp")
        size = own.shape[0]

        def rows(place):
            return out.at[pl.ds(pl.multiple_of(place * size, size), size)]

        self.partners = [(z + shift) % 4 for shift in (1, 2, 3)]
        held = z // 2 + 2 * (z % 2)
        routes = [
            ((z + 1) % 4, own, rows(z)),
            ((z + 3) % 4, own, rows(z)),
            (2 * (1 - z % 2) + z // 2, rows(held), rows(held)),
        ]
        self.copies = [
            pltpu.make_async_remote_copy(
                src_ref=source,
                dst_ref=target,
                send_sem=sent.at[index],
                recv_sem=came.at[index],
                device_id={"fsdp": partner},
                device_id_type=MESH,
            )
            for index, (partner, source, target) in enumerate(routes)
        ]
        self.kept = pltpu.make_async_copy(own, rows(z), local.at[0])

    def start(self):
        greet(self.partners, "fsdp")
        self.copies[0].start()
        self.copies[1].start()
        self.kept.start()

    def pass_on(self):
        self.copies[0].wait_recv()
        self.copies[1].wait_recv()
        self.kept.wait()
        self.copies[2].start()

    def finish(self):
        self.copies[2].wait_recv()
        for copy in self.copies:
            copy.wait_send()

    def ride(self, step, steps):
        pl.when(step == 0)(self.start)
        pl.when(step == steps - 1)(self.pass_on)


def line_shape(own):
    return jax.ShapeDtypeStruct((4 * own.shape[0], own.shape[1]), own.dtype)


def gathered_shape(own):
    return jax.ShapeDtypeStruct((2, 2, 4) + own.shape[1:], own.dtype)


ANYWHERE = pl.BlockSpec(memory_space=pl.ANY)


def talking(identity):
    return pltpu.CompilerParams(
        collective_id=identity, has_side_effects=True, vmem_limit_bytes=56 * 1024 * 1024
    )


def gather_kernel(count, *refs):
    scratch = len(Gather.SEMAPHORES)
    gathers = [
        Gather(refs[i], refs[count + i], *refs[2 * count + i * scratch : 2 * count + (i + 1) * scratch])
        for i in range(count)
    ]
    gathers[0].start()
    for index, gather in enumerate(gathers):
        gather.pass_on()
        if index + 1 < count:
            gathers[index + 1].send()
        gather.pass_seconds()
        gather.finish()


def gather_in_plane(owns, identity):
    size = sum(own.size * own.dtype.itemsize for own in owns)
    return pl.pallas_call(
        functools.partial(gather_kernel, len(owns)),
        in_specs=[ANYWHERE] * len(owns),
        out_specs=[ANYWHERE] * len(owns),
        out_shape=[gathered_shape(own) for own in owns],
        scratch_shapes=list(Gather.SEMAPHORES) * len(owns),
        compiler_params=talking(identity),
        cost_estimate=pl.CostEstimate(
            flops=0, bytes_accessed=16 * size, transcendentals=0, remote_bytes_transferred=7 * size
        ),
    )(*owns)


class Plane:
    def __init__(self, size):
        self.size = size
        self.relative = size == 8

    def swap(self, value, bits):
        return lax.ppermute(value, "ctx", [(i, i ^ bits) for i in range(self.size)])

    def gather(self, owns, identity):
        if self.relative:
            return gather_in_plane(owns, identity)
        wholes = [lax.all_gather(own, "ctx", axis=1, tiled=False) for own in owns]
        s, n, r, d = wholes[0].shape
        return [whole.reshape(s, n // 2, 2, r, d).transpose(2, 0, 1, 3, 4) for whole in wholes]

    def scatter(self, odd, even):
        if not self.relative:
            both = jnp.stack([even, odd], axis=2)
            s, q, p, r, d = both.shape
            return lax.psum_scatter(
                both.reshape(s, q * p, r, d), "ctx", scatter_dimension=1, tiled=False
            ).astype(f32)
        half = odd.shape[0] // 2
        came = self.swap(odd, 1)
        both = (even.astype(f32) + came.astype(f32)).astype(bf16)
        far_x, far_y = self.swap(both[:half, 3], 2), self.swap(both[half:, 3], 4)
        direct_x, direct_y = self.swap(both[:half, 1], 2), self.swap(both[half:, 2], 4)
        to_x = (both[half:, 1].astype(f32) + far_y.astype(f32)).astype(bf16)
        to_y = (both[:half, 2].astype(f32) + far_x.astype(f32)).astype(bf16)
        later_x, later_y = self.swap(to_x, 2), self.swap(to_y, 4)
        from_x = jnp.concatenate([direct_x, later_x], axis=0).astype(f32)
        from_y = jnp.concatenate([later_y, direct_y], axis=0).astype(f32)
        return both[:, 0].astype(f32) + from_x + from_y

    def order(self, places):
        s, n, r = places.shape
        if self.relative:
            me = lax.axis_index("ctx")
            bits = places.reshape(s, 2, 2, 2, r)
            for axis, bit in ((1, 4), (2, 2), (3, 1)):
                bits = jnp.where((me & bit) != 0, jnp.flip(bits, axis), bits)
            places = bits.reshape(s, n, r)
        return places.reshape(s, n // 2, 2, r).transpose(2, 0, 1, 3)


def zero_of(value):
    first = lax.slice(value, (0,) * value.ndim, (1,) * value.ndim).reshape(()).astype(f32)
    return (first != first).astype(jnp.int32)


def after(value, earlier):
    return jnp.where(zero_of(earlier) == 0, value, jnp.zeros_like(value))


def gather_rows(own):
    return lax.all_gather(own, "fsdp", axis=0, tiled=True)


def by_owners(partial, n, rows):
    depth, columns = partial.shape
    return partial.astype(bf16).reshape(n, depth // (n * rows), rows, columns).transpose(1, 0, 2, 3)


def sum_line(laid):
    z = lax.axis_index("fsdp")

    def block(shift):
        return lax.dynamic_index_in_dim(laid, (z + shift) % 4, 0, keepdims=False).astype(f32)

    def move(value, pairs):
        return lax.ppermute(value.astype(bf16), "fsdp", pairs)

    far = move(block(2), [(2, 0), (1, 3), (3, 2), (0, 1)]).astype(f32)
    down = move(block(3) + jnp.where(z == 2, far, 0.0), [(i, (i + 3) % 4) for i in range(4)])
    up = move(block(1) + jnp.where(z == 1, far, 0.0), [(i, (i + 1) % 4) for i in range(4)])
    ends = jnp.where((z == 0) | (z == 3), far, 0.0)
    return (block(0) + ends + down.astype(f32) + up.astype(f32)).astype(bf16)


def sum_rows(laid, permuted=False):
    groups, n, rows, columns = laid.shape
    if permuted and groups == 4:
        return sum_line(laid)
    return lax.psum_scatter(
        laid.reshape(groups * n * rows, columns), "fsdp", scatter_dimension=0, tiled=True
    ).reshape(n, rows, columns)


def to_owners(sums):
    return lax.all_to_all(sums, "ctx", split_axis=0, concat_axis=0, tiled=True)


PARAMS = pltpu.CompilerParams(vmem_limit_bytes=56 * 1024 * 1024)


def whole_spec(shape):
    return pl.BlockSpec(shape, lambda i: (0,) * len(shape), pipeline_mode=pl.Buffered(1))


def tile_spec(tile, width):
    return pl.BlockSpec((tile, width), lambda i: (i, 0))


def project_kernel(x_ref, gain_ref, cos_ref, sin_ref, w_ref, low_ref, q_ref, k_ref, v_ref):
    x = x_ref[...].astype(f32)
    low = (x * rms_scale(x) * gain_ref[...]).astype(bf16)
    low_ref[...] = low
    lanes = q_ref.shape[-1]
    projected = dot(low, w_ref[...])
    cosine, sine = cos_ref[...], sin_ref[...]
    q_ref[...] = rotate(projected[:, :lanes], cosine, sine).astype(bf16)
    k_ref[...] = rotate(projected[:, lanes : 2 * lanes], cosine, sine).astype(bf16)
    v_ref[...] = projected[:, 2 * lanes :].astype(bf16)


def project(x, gain, cosine, sine, weight):
    tokens, d = x.shape
    lanes = cosine.shape[1]
    tile = min(512, tokens)
    return pl.pallas_call(
        project_kernel,
        grid=(tokens // tile,),
        in_specs=[tile_spec(tile, d), whole_spec((1, d))]
        + [tile_spec(tile, lanes)] * 2
        + [whole_spec(weight.shape)],
        out_specs=[tile_spec(tile, d)] + [tile_spec(tile, lanes)] * 3,
        out_shape=[jax.ShapeDtypeStruct((tokens, d), bf16)]
        + [jax.ShapeDtypeStruct((tokens, lanes), bf16)] * 3,
        compiler_params=PARAMS,
        cost_estimate=pl.CostEstimate(
            flops=6 * tokens * d * lanes, bytes_accessed=6 * tokens * d, transcendentals=0
        ),
    )(x, gain.reshape(1, d), cosine, sine, weight)


def residual_kernel(x_ref, att_ref, gain_ref, w_ref, low_ref, res_ref):
    n, _, width = w_ref.shape
    for c in range(n):
        columns = slice(c * width, (c + 1) * width)
        res_ref[:, columns] = x_ref[:, columns].astype(f32) + dot(att_ref[...], w_ref[c])
    residual = res_ref[...]
    low_ref[...] = (residual * rms_scale(residual) * gain_ref[...]).astype(bf16)


def residuals(x, attended, gain, out_blocks):
    tokens, d = x.shape
    tile = min(512, tokens)
    return pl.pallas_call(
        residual_kernel,
        grid=(tokens // tile,),
        in_specs=[tile_spec(tile, d), tile_spec(tile, d), whole_spec((1, d)), whole_spec(out_blocks.shape)],
        out_specs=[tile_spec(tile, d), tile_spec(tile, d)],
        out_shape=[jax.ShapeDtypeStruct((tokens, d), bf16), jax.ShapeDtypeStruct((tokens, d), f32)],
        compiler_params=PARAMS,
        cost_estimate=pl.CostEstimate(
            flops=2 * tokens * d * d, bytes_accessed=10 * tokens * d, transcendentals=0
        ),
    )(x, attended, gain.reshape(1, d), out_blocks)


def gathered_residual_kernel(x_ref, gain_ref, w_ref, *refs):
    parts, (low_ref, res_ref, att, total) = refs[:8], refs[8:]
    width = w_ref.shape[-1]
    shape = low_ref.shape

    def columns(index):
        return pl.ds(pl.multiple_of(flipped(lax.axis_index("ctx"), index) * width, width), width)

    for index, part in enumerate(parts):
        att[:, columns(index)] = part[...].reshape(-1, width)
    attended = att[...]
    for index in range(8):
        total[:, columns(index)] = dot(attended, w_ref[index % 2, :, index // 2].reshape(-1, width))
    residual = total[...] + x_ref[...].reshape(attended.shape).astype(f32)
    res_ref[...] = residual.reshape(shape)
    low_ref[...] = (residual * rms_scale(residual) * gain_ref[...]).astype(bf16).reshape(shape)


def gathered_residuals(x, attended, gain, out_blocks):
    _, s, q, r, d = x.shape
    width = attended.shape[-1]
    tile = pl.BlockSpec((1, s, 1, r, d), lambda p, t: (p, 0, t, 0, 0))

    def sent(index):
        odd, other = index % 2, index // 2
        return pl.BlockSpec(
            (1, 1, 1, s, 1, r, width),
            lambda p, t: (odd, (p + odd) % 2, other, 0, flipped(t, other), 0, 0),
        )

    def fixed(shape):
        return pl.BlockSpec(shape, lambda p, t: (0,) * len(shape), pipeline_mode=pl.Buffered(1))

    return pl.pallas_call(
        gathered_residual_kernel,
        grid=(2, q),
        in_specs=[tile, fixed((1, d)), fixed(out_blocks.shape)]
        + [sent(i) for i in range(8)],
        out_specs=[tile, tile],
        out_shape=[jax.ShapeDtypeStruct(x.shape, bf16), jax.ShapeDtypeStruct(x.shape, f32)],
        scratch_shapes=[pltpu.VMEM((s * r, d), bf16), pltpu.VMEM((s * r, d), f32)],
        compiler_params=PARAMS,
        cost_estimate=pl.CostEstimate(
            flops=2 * x.size * d, bytes_accessed=10 * x.size, transcendentals=0
        ),
    )(x, gain.reshape(1, d), out_blocks, *[attended] * 8)


def hidden_kernel(skipped, low_ref, cot_ref, w_gate, w_up, w_down, *refs):
    refs = refs[skipped:]
    if len(refs) > 3:
        own_ref, hidden_ref, gate_ref, up_ref, all_ref = refs[:5]
        gather = LineGather(own_ref, all_ref, *refs[5:])
        step, steps = pl.program_id(0), pl.num_programs(0)
        gather.ride(step, steps)
    else:
        hidden_ref, gate_ref, up_ref = refs
    low = low_ref[...]
    gate, upward = dot(low, w_gate[...]), dot(low, w_up[...])
    grad_hidden = dot(cot_ref[...], w_down[...])
    sigmoid = jax.nn.sigmoid(gate)
    hidden_ref[...] = (gate * sigmoid * upward).astype(bf16)
    gate_ref[...] = (grad_hidden * upward * sigmoid * (1.0 + gate * (1.0 - sigmoid))).astype(bf16)
    up_ref[...] = (grad_hidden * gate * sigmoid).astype(bf16)
    if len(refs) > 3:
        pl.when(step == steps - 1)(gather.finish)


def block_specs(weights):
    return [
        pl.BlockSpec((array.shape[0], width), lambda i, pick=pick: (0, pick), pipeline_mode=pl.Buffered(1))
        for array, width, pick in weights
    ]


def arrays(weights):
    return [array for array, _, _ in weights]


def riding(own, shape, classes):
    if own is None:
        return [], [], [], []
    return [own], [ANYWHERE], [shape(own)], list(classes.SEMAPHORES)


def hidden_part(second_low, cot, weights, earlier=(), own=None, identity=None):
    tokens, d = second_low.shape
    step = weights[0][1]
    tile = min(512, tokens)
    extra, places, shapes, scratch = riding(own, line_shape, LineGather)
    return pl.pallas_call(
        functools.partial(hidden_kernel, len(earlier)),
        grid=(tokens // tile,),
        in_specs=[tile_spec(tile, d)] * 2
        + block_specs(weights)
        + [ANYWHERE] * len(earlier)
        + places,
        out_specs=[tile_spec(tile, step)] * 3 + places,
        out_shape=[jax.ShapeDtypeStruct((tokens, step), bf16)] * 3 + shapes,
        scratch_shapes=scratch,
        compiler_params=PARAMS if own is None else talking(identity),
        cost_estimate=pl.CostEstimate(
            flops=6 * tokens * d * step, bytes_accessed=4 * tokens * d, transcendentals=tokens * step
        ),
    )(second_low, cot, *arrays(weights), *earlier, *extra)


def back_kernel(count, *refs):
    lefts, weights = refs[:count], refs[count : 2 * count]
    total = None
    for left, weight in zip(lefts, weights):
        part = dot_rows(left[...], weight[...])
        total = part if total is None else total + part
    refs[2 * count][...] = total.astype(bf16)


def taken(weights):
    return [
        (array, width, pick)
        if width % 128 == 0
        else (lax.slice_in_dim(array, pick * width, (pick + 1) * width, axis=1), width, 0)
        for array, width, pick in weights
    ]


def back(lefts, weights, first, tokens):
    d = weights[0][0].shape[0]
    tile = min(256, tokens)
    start = first // tile
    weights = taken(weights)
    return pl.pallas_call(
        functools.partial(back_kernel, len(lefts)),
        grid=(tokens // tile,),
        in_specs=[pl.BlockSpec((tile, left.shape[1]), lambda i: (i + start, 0)) for left in lefts]
        + block_specs(weights),
        out_specs=tile_spec(tile, d),
        out_shape=jax.ShapeDtypeStruct((tokens, d), bf16),
        compiler_params=PARAMS,
        cost_estimate=pl.CostEstimate(
            flops=2 * tokens * d * sum(left.shape[1] for left in lefts),
            bytes_accessed=4 * tokens * d,
            transcendentals=0,
        ),
    )(*lefts, *arrays(weights))


FAR, BY_X, BY_Y, OWN = 3, 1, 2, 0
TURNS = ((1, FAR), (1, BY_X), (0, FAR), (1, BY_Y), (0, BY_X), (1, OWN), (0, BY_Y), (0, OWN))
PARITIES = sum(p << t for t, (p, _) in enumerate(TURNS))
PLACES = sum(q << (2 * t) for t, (_, q) in enumerate(TURNS))


def norm_back(grad, x, base, gain):
    scale = rms_scale(x)
    weighted = gain * grad
    mean = jnp.mean(weighted * x, axis=-1, keepdims=True)
    return base + scale * weighted - x * (scale * scale * scale) * mean, grad * x * scale


def back_scatter_kernel(count, skipped, *refs):
    lefts, weights, refs = refs[:count], refs[count : 2 * count], refs[2 * count + skipped :]
    x_ref, base_ref, gain_ref, grad_ref, low_ref, sum_ref = refs[:6]
    refs = refs[6:]
    given, got, sums, own, far, from_x, from_y, send_odd, came_odd, sent, came = refs
    sibling, by_x, by_y = neighbours()
    greet((sibling, by_x, by_y))
    s, r, d = own.shape
    half = s // 2

    def move(partner, source, target, send_sem, recv_sem):
        return pltpu.make_async_remote_copy(
            src_ref=source,
            dst_ref=target,
            send_sem=send_sem,
            recv_sem=recv_sem,
            device_id={"ctx": partner},
            device_id_type=MESH,
        )

    def odd_copy(q):
        return move(sibling, given.at[q], got.at[q], send_odd.at[q], came_odd.at[q])

    low_half, high_half = pl.ds(0, half), pl.ds(half, half)
    far_x = move(by_x, sums.at[FAR, low_half], far.at[low_half], sent.at[0], came.at[0])
    far_y = move(by_y, sums.at[FAR, high_half], far.at[high_half], sent.at[1], came.at[1])
    first_x = move(by_x, sums.at[BY_X, low_half], from_x.at[low_half], sent.at[2], came.at[2])
    first_y = move(by_y, sums.at[BY_Y, high_half], from_y.at[high_half], sent.at[3], came.at[3])
    last_x = move(by_x, sums.at[BY_X, high_half], from_x.at[high_half], sent.at[4], came.at[4])
    last_y = move(by_y, sums.at[BY_Y, low_half], from_y.at[low_half], sent.at[5], came.at[5])

    def turn(t, _):
        p = lax.shift_right_logical(jnp.int32(PARITIES), t) % 2
        q = lax.shift_right_logical(jnp.int32(PLACES), 2 * t) % 4
        total = None
        for left, weight in zip(lefts, weights):
            width = left.shape[-1]
            part = dot_rows(left[p, :, q].reshape(s * r, width), weight[...])
            total = part if total is None else total + part
        total = total.reshape(s, r, d)

        @pl.when(p == 1)
        def _():
            given[q] = total.astype(bf16)
            odd_copy(q).start()

        @pl.when(p == 0)
        def _():
            odd_copy(q).wait_recv()
            both = total + got[q].astype(f32)

            @pl.when(q == OWN)
            def _():
                own[...] = both

            @pl.when(q != OWN)
            def _():
                sums[q] = both.astype(bf16)

            @pl.when(q == FAR)
            def _():
                far_x.start()
                far_y.start()

            @pl.when(q == BY_X)
            def _():
                first_x.start()

            @pl.when(q == BY_Y)
            def _():
                first_y.start()

        return 0

    lax.fori_loop(0, len(TURNS), turn, 0)
    far_x.wait_recv()
    sums[BY_Y, low_half] = (sums[BY_Y, low_half].astype(f32) + far[low_half].astype(f32)).astype(bf16)
    last_y.start()
    far_y.wait_recv()
    sums[BY_X, high_half] = (sums[BY_X, high_half].astype(f32) + far[high_half].astype(f32)).astype(bf16)
    last_x.start()
    first_x.wait_recv()
    first_y.wait_recv()
    own[low_half] += from_x[low_half].astype(f32)
    own[high_half] += from_y[high_half].astype(f32)
    last_y.wait_recv()
    own[low_half] += from_y[low_half].astype(f32)
    last_x.wait_recv()
    own[high_half] += from_x[high_half].astype(f32)

    sum_ref[...] = jnp.zeros_like(sum_ref)
    slab = min(32, r)

    def finish(index, _):
        at = (index // (r // slab), pl.ds(pl.multiple_of((index % (r // slab)) * slab, slab), slab))
        grad, terms = norm_back(
            own[at], x_ref[at].astype(f32), base_ref[at].astype(f32), gain_ref[...]
        )
        grad_ref[at] = grad
        low_ref[at] = grad.astype(bf16)
        sum_ref[...] += jnp.sum(terms, axis=0, keepdims=True)
        return 0

    lax.fori_loop(0, s * (r // slab), finish, 0)
    for copy in (far_x, far_y, first_x, first_y, last_x, last_y):
        copy.wait_send()
    for q in range(4):
        odd_copy(q).wait_send()


def back_scatter(lefts, weights, shape, identity, x, base, gain, earlier=(), last=False):
    s, q, r, d = shape
    width = sum(left.shape[-1] for left in lefts)
    weights = taken(weights)
    lefts = [left.reshape(2, s, q, r, left.shape[-1]) for left in lefts]

    def fixed(whole):
        return pl.BlockSpec(whole, lambda i: (0,) * len(whole), pipeline_mode=pl.Buffered(1))

    operands = [*lefts, *arrays(weights), *earlier]
    in_specs = [fixed(left.shape) for left in lefts] + block_specs(weights)
    in_specs += [ANYWHERE] * len(earlier)
    operands += [x, base, gain.reshape(1, d)]
    in_specs += [fixed((s, r, d)), fixed((s, r, d)), fixed((1, d))]
    out_specs = [fixed((s, r, d)), fixed((s, r, d)), fixed((1, d))]
    out_shape = [
        jax.ShapeDtypeStruct((s, r, d), f32),
        jax.ShapeDtypeStruct((s, r, d), bf16),
        jax.ShapeDtypeStruct((1, d), f32),
    ]
    dma = pltpu.SemaphoreType.DMA
    return pl.pallas_call(
        functools.partial(back_scatter_kernel, len(lefts), len(earlier)),
        grid=(1,),
        in_specs=in_specs,
        out_specs=out_specs,
        out_shape=out_shape,
        scratch_shapes=[
            pltpu.VMEM((4, s, r, d), bf16),
            pltpu.VMEM((4, s, r, d), bf16),
            pltpu.VMEM((4, s, r, d), bf16),
            pltpu.VMEM((s, r, d), f32),
            pltpu.VMEM((s, r, d), bf16),
            pltpu.VMEM((s, r, d), bf16),
            pltpu.VMEM((s, r, d), bf16),
            dma((4,)),
            dma((4,)),
            dma((6,)),
            dma((6,)),
        ],
        compiler_params=talking(identity),
        cost_estimate=pl.CostEstimate(
            flops=1 if last else 16 * s * r * d * width,
            bytes_accessed=1 if last else 16 * s * r * d,
            transcendentals=0,
            remote_bytes_transferred=1 if last else 14 * s * r * d,
        ),
    )(*operands)


def riding_sums_kernel(counts, *refs):
    inputs = sum(counts) + len(counts)
    own_ref, out_ref, all_ref = refs[inputs : inputs + 3]
    gather = LineGather(own_ref, all_ref, *refs[inputs + 3 :])
    step, steps = pl.program_id(0), pl.num_programs(0)
    gather.ride(step, steps)
    token_sums_kernel(counts, *refs[:inputs], out_ref)
    pl.when(step == steps - 1)(gather.finish)


def token_sums_kernel(counts, *refs):
    out_ref = refs[-1]
    start = 0
    for count in counts:
        left, rights, refs = refs[0], refs[1 : 1 + count], refs[1 + count :]
        for right in rights:
            width = right.shape[1]
            part = dot_tokens(left[...], right[...]).astype(bf16)
            groups, owners, rows, _ = out_ref.shape
            part = part.reshape(owners, groups, rows, width)
            for owner in range(owners):
                out_ref[:, owner, :, start : start + width] = part[owner]
            start += width


def token_sums(pairs, n, rows, own=None, identity=None, earlier=()):
    groups = pairs[0][0].shape[1] // (n * rows)
    operands, in_specs, width = [], [], 0
    for left, rights in pairs:
        operands += [left, *rights]
        in_specs.append(pl.BlockSpec((left.shape[0], 2 * groups * rows), lambda i: (0, i)))
        in_specs += [whole_spec(right.shape) for right in rights]
        width += sum(right.shape[1] for right in rights)
    tokens, d = pairs[0][0].shape
    extra, places, shapes, scratch = riding(own, line_shape, LineGather)
    return pl.pallas_call(
        functools.partial(
            token_sums_kernel if own is None else riding_sums_kernel, [len(rights) for _, rights in pairs]
        ),
        grid=(n // 2,),
        in_specs=in_specs + places + [ANYWHERE] * len(earlier),
        out_specs=[pl.BlockSpec((groups, 2, rows, width), lambda i: (0, i, 0, 0))] + places,
        out_shape=[jax.ShapeDtypeStruct((groups, n, rows, width), bf16)] + shapes,
        scratch_shapes=scratch,
        compiler_params=PARAMS if own is None else talking(identity),
        cost_estimate=pl.CostEstimate(
            flops=2 * tokens * d * width, bytes_accessed=4 * tokens * d, transcendentals=0
        ),
    )(*operands, *extra, *earlier)


def output_back_kernel(low_ref, att_ref, w_ref, *refs):
    grad_ref, sum_ref, total = refs[-3:]

    @pl.when(pl.program_id(0) == 0)
    def _():
        total[...] = jnp.zeros_like(total)

    low = low_ref[...]
    grad_ref[...] = dot_rows(low, w_ref[...]).astype(bf16)
    total[...] += dot_tokens(att_ref[...], low)

    @pl.when(pl.program_id(0) == pl.num_programs(0) - 1)
    def _():
        sum_ref[...] = total[...].astype(bf16)


def output_back(grad_low, attended_low, out_rows, earlier=()):
    tokens, d = grad_low.shape
    lanes = attended_low.shape[1]
    tile = min(512, tokens)
    return pl.pallas_call(
        output_back_kernel,
        grid=(tokens // tile,),
        in_specs=[tile_spec(tile, d), tile_spec(tile, lanes), whole_spec((lanes, d))]
        + [ANYWHERE] * len(earlier),
        out_specs=[tile_spec(tile, lanes), pl.BlockSpec((lanes, d), lambda i: (0, 0))],
        out_shape=[
            jax.ShapeDtypeStruct((tokens, lanes), bf16),
            jax.ShapeDtypeStruct((lanes, d), bf16),
        ],
        scratch_shapes=[pltpu.VMEM((lanes, d), f32)],
        compiler_params=PARAMS,
        cost_estimate=pl.CostEstimate(
            flops=4 * tokens * d * lanes, bytes_accessed=2 * tokens * d, transcendentals=0
        ),
    )(grad_low, attended_low, out_rows, *earlier)


def gather_and_sum_kernel(hiddens, skipped, low_ref, gate_ref, up_ref, cot_ref, *refs):
    lefts, weights = refs[:hiddens], refs[hiddens : 2 * hiddens]
    refs = refs[2 * hiddens :]
    own_ref, refs = refs[0], refs[1 + skipped :]
    sum_ref, out_ref, all_ref = refs[:3]
    gather = Gather(own_ref, all_ref, *refs[3:])
    step, steps = pl.program_id(0), 8
    gather.ride(step, steps)
    tile = lefts[0].shape[0] // steps
    token_sums_kernel([2, 1], low_ref, gate_ref, up_ref, cot_ref, lefts[-1], sum_ref)
    rows = pl.ds(pl.multiple_of(step * tile, tile), tile)
    total = None
    for left, weight in zip(lefts, weights):
        part = dot_rows(left[rows, :], weight[...])
        total = part if total is None else total + part
    out_ref[...] = total.astype(bf16)
    pl.when(step == steps - 1)(gather.finish)


def gather_and_sum(own, second_low, grads, cot, hiddens, weights, rows, identity, earlier=()):
    tokens, d = second_low.shape
    step = hiddens[0].shape[1]
    groups = d // (8 * rows)
    column = pl.BlockSpec((tokens, groups * rows), lambda i: (0, i))
    return pl.pallas_call(
        functools.partial(gather_and_sum_kernel, len(hiddens), len(earlier)),
        grid=(8,),
        in_specs=[column, whole_spec(grads[0].shape), whole_spec(grads[1].shape), column]
        + [whole_spec(hidden.shape) for hidden in hiddens]
        + block_specs(weights)
        + [ANYWHERE] * (1 + len(earlier)),
        out_specs=[
            pl.BlockSpec((groups, 1, rows, 3 * step), lambda i: (0, i, 0, 0)),
            tile_spec(tokens // 8, d),
            ANYWHERE,
        ],
        out_shape=[
            jax.ShapeDtypeStruct((groups, 8, rows, 3 * step), bf16),
            jax.ShapeDtypeStruct((tokens, d), bf16),
            gathered_shape(own),
        ],
        scratch_shapes=list(Gather.SEMAPHORES),
        compiler_params=talking(identity),
        cost_estimate=pl.CostEstimate(
            flops=14 * tokens * d * step, bytes_accessed=12 * tokens * d, transcendentals=0
        ),
    )(second_low, *grads, cot, *hiddens, *arrays(weights), own, *earlier)


def spread_kernel(count, *refs):
    parts, out_ref, last_ref = refs[:count], refs[count], refs[count + 1]
    senders, _, width = parts[0].shape

    def write(target):
        for sender in range(senders):
            for index, part in enumerate(parts):
                start = (sender * count + index) * width
                target[:, start : start + width] = part[sender].astype(f32)

    pl.when(pl.program_id(0) < 2)(lambda: write(out_ref))
    pl.when(pl.program_id(0) == 2)(lambda: write(last_ref))


def spread(parts, width):
    n, rows, _ = parts[0].shape
    count = len(parts)
    pair = min(n, 2)
    wide = pair * count * width
    turns = n // pair
    return pl.pallas_call(
        functools.partial(spread_kernel, count),
        grid=(3, turns),
        in_specs=[pl.BlockSpec((pair, rows, width), lambda third, i: (i, 0, third))] * count,
        out_specs=[
            pl.BlockSpec((rows, wide), lambda third, i: (0, jnp.minimum(third * turns + i, 2 * turns - 1))),
            pl.BlockSpec((rows, wide), lambda third, i: (0, jnp.maximum(third - 1, 0) * i)),
        ],
        out_shape=[
            jax.ShapeDtypeStruct((rows, 2 * n * count * width), f32),
            jax.ShapeDtypeStruct((rows, n * count * width), f32),
        ],
        compiler_params=PARAMS,
        cost_estimate=pl.CostEstimate(
            flops=0, bytes_accessed=18 * n * rows * count * width, transcendentals=0
        ),
    )(*parts)


def spread_all_kernel(part_ref, _, out_ref):
    senders, _, width = part_ref.shape
    for sender in range(senders):
        out_ref[:, sender * width : (sender + 1) * width] = part_ref[sender].astype(f32)


def spread_all(part, width, earlier):
    n, rows, _ = part.shape
    return pl.pallas_call(
        spread_all_kernel,
        grid=(3,),
        in_specs=[pl.BlockSpec((n, rows, width), lambda i: (0, 0, i)), ANYWHERE],
        out_specs=pl.BlockSpec((rows, n * width), lambda i: (0, i)),
        out_shape=jax.ShapeDtypeStruct((rows, 3 * n * width), f32),
        compiler_params=PARAMS,
        cost_estimate=pl.CostEstimate(
            flops=0, bytes_accessed=18 * n * rows * width, transcendentals=0
        ),
    )(part, earlier)


def only(values, head, heads):
    if heads == 1:
        return values
    lane = lax.broadcasted_iota(jnp.int32, values.shape, 1)
    inside = (lane >= head * HEAD_SIZE) & (lane < (head + 1) * HEAD_SIZE)
    return jnp.where(inside, values, jnp.zeros_like(values))


def forward_kernel(heads, q_spot, k_spot, q_ref, k_ref, v_ref, *refs):
    if len(refs) > 2:
        own_ref, low_ref, total_ref, all_ref = refs[:4]
        gather = Gather(own_ref, all_ref, *refs[4:])
        steps = pl.num_programs(0) * pl.num_programs(1) * pl.num_programs(2)
        step = (pl.program_id(0) * pl.num_programs(1) + pl.program_id(1)) * pl.num_programs(2)
        step += pl.program_id(2)
        gather.ride(step, steps)
    else:
        low_ref, total_ref = refs
    lanes = q_ref.shape[-1]
    queries = q_ref[0, 0] * bf16(HEAD_SIZE**-0.5)
    keys = k_ref[:, 0].reshape(-1, lanes)
    values = v_ref[:, 0].reshape(-1, lanes)
    allowed = k_spot[0] <= q_spot[0, 0]
    attended = jnp.zeros(queries.shape, f32)
    for head in range(heads):
        scores = dot_rows(keys, only(queries, head, heads))
        scores = jnp.where(allowed, scores, -1e30)
        highest = jnp.max(scores, axis=0, keepdims=True)
        raised = jnp.exp(scores - highest)
        summed = jnp.sum(raised, axis=0, keepdims=True)
        probs = (raised * (1.0 / summed)).astype(bf16)
        total_ref[0, 0, head : head + 1, :] = highest + jnp.log(summed)
        attended += dot_tokens(probs, only(values, head, heads))
    low_ref[0, 0] = attended.astype(bf16)
    if len(refs) > 2:
        pl.when(step == steps - 1)(gather.finish)


def backward_kernel(
    heads, q_spot, k_spot, q_ref, k_ref, v_ref, grad_ref, total_ref, qc_ref, qs_ref, kc_ref, ks_ref, *refs
):
    dq_ref, dk_ref, dv_ref, dk_sum, dv_sum = refs[-5:]
    lanes = q_ref.shape[-1]
    scale = HEAD_SIZE**-0.5
    step = pl.program_id(1) * pl.num_programs(2) + pl.program_id(2)

    @pl.when(step == 0)
    def _():
        dk_sum[...] = jnp.zeros_like(dk_sum)
        dv_sum[...] = jnp.zeros_like(dv_sum)

    queries = q_ref[0, 0] * bf16(scale)
    grads = grad_ref[0, 0]
    keys = k_ref[:, 0].reshape(-1, lanes)
    values = v_ref[:, 0].reshape(-1, lanes)
    allowed = k_spot[0] <= q_spot[0, 0]
    grad_q = jnp.zeros(queries.shape, f32)
    for head in range(heads):
        query = only(queries, head, heads)
        grad = only(grads, head, heads)
        scores = jnp.where(allowed, dot_rows(keys, query), -1e30)
        probs = jnp.exp(scores - total_ref[0, 0, head : head + 1, :])
        dv_sum[...] += dot(probs.astype(bf16), grad)
        weighted = probs * dot_rows(values, grad)
        delta = jnp.sum(weighted, axis=0, keepdims=True)
        grad_scores = (weighted - probs * delta).astype(bf16)
        dk_sum[...] += dot(grad_scores, query)
        grad_q += dot_tokens(grad_scores, only(keys, head, heads))
    dq_ref[0, 0] = rotate_back(grad_q * scale, qc_ref[0, 0], qs_ref[0, 0]).astype(bf16)

    @pl.when(step == pl.num_programs(1) * pl.num_programs(2) - 1)
    def _():
        shape = (dk_ref.shape[0],) + dk_ref.shape[2:]
        cosine = kc_ref[:, 0].reshape(-1, lanes)
        sine = ks_ref[:, 0].reshape(-1, lanes)
        dk_ref[:, 0] = rotate_back(dk_sum[...], cosine, sine).astype(bf16).reshape(shape)
        dv_ref[:, 0] = dv_sum[...].astype(bf16).reshape(shape)


def attention_specs(shape, heads):
    p, s, rows, lanes = shape
    tile = min(256, rows)
    one = pl.BlockSpec((1, 1, tile, lanes), lambda i, j, t: (j, i, t, 0))
    side = pl.BlockSpec((p, 1, rows, lanes), lambda i, j, t: (0, i, 0, 0))
    stat = pl.BlockSpec((1, 1, heads, tile), lambda i, j, t: (j, i, 0, t))
    q_spot = pl.BlockSpec((1, 1, 1, tile), lambda i, j, t: (j, i, 0, t))
    k_spot = pl.BlockSpec((1, p * rows, 1), lambda i, j, t: (i, 0, 0))
    return (s, p, rows // tile), one, side, stat, q_spot, k_spot


def attend(q_spot, k_spot, queries, keys, values, own=None, identity=None):
    p, s, rows, lanes = queries.shape
    heads = lanes // HEAD_SIZE
    grid, one, side, stat, q_spec, k_spec = attention_specs(queries.shape, heads)
    pairs = p * rows * s * p * rows
    out_shape = [
        jax.ShapeDtypeStruct(queries.shape, bf16),
        jax.ShapeDtypeStruct((p, s, heads, rows), f32),
    ]
    riding = own is not None
    return pl.pallas_call(
        functools.partial(forward_kernel, heads),
        grid=grid,
        in_specs=[q_spec, k_spec, one, side, side] + [ANYWHERE] * riding,
        out_specs=[one, stat] + [ANYWHERE] * riding,
        out_shape=out_shape + ([gathered_shape(own)] if riding else []),
        scratch_shapes=list(Gather.SEMAPHORES) if riding else [],
        compiler_params=talking(identity) if riding else PARAMS,
        cost_estimate=pl.CostEstimate(
            flops=pairs * heads * 2048, bytes_accessed=queries.size * 14, transcendentals=pairs * heads
        ),
    )(q_spot, k_spot, queries, keys, values, *([own] if riding else []))


def attend_back(q_spot, k_spot, queries, keys, values, grads, totals, cosine, sine, earlier=()):
    p, s, rows, lanes = queries.shape
    heads = lanes // HEAD_SIZE
    grid, one, side, stat, q_spec, k_spec = attention_specs(queries.shape, heads)
    pairs = p * rows * s * p * rows
    return pl.pallas_call(
        functools.partial(backward_kernel, heads),
        grid=grid,
        in_specs=[q_spec, k_spec, one, side, side, one, stat, one, one, side, side]
        + [ANYWHERE] * len(earlier),
        out_specs=[one, side, side],
        out_shape=[jax.ShapeDtypeStruct(queries.shape, bf16)] * 3,
        scratch_shapes=[pltpu.VMEM((p * rows, lanes), f32)] * 2,
        compiler_params=PARAMS,
        cost_estimate=pl.CostEstimate(
            flops=pairs * heads * 5120, bytes_accessed=queries.size * 20, transcendentals=pairs * heads
        ),
    )(q_spot, k_spot, queries, keys, values, grads, totals, cosine, sine, cosine, sine, *earlier)


def on_device(
    plane,
    inputs,
    positions,
    first_gain,
    attention_weight,
    output_weight,
    second_gain,
    gate_up_weight,
    down_weight,
    cotangent,
):
    s, r, d = inputs.shape
    n = plane.size
    ff = down_weight.shape[1]
    me = lax.axis_index("ctx")
    lanes = d // n
    mine = ff // n
    step = mine // CHUNKS
    tokens = s * r * n
    rows = d // (n * lax.axis_size("fsdp"))
    half = tokens // 2
    group = (2, s, n // 2 * r)
    blocks = (s, n // 2, r, d)

    def columns(weight, start, width):
        return lax.dynamic_slice_in_dim(weight, start, width, 1)

    qkv = gather_rows(
        jnp.concatenate(
            [columns(attention_weight, part * d + me * lanes, lanes) for part in range(3)], axis=1
        )
    )
    out_own = gather_rows(columns(output_weight, me * lanes, lanes))
    ffn = []
    riders = []
    for chunk in range(CHUNKS):
        start = me * mine + chunk * step
        parts = [
            columns(gate_up_weight, start, step),
            columns(gate_up_weight, ff + start, step),
            columns(down_weight, start, step),
        ]
        if plane.relative and lax.axis_size("fsdp") == 4 and chunk >= CHUNKS - RIDING:
            riders += parts
            ffn.append([])
        else:
            whole = gather_rows(jnp.concatenate(parts, axis=1))
            ffn.append([(whole, step, part) for part in range(3)])
    whole_inputs, cot = plane.gather([inputs, cotangent], 1)

    places = plane.order(positions.reshape(s, n, r)).reshape(group)
    q_spot = places[:, :, None, :]
    k_spot = places.transpose(1, 0, 2).reshape(s, n * r, 1)
    cosine, sine = rope_tables(places.reshape(tokens), lanes)
    normed_low, queries, keys, values = project(
        whole_inputs.reshape(tokens, d), first_gain, cosine, sine, qkv
    )
    queries, keys, values, cosine, sine = (
        part.reshape(*group, lanes) for part in (queries, keys, values, cosine, sine)
    )
    if plane.relative:
        attended_low, totals, out_blocks = attend(
            q_spot, k_spot, queries, keys, values, out_own.reshape(2, d // 2, lanes), 2
        )
        (attended_whole,) = plane.gather([attended_low.reshape(2, half, lanes)], 3)
        second_low, residual = gathered_residuals(
            whole_inputs,
            attended_whole.reshape(2, 2, 4, s, 4, r, lanes),
            second_gain,
            out_blocks,
        )
        second_low = second_low.reshape(tokens, d)
        residual = residual[0, :, 0]
    else:
        attended_low, totals = attend(q_spot, k_spot, queries, keys, values)
        out_blocks = lax.all_gather(out_own, "ctx", axis=0, tiled=False)
        attended_whole = lax.all_gather(
            attended_low.reshape(tokens, lanes), "ctx", axis=1, tiled=True
        )
        second_low, residual = residuals(
            whole_inputs.reshape(tokens, d), attended_whole, second_gain, out_blocks
        )
        residual = lax.dynamic_index_in_dim(residual.reshape(2, *blocks), me % 2, 0, keepdims=False)
        residual = lax.dynamic_index_in_dim(residual, me // 2, 1, keepdims=False)
    cot = cot.reshape(tokens, d)
    attended_low = attended_low.reshape(tokens, lanes)

    if plane.relative:
        out_rows = lax.dynamic_slice(
            out_blocks, (0, me // 4, 0, (me % 4) * lanes, 0), (2, 1, 4, lanes, lanes)
        ).reshape(2, 2, 2, lanes, lanes)
        for axis, bit in ((0, 1), (1, 4), (2, 2)):
            out_rows = jnp.where((me & bit) != 0, jnp.flip(out_rows, axis), out_rows)
        out_rows = out_rows.transpose(3, 1, 2, 0, 4).reshape(lanes, d)
    else:
        out_rows = lax.dynamic_slice_in_dim(out_blocks, me * lanes, lanes, 1)
        out_rows = out_rows.transpose(1, 0, 2).reshape(lanes, d)

    def summed(pairs, earlier=()):
        if plane.relative:
            return token_sums(pairs, n, rows, earlier=earlier)[0]
        partial = [dot_tokens(left, right) for left, rights in pairs for right in rights]
        return by_owners(jnp.concatenate(partial, axis=1), n, rows)

    hiddens, grads, partials, sums = [], [], [], []
    landed = []

    def rider():
        if len(landed) == len(riders):
            return None, None
        return riders[len(landed)], 10 + len(landed)

    def land(results, count):
        for whole in results[count:]:
            landed.append(whole)
            for weights in ffn:
                if len(weights) < 3:
                    weights.append((whole, step, 0))
                    break
        return results[:count]

    for chunk, weights in enumerate(ffn):
        hidden, *grad_gate_up = land(
            hidden_part(
                second_low,
                cot,
                taken(weights),
                partials[-1:] or [out_rows],
                *rider(),
            ),
            3,
        )
        hiddens.append(hidden)
        grads.append(grad_gate_up)
        pairs = [(second_low, grad_gate_up), (cot, [hidden])]
        if not plane.relative:
            partials.append(summed(pairs))
        elif chunk < CHUNKS - 1:
            partials += land(token_sums(pairs, n, rows, *rider()), 1)
        if len(partials) > len(sums):
            sums.append(sum_rows(partials[-1], chunk < PERMUTED))

    def apart(lefts, weights):
        odd, even = back(lefts, weights, half, half), back(lefts, weights, 0, half)
        return plane.scatter(odd.reshape(blocks), even.reshape(blocks))

    def norm_step(identity, lefts, weights, x, base, gain, earlier, last=False):
        if plane.relative:
            return back_scatter(lefts, weights, blocks, identity, x, base, gain, earlier, last)
        grad, terms = norm_back(apart(lefts, weights), x.astype(f32), base.astype(f32), gain)
        return grad, grad.astype(bf16), jnp.sum(terms, axis=(0, 1))

    grad_residual, grad_residual_low, second_gain_part = norm_step(
        5,
        [grad for pair in grads for grad in pair],
        [weight for weights in ffn for weight in weights[:2]],
        residual,
        cotangent,
        second_gain,
        partials[-1:],
    )
    downs = [weights[2] for weights in ffn]
    if plane.relative:
        last, output_parts, grad_low = gather_and_sum(
            grad_residual_low, second_low, grads[-1], cot, hiddens, downs, rows, 6, sums[:1]
        )
        sums.append(sum_rows(last))
    else:
        (grad_low,) = plane.gather([grad_residual_low], 6)
    grad_low = grad_low.reshape(tokens, d)

    grad_attended, out_part = output_back(grad_low, attended_low, out_rows, sums[1:2])
    grad_projected = attend_back(
        q_spot, k_spot, queries, keys, values, grad_attended.reshape(*group, lanes), totals, cosine, sine
    )
    grad_projected = [part.reshape(tokens, lanes) for part in grad_projected]
    attention_parts = summed([(normed_low, grad_projected)])
    attention_sums = sum_rows(attention_parts)
    grad_output_weight = lax.psum_scatter(
        after(out_part, attention_parts), "fsdp", scatter_dimension=0, tiled=True
    )
    grad_input, _, first_gain_part = norm_step(
        7,
        grad_projected,
        [(qkv, lanes, part) for part in range(3)],
        inputs,
        grad_residual,
        first_gain,
        [attention_parts],
        True,
    )
    gains = jnp.stack([first_gain_part.reshape(d), second_gain_part.reshape(d)])
    gains = gains.reshape(2, d // rows, rows).transpose(1, 0, 2)
    gains = jnp.sum(
        lax.all_to_all(gains, ("ctx", "fsdp"), split_axis=0, concat_axis=0, tiled=True), axis=0
    )
    if plane.relative:
        output_parts = output_parts.reshape(2, *blocks)
        odd = lax.dynamic_index_in_dim(output_parts, 1 + zero_of(grad_input), 0, keepdims=False)
        output = residual + plane.scatter(odd, output_parts[0])
    else:
        output = residual + apart(hiddens, downs)[0]

    early = to_owners(after(jnp.concatenate(sums[:-1], axis=2), grad_input))
    late = to_owners(after(sums[-1], grad_input))
    attention_sums = to_owners(attention_sums)
    parts = [early[:, :, 3 * step * chunk : 3 * step * (chunk + 1)] for chunk in range(CHUNKS - 1)]
    if plane.relative:
        grad_gate_up, grad_down = spread([*parts, late], step)
        grad_attention = spread_all(attention_sums, lanes, grad_down)
    else:
        whole = jnp.stack([part.reshape(n, rows, 3, step) for part in [*parts, late]], axis=3)
        whole = whole.transpose(1, 2, 0, 3, 4).reshape(rows, 3, ff).astype(f32)
        grad_gate_up, grad_down = whole[:, :2].reshape(rows, 2 * ff), whole[:, 2]
        grad_attention = attention_sums.reshape(n, rows, 3, lanes).transpose(1, 2, 0, 3)
        grad_attention = grad_attention.reshape(rows, 3 * d).astype(f32)
    return (
        output,
        grad_input,
        grad_attention,
        after(grad_output_weight, grad_attention).astype(f32),
        grad_gate_up,
        grad_down,
        gains[0],
        gains[1],
    )


def solution(mesh):
    plane = Plane(mesh.shape["ctx"])
    return jax.shard_map(
        functools.partial(on_device, plane),
        mesh=mesh,
        in_specs=(
            P("fsdp", "ctx", None),
            P("fsdp", None),
            P(),
            P("fsdp", None),
            P("fsdp", None),
            P(),
            P("fsdp", None),
            P("fsdp", None),
            P("fsdp", "ctx", None),
        ),
        out_specs=(
            P("fsdp", "ctx", None),
            P("fsdp", "ctx", None),
            P(("ctx", "fsdp"), None),
            P(("ctx", "fsdp"), None),
            P(("ctx", "fsdp"), None),
            P(("ctx", "fsdp"), None),
            P(("ctx", "fsdp")),
            P(("ctx", "fsdp")),
        ),
        check_vma=False,
    )
```

```python
import functools

import jax
import jax.numpy as jnp
from jax import lax
from jax.experimental import pallas as pl
from jax.experimental.pallas import tpu as pltpu
from jax.sharding import PartitionSpec as P

HEAD_SIZE = 64
EPSILON = 1e-05
ROPE_BASE = 130000.0
CHUNKS = 4
ORDER = (0, 3, 1, 2)
RIDING = 3

f32 = jnp.float32
bf16 = jnp.bfloat16


def rms_scale(values):
    return lax.rsqrt(jnp.mean(values * values, axis=-1, keepdims=True) + EPSILON)


def dot(left, right):
    return jnp.dot(left, right, preferred_element_type=f32)


def dot_rows(left, right):
    return lax.dot_general(left, right, (((1,), (1,)), ((), ())), preferred_element_type=f32)


def dot_tokens(left, right):
    return lax.dot_general(left, right, (((0,), (0,)), ((), ())), preferred_element_type=f32)


def tables_kernel(places_ref, _, cos_ref, sin_ref):
    half = HEAD_SIZE // 2
    width = cos_ref.shape[1]
    narrow = min(width, 128)
    lane = lax.broadcasted_iota(jnp.int32, (1, narrow), 1) % half
    inverse = jnp.exp(-(2.0 * lane.astype(f32) / HEAD_SIZE) * jnp.log(f32(ROPE_BASE)))
    angles = places_ref[...].astype(f32) * inverse
    cosine, sine = jnp.cos(angles), jnp.sin(angles)
    for start in range(0, width, narrow):
        cos_ref[:, start : start + narrow] = cosine
        sin_ref[:, start : start + narrow] = sine


def rope_tables(places, lanes, earlier):
    tokens = places.shape[0]
    tile = min(512, tokens)
    return pl.pallas_call(
        tables_kernel,
        grid=(tokens // tile,),
        in_specs=[pl.BlockSpec((tile, 1), lambda i: (i, 0)), ANYWHERE],
        out_specs=[pl.BlockSpec((tile, lanes), lambda i: (i, 0))] * 2,
        out_shape=[jax.ShapeDtypeStruct((tokens, lanes), f32)] * 2,
        cost_estimate=pl.CostEstimate(
            flops=100 * tokens * lanes, bytes_accessed=8 * tokens * lanes, transcendentals=0
        ),
    )(places.reshape(tokens, 1), earlier)


def other_half(values):
    half = HEAD_SIZE // 2
    lanes = values.shape[-1]
    if lanes == HEAD_SIZE:
        return jnp.concatenate([-values[:, half:], values[:, :half]], axis=1)
    lane = lax.broadcasted_iota(jnp.int32, values.shape, 1)
    return jnp.where(
        lane % HEAD_SIZE < half,
        -pltpu.roll(values, lanes - half, 1),
        pltpu.roll(values, half, 1),
    )


def rotate(values, cosine, sine):
    return values * cosine + other_half(values) * sine


def rotate_back(gradient, cosine, sine):
    return gradient * cosine - other_half(gradient * sine)


MESH = pl.DeviceIdType.MESH


def greet(line=False):
    barrier = pltpu.get_barrier_semaphore()
    partners = [{"ctx": partner} for partner in neighbours()]
    size = lax.axis_size("fsdp")
    if line:
        z = lax.axis_index("fsdp")
        partners += [{"fsdp": (z + shift) % size} for shift in range(1, size)]
    for partner in partners:
        pl.semaphore_signal(barrier, inc=1, device_id=partner, device_id_type=MESH)
    pl.semaphore_wait(barrier, len(partners))


def flipped(place, bits):
    for bit in (1, 2, 4):
        if bits & bit:
            place = place + bit - 2 * bit * ((place // bit) % 2)
    return place


def neighbours():
    me = lax.axis_index("ctx")
    return [flipped(me, bit) for bit in (1, 2, 4)]


class Gather:
    SEMAPHORES = (
        pltpu.SemaphoreType.DMA((2,)),
        pltpu.SemaphoreType.DMA((14,)),
        pltpu.SemaphoreType.DMA((14,)),
    )

    def __init__(self, own, out, local, sent, came):
        sibling, by_x, by_y = neighbours()
        routes = [
            (by_x, own.at[0], out.at[0, 0, 1]),
            (by_y, own.at[1], out.at[0, 1, 2]),
            (by_x, own.at[1], out.at[0, 1, 1]),
            (by_y, own.at[0], out.at[0, 0, 2]),
            (by_y, out.at[0, 0, 1], out.at[0, 0, 3]),
            (by_x, out.at[0, 1, 2], out.at[0, 1, 3]),
        ]
        for h in range(2):
            routes.append((sibling, own.at[h], out.at[1, h, 0]))
        for h, q in ((0, 1), (1, 2), (1, 1), (0, 2), (0, 3), (1, 3)):
            routes.append((sibling, out.at[0, h, q], out.at[1, h, q]))
        self.copies = [
            pltpu.make_async_remote_copy(
                src_ref=source,
                dst_ref=target,
                send_sem=sent.at[index],
                recv_sem=came.at[index],
                device_id={"ctx": partner},
                device_id_type=MESH,
            )
            for index, (partner, source, target) in enumerate(routes)
        ]
        self.kept = [
            pltpu.make_async_copy(own.at[h], out.at[0, h, 0], local.at[h]) for h in range(2)
        ]

    def send(self):
        for index in (0, 1, 2, 3, 6, 7):
            self.copies[index].start()
        for copy in self.kept:
            copy.start()

    def pass_on(self):
        self.copies[0].wait_recv()
        self.copies[4].start()
        self.copies[8].start()
        self.copies[1].wait_recv()
        self.copies[5].start()
        self.copies[9].start()

    def pass_seconds(self):
        self.copies[2].wait_recv()
        self.copies[10].start()
        self.copies[3].wait_recv()
        self.copies[11].start()

    def finish(self):
        self.copies[4].wait_recv()
        self.copies[12].start()
        self.copies[5].wait_recv()
        self.copies[13].start()
        for copy in self.copies[6:]:
            copy.wait_recv()
        for copy in self.copies:
            copy.wait_send()
        for copy in self.kept:
            copy.wait()

    def ride(self, step, steps):
        for turn, phase in ((0, self.send), (steps // 2, self.pass_on), (steps - 1, self.pass_seconds)):
            pl.when(step == turn)(phase)


class LineGather:
    SEMAPHORES = (
        pltpu.SemaphoreType.DMA((1,)),
        pltpu.SemaphoreType.DMA((3,)),
        pltpu.SemaphoreType.DMA((3,)),
    )

    def __init__(self, own, out, local, sent, came):
        z = lax.axis_index("fsdp")
        size = own.shape[0]

        def rows(place):
            return out.at[pl.ds(pl.multiple_of(place * size, size), size)]

        held = z // 2 + 2 * (z % 2)
        routes = [
            ((z + 1) % 4, own, rows(z)),
            ((z + 3) % 4, own, rows(z)),
            (2 * (1 - z % 2) + z // 2, rows(held), rows(held)),
        ]
        if lax.axis_size("fsdp") == 1:
            routes = []
        copies = [
            pltpu.make_async_remote_copy(
                src_ref=source,
                dst_ref=target,
                send_sem=sent.at[index],
                recv_sem=came.at[index],
                device_id={"fsdp": partner},
                device_id_type=MESH,
            )
            for index, (partner, source, target) in enumerate(routes)
        ]
        self.first, self.second = copies[:2], copies[2:]
        self.kept = pltpu.make_async_copy(own, rows(z), local.at[0])

    def send(self):
        for copy in (*self.first, self.kept):
            copy.start()

    def pass_on(self):
        for copy in self.first:
            copy.wait_recv()
        self.kept.wait()
        for copy in self.second:
            copy.start()

    def finish(self):
        for copy in self.second:
            copy.wait_recv()
        for copy in (*self.first, *self.second):
            copy.wait_send()

    def ride(self, step, steps):
        pl.when(step == 0)(self.send)
        pl.when(step == steps - 1)(self.pass_on)


def line_shape(own):
    return jax.ShapeDtypeStruct((lax.axis_size("fsdp") * own.shape[0], own.shape[1]), own.dtype)


def gathered_shape(own):
    return jax.ShapeDtypeStruct((2, 2, 4) + own.shape[1:], own.dtype)


ANYWHERE = pl.BlockSpec(memory_space=pl.ANY)
STAGED = pl.BlockSpec(memory_space=pltpu.VMEM)


def talking(identity):
    return pltpu.CompilerParams(
        collective_id=identity, has_side_effects=True, vmem_limit_bytes=56 * 1024 * 1024
    )


def gather_kernel(count, lines, *refs):
    sources, targets, refs = refs[: count + lines], refs[count + lines : 2 * (count + lines)], refs[2 * (count + lines) :]
    moves = [
        (Gather if i < count else LineGather)(sources[i], targets[i], *refs[3 * i : 3 * i + 3])
        for i in range(count + lines)
    ]
    gathers, lines = moves[:count], moves[count:]
    greet(line=True)
    gathers[0].send()
    for line in lines:
        line.send()
    gathers[0].pass_on()
    for gather in gathers[1:]:
        gather.send()
    gathers[0].pass_seconds()
    for line in lines:
        line.pass_on()
    gathers[0].finish()
    for gather in gathers[1:]:
        gather.pass_on()
        gather.pass_seconds()
        gather.finish()
    for line in lines:
        line.finish()


def gather_in_plane(owns, lines, identity):
    size = sum(own.size * own.dtype.itemsize for own in owns)
    count = len(owns) + len(lines)
    return pl.pallas_call(
        functools.partial(gather_kernel, len(owns), len(lines)),
        in_specs=[STAGED] * count,
        out_specs=[ANYWHERE] * count,
        out_shape=[gathered_shape(own) for own in owns] + [line_shape(own) for own in lines],
        scratch_shapes=list(Gather.SEMAPHORES) * len(owns) + list(LineGather.SEMAPHORES) * len(lines),
        compiler_params=talking(identity),
        cost_estimate=pl.CostEstimate(
            flops=0, bytes_accessed=16 * size, transcendentals=0, remote_bytes_transferred=7 * size
        ),
    )(*owns, *lines)


class Plane:
    def __init__(self, size):
        self.size = size
        self.relative = size == 8

    def swap(self, value, bits):
        return lax.ppermute(value, "ctx", [(i, i ^ bits) for i in range(self.size)])

    def gather(self, owns):
        wholes = [lax.all_gather(own, "ctx", axis=1, tiled=False) for own in owns]
        s, n, r, d = wholes[0].shape
        return [whole.reshape(s, n // 2, 2, r, d).transpose(2, 0, 1, 3, 4) for whole in wholes]

    def scatter(self, odd, even):
        if not self.relative:
            both = jnp.stack([even, odd], axis=2)
            s, q, p, r, d = both.shape
            return lax.psum_scatter(
                both.reshape(s, q * p, r, d), "ctx", scatter_dimension=1, tiled=False
            ).astype(f32)
        half = odd.shape[0] // 2
        came = self.swap(odd, 1)
        both = (even.astype(f32) + came.astype(f32)).astype(bf16)
        far_x, far_y = self.swap(both[:half, 3], 2), self.swap(both[half:, 3], 4)
        direct_x, direct_y = self.swap(both[:half, 1], 2), self.swap(both[half:, 2], 4)
        to_x = (both[half:, 1].astype(f32) + far_y.astype(f32)).astype(bf16)
        to_y = (both[:half, 2].astype(f32) + far_x.astype(f32)).astype(bf16)
        later_x, later_y = self.swap(to_x, 2), self.swap(to_y, 4)
        from_x = jnp.concatenate([direct_x, later_x], axis=0).astype(f32)
        from_y = jnp.concatenate([later_y, direct_y], axis=0).astype(f32)
        return both[:, 0].astype(f32) + from_x + from_y

    def order(self, places):
        s, n, r = places.shape
        if self.relative:
            me = lax.axis_index("ctx")
            bits = places.reshape(s, 2, 2, 2, r)
            for axis, bit in ((1, 4), (2, 2), (3, 1)):
                bits = jnp.where((me & bit) != 0, jnp.flip(bits, axis), bits)
            places = bits.reshape(s, n, r)
        return places.reshape(s, n // 2, 2, r).transpose(2, 0, 1, 3)


def zero_of(value):
    first = lax.slice(value, (0,) * value.ndim, (1,) * value.ndim).reshape(()).astype(f32)
    return (first != first).astype(jnp.int32)


def after(value, earlier):
    return jnp.where(zero_of(earlier) == 0, value, jnp.zeros_like(value))


def gather_rows(own):
    return lax.all_gather(own, "fsdp", axis=0, tiled=True)


def by_owners(partial, n, rows):
    depth, columns = partial.shape
    return partial.astype(bf16).reshape(n, depth // (n * rows), rows, columns).transpose(1, 0, 2, 3)


def sum_rows(laid):
    groups, n, rows, columns = laid.shape
    return lax.psum_scatter(
        laid.reshape(groups * n * rows, columns), "fsdp", scatter_dimension=0, tiled=True
    ).reshape(n, rows, columns)


def to_owners(sums):
    return lax.all_to_all(sums, "ctx", split_axis=0, concat_axis=0, tiled=True)


PARAMS = pltpu.CompilerParams(vmem_limit_bytes=56 * 1024 * 1024)


def whole_spec(shape):
    return pl.BlockSpec(shape, lambda i: (0,) * len(shape), pipeline_mode=pl.Buffered(1))


def tile_spec(tile, width):
    return pl.BlockSpec((tile, width), lambda i: (i, 0))


def project_kernel(x_ref, gain_ref, cos_ref, sin_ref, w_ref, low_ref, q_ref, k_ref, v_ref):
    x = x_ref[...].astype(f32)
    low = (x * rms_scale(x) * gain_ref[...]).astype(bf16)
    low_ref[...] = low
    lanes = q_ref.shape[-1]
    projected = dot(low, w_ref[...])
    cosine, sine = cos_ref[...], sin_ref[...]
    q_ref[...] = rotate(projected[:, :lanes], cosine, sine).astype(bf16)
    k_ref[...] = rotate(projected[:, lanes : 2 * lanes], cosine, sine).astype(bf16)
    v_ref[...] = projected[:, 2 * lanes :].astype(bf16)


def project(x, gain, cosine, sine, weight):
    tokens, d = x.shape
    lanes = cosine.shape[1]
    tile = min(512, tokens)
    return pl.pallas_call(
        project_kernel,
        grid=(tokens // tile,),
        in_specs=[tile_spec(tile, d), whole_spec((1, d))]
        + [tile_spec(tile, lanes)] * 2
        + [whole_spec(weight.shape)],
        out_specs=[tile_spec(tile, d)] + [tile_spec(tile, lanes)] * 3,
        out_shape=[jax.ShapeDtypeStruct((tokens, d), bf16)]
        + [jax.ShapeDtypeStruct((tokens, lanes), bf16)] * 3,
        compiler_params=PARAMS,
        cost_estimate=pl.CostEstimate(
            flops=6 * tokens * d * lanes, bytes_accessed=6 * tokens * d, transcendentals=0
        ),
    )(x, gain.reshape(1, d), cosine, sine, weight)


def residual_kernel(x_ref, att_ref, gain_ref, w_ref, low_ref, res_ref):
    n, _, width = w_ref.shape
    for c in range(n):
        columns = slice(c * width, (c + 1) * width)
        res_ref[:, columns] = x_ref[:, columns].astype(f32) + dot(att_ref[...], w_ref[c])
    residual = res_ref[...]
    low_ref[...] = (residual * rms_scale(residual) * gain_ref[...]).astype(bf16)


def residuals(x, attended, gain, out_blocks):
    tokens, d = x.shape
    tile = min(512, tokens)
    return pl.pallas_call(
        residual_kernel,
        grid=(tokens // tile,),
        in_specs=[tile_spec(tile, d), tile_spec(tile, d), whole_spec((1, d)), whole_spec(out_blocks.shape)],
        out_specs=[tile_spec(tile, d), tile_spec(tile, d)],
        out_shape=[jax.ShapeDtypeStruct((tokens, d), bf16), jax.ShapeDtypeStruct((tokens, d), f32)],
        compiler_params=PARAMS,
        cost_estimate=pl.CostEstimate(
            flops=2 * tokens * d * d, bytes_accessed=10 * tokens * d, transcendentals=0
        ),
    )(x, attended, gain.reshape(1, d), out_blocks)


def gathered_residual_kernel(x_ref, gain_ref, w_ref, *refs):
    parts, (own_ref, low_ref, res_ref, all_ref, att, total) = refs[:8], refs[8:14]
    line = LineGather(own_ref, all_ref, *refs[14:])
    step, steps = pl.program_id(0) * pl.num_programs(1) + pl.program_id(1), 8
    pl.when(step == 0)(lambda: greet(line=True))
    line.ride(step, steps)
    width = w_ref.shape[-1]
    shape = low_ref.shape

    def columns(index):
        return pl.ds(pl.multiple_of(flipped(lax.axis_index("ctx"), index) * width, width), width)

    for index, part in enumerate(parts):
        att[:, columns(index)] = part[...].reshape(-1, width)
    attended = att[...]
    for index in range(8):
        total[:, columns(index)] = dot(attended, w_ref[index % 2, :, index // 2].reshape(-1, width))
    residual = total[...] + x_ref[...].reshape(attended.shape).astype(f32)
    res_ref[...] = residual.reshape(shape)
    low_ref[...] = (residual * rms_scale(residual) * gain_ref[...]).astype(bf16).reshape(shape)
    pl.when(step == steps - 1)(line.finish)


def gathered_residuals(x, attended, gain, out_blocks, own, identity):
    _, s, q, r, d = x.shape
    width = attended.shape[-1]
    tile = pl.BlockSpec((1, s, 1, r, d), lambda p, t: (p, 0, t, 0, 0))

    def sent(index):
        odd, other = index % 2, index // 2
        return pl.BlockSpec(
            (1, 1, 1, s, 1, r, width),
            lambda p, t: (odd, (p + odd) % 2, other, 0, flipped(t, other), 0, 0),
        )

    def fixed(shape):
        return pl.BlockSpec(shape, lambda p, t: (0,) * len(shape), pipeline_mode=pl.Buffered(1))

    return pl.pallas_call(
        gathered_residual_kernel,
        grid=(2, q),
        in_specs=[tile, fixed((1, d)), fixed(out_blocks.shape)]
        + [sent(i) for i in range(8)]
        + [STAGED],
        out_specs=[tile, tile, ANYWHERE],
        out_shape=[
            jax.ShapeDtypeStruct(x.shape, bf16),
            jax.ShapeDtypeStruct(x.shape, f32),
            line_shape(own),
        ],
        scratch_shapes=[
            pltpu.VMEM((s * r, d), bf16),
            pltpu.VMEM((s * r, d), f32),
            *LineGather.SEMAPHORES,
        ],
        compiler_params=talking(identity),
        cost_estimate=pl.CostEstimate(
            flops=2 * x.size * d, bytes_accessed=10 * x.size, transcendentals=0
        ),
    )(x, gain.reshape(1, d), out_blocks, *[attended] * 8, own)


def hidden_kernel(skipped, low_ref, cot_ref, w_gate, w_up, w_down, *refs):
    hidden_ref, gate_ref, up_ref = refs[skipped:]
    low = low_ref[...]
    gate, upward = dot(low, w_gate[...]), dot(low, w_up[...])
    grad_hidden = dot(cot_ref[...], w_down[...])
    sigmoid = jax.nn.sigmoid(gate)
    hidden_ref[...] = (gate * sigmoid * upward).astype(bf16)
    gate_ref[...] = (grad_hidden * upward * sigmoid * (1.0 + gate * (1.0 - sigmoid))).astype(bf16)
    up_ref[...] = (grad_hidden * gate * sigmoid).astype(bf16)


def block_specs(weights):
    return [
        pl.BlockSpec((array.shape[0], width), lambda i, pick=pick: (0, pick), pipeline_mode=pl.Buffered(1))
        for array, width, pick in weights
    ]


def arrays(weights):
    return [array for array, _, _ in weights]


def hidden_part(second_low, cot, weights, earlier=()):
    tokens, d = second_low.shape
    step = weights[0][1]
    tile = min(512, tokens)
    return pl.pallas_call(
        functools.partial(hidden_kernel, len(earlier)),
        grid=(tokens // tile,),
        in_specs=[tile_spec(tile, d)] * 2 + block_specs(weights) + [ANYWHERE] * len(earlier),
        out_specs=[tile_spec(tile, step)] * 3,
        out_shape=[jax.ShapeDtypeStruct((tokens, step), bf16)] * 3,
        compiler_params=PARAMS,
        cost_estimate=pl.CostEstimate(
            flops=6 * tokens * d * step, bytes_accessed=4 * tokens * d, transcendentals=tokens * step
        ),
    )(second_low, cot, *arrays(weights), *earlier)


def back_kernel(count, *refs):
    lefts, weights = refs[:count], refs[count : 2 * count]
    total = None
    for left, weight in zip(lefts, weights):
        part = dot_rows(left[...], weight[...])
        total = part if total is None else total + part
    refs[2 * count][...] = total.astype(bf16)


def taken(weights):
    return [
        (array, width, pick)
        if width % 128 == 0
        else (lax.slice_in_dim(array, pick * width, (pick + 1) * width, axis=1), width, 0)
        for array, width, pick in weights
    ]


def back(lefts, weights, first, tokens):
    d = weights[0][0].shape[0]
    tile = min(256, tokens)
    start = first // tile
    weights = taken(weights)
    return pl.pallas_call(
        functools.partial(back_kernel, len(lefts)),
        grid=(tokens // tile,),
        in_specs=[pl.BlockSpec((tile, left.shape[1]), lambda i: (i + start, 0)) for left in lefts]
        + block_specs(weights),
        out_specs=tile_spec(tile, d),
        out_shape=jax.ShapeDtypeStruct((tokens, d), bf16),
        compiler_params=PARAMS,
        cost_estimate=pl.CostEstimate(
            flops=2 * tokens * d * sum(left.shape[1] for left in lefts),
            bytes_accessed=4 * tokens * d,
            transcendentals=0,
        ),
    )(*lefts, *arrays(weights))


FAR, BY_X, BY_Y, OWN = 3, 1, 2, 0
TURNS = ((1, FAR), (1, BY_X), (0, FAR), (1, BY_Y), (0, BY_X), (1, OWN), (0, BY_Y), (0, OWN))
PARITIES = sum(p << t for t, (p, _) in enumerate(TURNS))
PLACES = sum(q << (2 * t) for t, (_, q) in enumerate(TURNS))


def norm_back(grad, x, base, gain):
    scale = rms_scale(x)
    weighted = gain * grad
    mean = jnp.mean(weighted * x, axis=-1, keepdims=True)
    return base + scale * weighted - x * (scale * scale * scale) * mean, grad * x * scale


def back_scatter_kernel(count, skipped, *refs):
    lefts, weights, refs = refs[:count], refs[count : 2 * count], refs[2 * count + skipped :]
    x_ref, base_ref, gain_ref, grad_ref, low_ref, sum_ref = refs[:6]
    refs = refs[6:]
    given, got, sums, own, far, from_x, from_y, send_odd, came_odd, sent, came = refs
    sibling, by_x, by_y = neighbours()
    greet()
    s, r, d = own.shape
    half = s // 2

    def move(partner, source, target, send_sem, recv_sem):
        return pltpu.make_async_remote_copy(
            src_ref=source,
            dst_ref=target,
            send_sem=send_sem,
            recv_sem=recv_sem,
            device_id={"ctx": partner},
            device_id_type=MESH,
        )

    def odd_copy(q):
        return move(sibling, given.at[q], got.at[q], send_odd.at[q], came_odd.at[q])

    low_half, high_half = pl.ds(0, half), pl.ds(half, half)
    far_x = move(by_x, sums.at[FAR, low_half], far.at[low_half], sent.at[0], came.at[0])
    far_y = move(by_y, sums.at[FAR, high_half], far.at[high_half], sent.at[1], came.at[1])
    first_x = move(by_x, sums.at[BY_X, low_half], from_x.at[low_half], sent.at[2], came.at[2])
    first_y = move(by_y, sums.at[BY_Y, high_half], from_y.at[high_half], sent.at[3], came.at[3])
    last_x = move(by_x, sums.at[BY_X, high_half], from_x.at[high_half], sent.at[4], came.at[4])
    last_y = move(by_y, sums.at[BY_Y, low_half], from_y.at[low_half], sent.at[5], came.at[5])

    def turn(t, _):
        p = lax.shift_right_logical(jnp.int32(PARITIES), t) % 2
        q = lax.shift_right_logical(jnp.int32(PLACES), 2 * t) % 4
        total = None
        for left, weight in zip(lefts, weights):
            width = left.shape[-1]
            part = dot_rows(left[p, :, q].reshape(s * r, width), weight[...])
            total = part if total is None else total + part
        total = total.reshape(s, r, d)

        @pl.when(p == 1)
        def _():
            given[q] = total.astype(bf16)
            odd_copy(q).start()

        @pl.when(p == 0)
        def _():
            odd_copy(q).wait_recv()
            both = total + got[q].astype(f32)

            @pl.when(q == OWN)
            def _():
                own[...] = both

            @pl.when(q != OWN)
            def _():
                sums[q] = both.astype(bf16)

            @pl.when(q == FAR)
            def _():
                far_x.start()
                far_y.start()

            @pl.when(q == BY_X)
            def _():
                first_x.start()

            @pl.when(q == BY_Y)
            def _():
                first_y.start()

        return 0

    lax.fori_loop(0, len(TURNS), turn, 0)
    far_x.wait_recv()
    sums[BY_Y, low_half] = (sums[BY_Y, low_half].astype(f32) + far[low_half].astype(f32)).astype(bf16)
    last_y.start()
    far_y.wait_recv()
    sums[BY_X, high_half] = (sums[BY_X, high_half].astype(f32) + far[high_half].astype(f32)).astype(bf16)
    last_x.start()
    first_x.wait_recv()
    first_y.wait_recv()
    own[low_half] += from_x[low_half].astype(f32)
    own[high_half] += from_y[high_half].astype(f32)
    last_y.wait_recv()
    own[low_half] += from_y[low_half].astype(f32)
    last_x.wait_recv()
    own[high_half] += from_x[high_half].astype(f32)

    sum_ref[...] = jnp.zeros_like(sum_ref)
    slab = min(32, r)

    def finish(index, _):
        at = (index // (r // slab), pl.ds(pl.multiple_of((index % (r // slab)) * slab, slab), slab))
        grad, terms = norm_back(
            own[at], x_ref[at].astype(f32), base_ref[at].astype(f32), gain_ref[...]
        )
        grad_ref[at] = grad
        low_ref[at] = grad.astype(bf16)
        sum_ref[...] += jnp.sum(terms, axis=0, keepdims=True)
        return 0

    lax.fori_loop(0, s * (r // slab), finish, 0)
    for copy in (far_x, far_y, first_x, first_y, last_x, last_y):
        copy.wait_send()
    for q in range(4):
        odd_copy(q).wait_send()


def back_scatter(lefts, weights, shape, identity, x, base, gain, earlier=(), last=False):
    s, q, r, d = shape
    width = sum(left.shape[-1] for left in lefts)
    weights = taken(weights)
    lefts = [left.reshape(2, s, q, r, left.shape[-1]) for left in lefts]

    def fixed(whole):
        return pl.BlockSpec(whole, lambda i: (0,) * len(whole), pipeline_mode=pl.Buffered(1))

    operands = [*lefts, *arrays(weights), *earlier]
    in_specs = [fixed(left.shape) for left in lefts] + block_specs(weights)
    in_specs += [ANYWHERE] * len(earlier)
    operands += [x, base, gain.reshape(1, d)]
    in_specs += [fixed((s, r, d)), fixed((s, r, d)), fixed((1, d))]
    out_specs = [fixed((s, r, d)), fixed((s, r, d)), fixed((1, d))]
    out_shape = [
        jax.ShapeDtypeStruct((s, r, d), f32),
        jax.ShapeDtypeStruct((s, r, d), bf16),
        jax.ShapeDtypeStruct((1, d), f32),
    ]
    dma = pltpu.SemaphoreType.DMA
    return pl.pallas_call(
        functools.partial(back_scatter_kernel, len(lefts), len(earlier)),
        grid=(1,),
        in_specs=in_specs,
        out_specs=out_specs,
        out_shape=out_shape,
        scratch_shapes=[
            pltpu.VMEM((4, s, r, d), bf16),
            pltpu.VMEM((4, s, r, d), bf16),
            pltpu.VMEM((4, s, r, d), bf16),
            pltpu.VMEM((s, r, d), f32),
            pltpu.VMEM((s, r, d), bf16),
            pltpu.VMEM((s, r, d), bf16),
            pltpu.VMEM((s, r, d), bf16),
            dma((4,)),
            dma((4,)),
            dma((6,)),
            dma((6,)),
        ],
        compiler_params=talking(identity),
        cost_estimate=pl.CostEstimate(
            flops=1 if last else 16 * s * r * d * width,
            bytes_accessed=1 if last else 16 * s * r * d,
            transcendentals=0,
            remote_bytes_transferred=1 if last else 14 * s * r * d,
        ),
    )(*operands)


def token_sums_kernel(counts, *refs):
    out_ref = refs[-1]
    start = 0
    for count in counts:
        left, rights, refs = refs[0], refs[1 : 1 + count], refs[1 + count :]
        for right in rights:
            width = right.shape[1]
            part = dot_tokens(left[...], right[...]).astype(bf16)
            groups, owners, rows, _ = out_ref.shape
            part = part.reshape(owners, groups, rows, width)
            for owner in range(owners):
                out_ref[:, owner, :, start : start + width] = part[owner]
            start += width


def token_sums(pairs, n, rows):
    groups = pairs[0][0].shape[1] // (n * rows)
    operands, in_specs, width = [], [], 0
    for left, rights in pairs:
        operands += [left, *rights]
        in_specs.append(pl.BlockSpec((left.shape[0], 2 * groups * rows), lambda i: (0, i)))
        in_specs += [whole_spec(right.shape) for right in rights]
        width += sum(right.shape[1] for right in rights)
    tokens, d = pairs[0][0].shape
    return pl.pallas_call(
        functools.partial(token_sums_kernel, [len(rights) for _, rights in pairs]),
        grid=(n // 2,),
        in_specs=in_specs,
        out_specs=pl.BlockSpec((groups, 2, rows, width), lambda i: (0, i, 0, 0)),
        out_shape=jax.ShapeDtypeStruct((groups, n, rows, width), bf16),
        compiler_params=PARAMS,
        cost_estimate=pl.CostEstimate(
            flops=2 * tokens * d * width, bytes_accessed=4 * tokens * d, transcendentals=0
        ),
    )(*operands)


def output_back_kernel(low_ref, att_ref, w_ref, *refs):
    grad_ref, sum_ref, total = refs[-3:]

    @pl.when(pl.program_id(0) == 0)
    def _():
        total[...] = jnp.zeros_like(total)

    low = low_ref[...]
    grad_ref[...] = dot_rows(low, w_ref[...]).astype(bf16)
    total[...] += dot_tokens(att_ref[...], low)

    @pl.when(pl.program_id(0) == pl.num_programs(0) - 1)
    def _():
        sum_ref[...] = total[...].astype(bf16)


def output_back(grad_low, attended_low, out_rows, earlier=()):
    tokens, d = grad_low.shape
    lanes = attended_low.shape[1]
    tile = min(512, tokens)
    return pl.pallas_call(
        output_back_kernel,
        grid=(tokens // tile,),
        in_specs=[tile_spec(tile, d), tile_spec(tile, lanes), whole_spec((lanes, d))]
        + [ANYWHERE] * len(earlier),
        out_specs=[tile_spec(tile, lanes), pl.BlockSpec((lanes, d), lambda i: (0, 0))],
        out_shape=[
            jax.ShapeDtypeStruct((tokens, lanes), bf16),
            jax.ShapeDtypeStruct((lanes, d), bf16),
        ],
        scratch_shapes=[pltpu.VMEM((lanes, d), f32)],
        compiler_params=PARAMS,
        cost_estimate=pl.CostEstimate(
            flops=4 * tokens * d * lanes, bytes_accessed=2 * tokens * d, transcendentals=0
        ),
    )(grad_low, attended_low, out_rows, *earlier)


def gather_and_sum_kernel(hiddens, skipped, low_ref, gate_ref, up_ref, cot_ref, *refs):
    lefts, weights = refs[:hiddens], refs[hiddens : 2 * hiddens]
    refs = refs[2 * hiddens :]
    own_ref, refs = refs[0], refs[1 + skipped :]
    sum_ref, out_ref, all_ref = refs[:3]
    gather = Gather(own_ref, all_ref, *refs[3:])
    step, steps = pl.program_id(0), 8
    pl.when(step == 0)(greet)
    gather.ride(step, steps)
    tile = lefts[0].shape[0] // steps
    token_sums_kernel([2, 1], low_ref, gate_ref, up_ref, cot_ref, lefts[-1], sum_ref)
    rows = pl.ds(pl.multiple_of(step * tile, tile), tile)
    total = None
    for left, weight in zip(lefts, weights):
        part = dot_rows(left[rows, :], weight[...])
        total = part if total is None else total + part
    out_ref[...] = total.astype(bf16)
    pl.when(step == steps - 1)(gather.finish)


def gather_and_sum(own, second_low, grads, cot, hiddens, weights, rows, identity, earlier=()):
    tokens, d = second_low.shape
    step = hiddens[0].shape[1]
    groups = d // (8 * rows)
    column = pl.BlockSpec((tokens, groups * rows), lambda i: (0, i))
    return pl.pallas_call(
        functools.partial(gather_and_sum_kernel, len(hiddens), len(earlier)),
        grid=(8,),
        in_specs=[column, whole_spec(grads[0].shape), whole_spec(grads[1].shape), column]
        + [whole_spec(hidden.shape) for hidden in hiddens]
        + block_specs(weights)
        + [STAGED]
        + [ANYWHERE] * len(earlier),
        out_specs=[
            pl.BlockSpec((groups, 1, rows, 3 * step), lambda i: (0, i, 0, 0)),
            tile_spec(tokens // 8, d),
            ANYWHERE,
        ],
        out_shape=[
            jax.ShapeDtypeStruct((groups, 8, rows, 3 * step), bf16),
            jax.ShapeDtypeStruct((tokens, d), bf16),
            gathered_shape(own),
        ],
        scratch_shapes=list(Gather.SEMAPHORES),
        compiler_params=talking(identity),
        cost_estimate=pl.CostEstimate(
            flops=14 * tokens * d * step, bytes_accessed=12 * tokens * d, transcendentals=0
        ),
    )(second_low, *grads, cot, *hiddens, *arrays(weights), own, *earlier)


def spread_kernel(count, *refs):
    parts, out_ref, last_ref = refs[:count], refs[count], refs[count + 1]
    senders, _, width = parts[0].shape

    def write(target):
        for sender in range(senders):
            for index, part in enumerate(parts):
                start = (sender * count + index) * width
                target[:, start : start + width] = part[sender].astype(f32)

    pl.when(pl.program_id(0) < 2)(lambda: write(out_ref))
    pl.when(pl.program_id(0) == 2)(lambda: write(last_ref))


def spread(whole, places, width):
    n, rows, _ = whole.shape
    count = len(places)
    pair = min(n, 2)
    wide = pair * count * width
    turns = n // pair
    return pl.pallas_call(
        functools.partial(spread_kernel, count),
        grid=(3, turns),
        in_specs=[
            pl.BlockSpec((pair, rows, width), lambda third, i, place=place: (i, 0, 3 * place + third))
            for place in places
        ],
        out_specs=[
            pl.BlockSpec((rows, wide), lambda third, i: (0, jnp.minimum(third * turns + i, 2 * turns - 1))),
            pl.BlockSpec((rows, wide), lambda third, i: (0, jnp.maximum(third - 1, 0) * i)),
        ],
        out_shape=[
            jax.ShapeDtypeStruct((rows, 2 * n * count * width), f32),
            jax.ShapeDtypeStruct((rows, n * count * width), f32),
        ],
        compiler_params=PARAMS,
        cost_estimate=pl.CostEstimate(
            flops=0, bytes_accessed=18 * n * rows * count * width, transcendentals=0
        ),
    )(*[whole] * count)


def spread_all_kernel(part_ref, _, out_ref):
    senders, _, width = part_ref.shape
    for sender in range(senders):
        out_ref[:, sender * width : (sender + 1) * width] = part_ref[sender].astype(f32)


def spread_all(part, width, earlier):
    n, rows, _ = part.shape
    return pl.pallas_call(
        spread_all_kernel,
        grid=(3,),
        in_specs=[pl.BlockSpec((n, rows, width), lambda i: (0, 0, i)), ANYWHERE],
        out_specs=pl.BlockSpec((rows, n * width), lambda i: (0, i)),
        out_shape=jax.ShapeDtypeStruct((rows, 3 * n * width), f32),
        compiler_params=PARAMS,
        cost_estimate=pl.CostEstimate(
            flops=0, bytes_accessed=18 * n * rows * width, transcendentals=0
        ),
    )(part, earlier)


def only(values, head, heads):
    if heads == 1:
        return values
    lane = lax.broadcasted_iota(jnp.int32, values.shape, 1)
    inside = (lane >= head * HEAD_SIZE) & (lane < (head + 1) * HEAD_SIZE)
    return jnp.where(inside, values, jnp.zeros_like(values))


def forward_kernel(heads, q_spot, k_spot, q_ref, k_ref, v_ref, *refs):
    if len(refs) > 2:
        own_ref, line_ref, low_ref, total_ref, all_ref, line_all_ref = refs[:6]
        gather = Gather(own_ref, all_ref, *refs[6:9])
        line = LineGather(line_ref, line_all_ref, *refs[9:])
        steps = pl.num_programs(0) * pl.num_programs(1) * pl.num_programs(2)
        step = (pl.program_id(0) * pl.num_programs(1) + pl.program_id(1)) * pl.num_programs(2)
        step += pl.program_id(2)
        pl.when(step == 0)(lambda: greet(line=True))
        gather.ride(step, steps)
        line.ride(step, steps)
    else:
        low_ref, total_ref = refs
    lanes = q_ref.shape[-1]
    queries = q_ref[0, 0] * bf16(HEAD_SIZE**-0.5)
    keys = k_ref[:, 0].reshape(-1, lanes)
    values = v_ref[:, 0].reshape(-1, lanes)
    allowed = k_spot[0] <= q_spot[0, 0]
    attended = jnp.zeros(queries.shape, f32)
    for head in range(heads):
        scores = dot_rows(keys, only(queries, head, heads))
        scores = jnp.where(allowed, scores, -1e30)
        highest = jnp.max(scores, axis=0, keepdims=True)
        raised = jnp.exp(scores - highest)
        summed = jnp.sum(raised, axis=0, keepdims=True)
        probs = (raised * (1.0 / summed)).astype(bf16)
        total_ref[0, 0, head : head + 1, :] = highest + jnp.log(summed)
        attended += dot_tokens(probs, only(values, head, heads))
    low_ref[0, 0] = attended.astype(bf16)
    if len(refs) > 2:
        pl.when(step == steps - 1)(line.finish)
        pl.when(step == steps - 1)(gather.finish)


def backward_kernel(
    heads, q_spot, k_spot, q_ref, k_ref, v_ref, grad_ref, total_ref, qc_ref, qs_ref, kc_ref, ks_ref, *refs
):
    dq_ref, dk_ref, dv_ref, dk_sum, dv_sum = refs[-5:]
    lanes = q_ref.shape[-1]
    scale = HEAD_SIZE**-0.5
    step = pl.program_id(1) * pl.num_programs(2) + pl.program_id(2)

    @pl.when(step == 0)
    def _():
        dk_sum[...] = jnp.zeros_like(dk_sum)
        dv_sum[...] = jnp.zeros_like(dv_sum)

    queries = q_ref[0, 0] * bf16(scale)
    grads = grad_ref[0, 0]
    keys = k_ref[:, 0].reshape(-1, lanes)
    values = v_ref[:, 0].reshape(-1, lanes)
    allowed = k_spot[0] <= q_spot[0, 0]
    grad_q = jnp.zeros(queries.shape, f32)
    for head in range(heads):
        query = only(queries, head, heads)
        grad = only(grads, head, heads)
        scores = jnp.where(allowed, dot_rows(keys, query), -1e30)
        probs = jnp.exp(scores - total_ref[0, 0, head : head + 1, :])
        dv_sum[...] += dot(probs.astype(bf16), grad)
        weighted = probs * dot_rows(values, grad)
        delta = jnp.sum(weighted, axis=0, keepdims=True)
        grad_scores = (weighted - probs * delta).astype(bf16)
        dk_sum[...] += dot(grad_scores, query)
        grad_q += dot_tokens(grad_scores, only(keys, head, heads))
    dq_ref[0, 0] = rotate_back(grad_q * scale, qc_ref[0, 0], qs_ref[0, 0]).astype(bf16)

    @pl.when(step == pl.num_programs(1) * pl.num_programs(2) - 1)
    def _():
        shape = (dk_ref.shape[0],) + dk_ref.shape[2:]
        cosine = kc_ref[:, 0].reshape(-1, lanes)
        sine = ks_ref[:, 0].reshape(-1, lanes)
        dk_ref[:, 0] = rotate_back(dk_sum[...], cosine, sine).astype(bf16).reshape(shape)
        dv_ref[:, 0] = dv_sum[...].astype(bf16).reshape(shape)


def attention_specs(shape, heads):
    p, s, rows, lanes = shape
    tile = min(256, rows)
    one = pl.BlockSpec((1, 1, tile, lanes), lambda i, j, t: (j, i, t, 0))
    side = pl.BlockSpec((p, 1, rows, lanes), lambda i, j, t: (0, i, 0, 0))
    stat = pl.BlockSpec((1, 1, heads, tile), lambda i, j, t: (j, i, 0, t))
    q_spot = pl.BlockSpec((1, 1, 1, tile), lambda i, j, t: (j, i, 0, t))
    k_spot = pl.BlockSpec((1, p * rows, 1), lambda i, j, t: (i, 0, 0))
    return (s, p, rows // tile), one, side, stat, q_spot, k_spot


def attend(q_spot, k_spot, queries, keys, values, own=None, line=None, identity=None):
    p, s, rows, lanes = queries.shape
    heads = lanes // HEAD_SIZE
    grid, one, side, stat, q_spec, k_spec = attention_specs(queries.shape, heads)
    pairs = p * rows * s * p * rows
    out_shape = [
        jax.ShapeDtypeStruct(queries.shape, bf16),
        jax.ShapeDtypeStruct((p, s, heads, rows), f32),
    ]
    riding = own is not None
    return pl.pallas_call(
        functools.partial(forward_kernel, heads),
        grid=grid,
        in_specs=[q_spec, k_spec, one, side, side] + [STAGED] * (2 * riding),
        out_specs=[one, stat] + [ANYWHERE] * (2 * riding),
        out_shape=out_shape + ([gathered_shape(own), line_shape(line)] if riding else []),
        scratch_shapes=[*Gather.SEMAPHORES, *LineGather.SEMAPHORES] if riding else [],
        compiler_params=talking(identity) if riding else PARAMS,
        cost_estimate=pl.CostEstimate(
            flops=pairs * heads * 2048, bytes_accessed=queries.size * 14, transcendentals=pairs * heads
        ),
    )(q_spot, k_spot, queries, keys, values, *([own, line] if riding else []))


def attend_back(q_spot, k_spot, queries, keys, values, grads, totals, cosine, sine, earlier=()):
    p, s, rows, lanes = queries.shape
    heads = lanes // HEAD_SIZE
    grid, one, side, stat, q_spec, k_spec = attention_specs(queries.shape, heads)
    pairs = p * rows * s * p * rows
    return pl.pallas_call(
        functools.partial(backward_kernel, heads),
        grid=grid,
        in_specs=[q_spec, k_spec, one, side, side, one, stat, one, one, side, side]
        + [ANYWHERE] * len(earlier),
        out_specs=[one, side, side],
        out_shape=[jax.ShapeDtypeStruct(queries.shape, bf16)] * 3,
        scratch_shapes=[pltpu.VMEM((p * rows, lanes), f32)] * 2,
        compiler_params=PARAMS,
        cost_estimate=pl.CostEstimate(
            flops=pairs * heads * 5120, bytes_accessed=queries.size * 20, transcendentals=pairs * heads
        ),
    )(q_spot, k_spot, queries, keys, values, grads, totals, cosine, sine, cosine, sine, *earlier)


def on_device(
    plane,
    inputs,
    positions,
    first_gain,
    attention_weight,
    output_weight,
    second_gain,
    gate_up_weight,
    down_weight,
    cotangent,
):
    s, r, d = inputs.shape
    n = plane.size
    ff = down_weight.shape[1]
    me = lax.axis_index("ctx")
    lanes = d // n
    mine = ff // n
    step = mine // CHUNKS
    tokens = s * r * n
    rows = d // (n * lax.axis_size("fsdp"))
    half = tokens // 2
    group = (2, s, n // 2 * r)
    blocks = (s, n // 2, r, d)

    def columns(weight, start, width):
        return lax.dynamic_slice_in_dim(weight, start, width, 1)

    qkv = jnp.concatenate(
        [columns(attention_weight, part * d + me * lanes, lanes) for part in range(3)], axis=1
    )
    out_own = columns(output_weight, me * lanes, lanes)
    if plane.relative:
        whole_inputs, cot, qkv, out_own = gather_in_plane([inputs, cotangent], [qkv, out_own], 1)
    else:
        whole_inputs, cot = plane.gather([inputs, cotangent])
        qkv, out_own = gather_rows(qkv), gather_rows(out_own)

    def chunk_parts(chunk, earlier):
        start = (me + zero_of(earlier)) * mine + chunk * step
        return [
            columns(gate_up_weight, start, step),
            columns(gate_up_weight, ff + start, step),
            columns(down_weight, start, step),
        ]

    ffn = {}
    for chunk in range(CHUNKS):
        if chunk != RIDING or not plane.relative:
            whole = gather_rows(jnp.concatenate(chunk_parts(chunk, qkv), axis=1))
            ffn[chunk] = [(whole, step, part) for part in range(3)]

    places = plane.order(positions.reshape(s, n, r)).reshape(group)
    q_spot = places[:, :, None, :]
    k_spot = places.transpose(1, 0, 2).reshape(s, n * r, 1)
    cosine, sine = rope_tables(places.reshape(tokens), lanes, whole_inputs)
    normed_low, queries, keys, values = project(
        whole_inputs.reshape(tokens, d), first_gain, cosine, sine, qkv
    )
    queries, keys, values, cosine, sine = (
        part.reshape(*group, lanes) for part in (queries, keys, values, cosine, sine)
    )
    if plane.relative:
        riders = chunk_parts(RIDING, qkv)
        attended_low, totals, out_blocks, gate = attend(
            q_spot, k_spot, queries, keys, values, out_own.reshape(2, d // 2, lanes), riders[0], 2
        )
        attended_whole, upward = gather_in_plane(
            [attended_low.reshape(2, half, lanes)], riders[1:2], 3
        )
        second_low, residual, down = gathered_residuals(
            whole_inputs,
            attended_whole.reshape(2, 2, 4, s, 4, r, lanes),
            second_gain,
            out_blocks,
            riders[2],
            4,
        )
        ffn[RIDING] = [(whole, step, 0) for whole in (gate, upward, down)]
        second_low = second_low.reshape(tokens, d)
        residual = residual[0, :, 0]
    else:
        attended_low, totals = attend(q_spot, k_spot, queries, keys, values)
        out_blocks = lax.all_gather(out_own, "ctx", axis=0, tiled=False)
        attended_whole = lax.all_gather(
            attended_low.reshape(tokens, lanes), "ctx", axis=1, tiled=True
        )
        second_low, residual = residuals(
            whole_inputs.reshape(tokens, d), attended_whole, second_gain, out_blocks
        )
        residual = lax.dynamic_index_in_dim(residual.reshape(2, *blocks), me % 2, 0, keepdims=False)
        residual = lax.dynamic_index_in_dim(residual, me // 2, 1, keepdims=False)
    cot = cot.reshape(tokens, d)
    attended_low = attended_low.reshape(tokens, lanes)

    if plane.relative:
        out_rows = lax.dynamic_slice(
            out_blocks, (0, me // 4, 0, (me % 4) * lanes, 0), (2, 1, 4, lanes, lanes)
        ).reshape(2, 2, 2, lanes, lanes)
        for axis, bit in ((0, 1), (1, 4), (2, 2)):
            out_rows = jnp.where((me & bit) != 0, jnp.flip(out_rows, axis), out_rows)
        out_rows = out_rows.transpose(3, 1, 2, 0, 4).reshape(lanes, d)
    else:
        out_rows = lax.dynamic_slice_in_dim(out_blocks, me * lanes, lanes, 1)
        out_rows = out_rows.transpose(1, 0, 2).reshape(lanes, d)

    def summed(pairs):
        if plane.relative:
            return token_sums(pairs, n, rows)
        partial = [dot_tokens(left, right) for left, rights in pairs for right in rights]
        return by_owners(jnp.concatenate(partial, axis=1), n, rows)

    hiddens, grads, partials, sums = [], [], [], []
    for chunk in ORDER:
        hidden, *grad_gate_up = hidden_part(
            second_low, cot, taken(ffn[chunk]), partials[-1:] or [out_rows]
        )
        hiddens.append(hidden)
        grads.append(grad_gate_up)
        if len(hiddens) < CHUNKS or not plane.relative:
            partials.append(summed([(second_low, grad_gate_up), (cot, [hidden])]))
            sums.append(sum_rows(partials[-1]))

    def apart(lefts, weights):
        odd, even = back(lefts, weights, half, half), back(lefts, weights, 0, half)
        return plane.scatter(odd.reshape(blocks), even.reshape(blocks))

    def norm_step(identity, lefts, weights, x, base, gain, earlier, last=False):
        if plane.relative:
            return back_scatter(lefts, weights, blocks, identity, x, base, gain, earlier, last)
        grad, terms = norm_back(apart(lefts, weights), x.astype(f32), base.astype(f32), gain)
        return grad, grad.astype(bf16), jnp.sum(terms, axis=(0, 1))

    grad_residual, grad_residual_low, second_gain_part = norm_step(
        5,
        [grad for pair in grads for grad in pair],
        [weight for chunk in ORDER for weight in ffn[chunk][:2]],
        residual,
        cotangent,
        second_gain,
        partials[-1:],
    )
    downs = [ffn[chunk][2] for chunk in ORDER]
    if plane.relative:
        last, output_parts, grad_low = gather_and_sum(
            grad_residual_low, second_low, grads[-1], cot, hiddens, downs, rows, 6, sums[:1]
        )
        sums.append(sum_rows(last))
    else:
        (grad_low,) = plane.gather([grad_residual_low])
    grad_low = grad_low.reshape(tokens, d)

    grad_attended, out_part = output_back(grad_low, attended_low, out_rows, sums[1:2])
    grad_projected = attend_back(
        q_spot, k_spot, queries, keys, values, grad_attended.reshape(*group, lanes), totals, cosine, sine
    )
    grad_projected = [part.reshape(tokens, lanes) for part in grad_projected]
    attention_parts = summed([(normed_low, grad_projected)])
    attention_sums = sum_rows(attention_parts)
    grad_output_weight = lax.psum_scatter(
        after(out_part, attention_parts), "fsdp", scatter_dimension=0, tiled=True
    )
    grad_input, _, first_gain_part = norm_step(
        7,
        grad_projected,
        [(qkv, lanes, part) for part in range(3)],
        inputs,
        grad_residual,
        first_gain,
        [attention_parts],
        True,
    )
    gains = jnp.stack([first_gain_part.reshape(d), second_gain_part.reshape(d)])
    gains = gains.reshape(2, d // rows, rows).transpose(1, 0, 2)
    gains = jnp.sum(
        lax.all_to_all(gains, ("ctx", "fsdp"), split_axis=0, concat_axis=0, tiled=True), axis=0
    )
    sums = to_owners(after(jnp.concatenate(sums, axis=2), grad_input))
    attention_sums = to_owners(attention_sums)
    places = [ORDER.index(chunk) for chunk in range(CHUNKS)]
    if plane.relative:
        grad_gate_up, grad_down = spread(sums, places, step)
        grad_attention = spread_all(attention_sums, lanes, grad_down)
    else:
        whole = sums.reshape(n, rows, CHUNKS, 3, step)[:, :, jnp.array(places)].transpose(0, 1, 3, 2, 4)
        whole = whole.transpose(1, 2, 0, 3, 4).reshape(rows, 3, ff).astype(f32)
        grad_gate_up, grad_down = whole[:, :2].reshape(rows, 2 * ff), whole[:, 2]
        grad_attention = attention_sums.reshape(n, rows, 3, lanes).transpose(1, 2, 0, 3)
        grad_attention = grad_attention.reshape(rows, 3 * d).astype(f32)
    if plane.relative:
        output_parts = output_parts.reshape(2, *blocks)
        odd = lax.dynamic_index_in_dim(output_parts, 1 + zero_of(grad_input), 0, keepdims=False)
        output = after(residual, grad_down) + plane.scatter(odd, output_parts[0])
    else:
        output = residual + apart(hiddens, downs)[0]
    return (
        output,
        grad_input,
        grad_attention,
        after(grad_output_weight, grad_attention).astype(f32),
        grad_gate_up,
        grad_down,
        gains[0],
        gains[1],
    )


def solution(mesh):
    plane = Plane(mesh.shape["ctx"])
    return jax.shard_map(
        functools.partial(on_device, plane),
        mesh=mesh,
        in_specs=(
            P("fsdp", "ctx", None),
            P("fsdp", None),
            P(),
            P("fsdp", None),
            P("fsdp", None),
            P(),
            P("fsdp", None),
            P("fsdp", None),
            P("fsdp", "ctx", None),
        ),
        out_specs=(
            P("fsdp", "ctx", None),
            P("fsdp", "ctx", None),
            P(("ctx", "fsdp"), None),
            P(("ctx", "fsdp"), None),
            P(("ctx", "fsdp"), None),
            P(("ctx", "fsdp"), None),
            P(("ctx", "fsdp")),
            P(("ctx", "fsdp")),
        ),
        check_vma=False,
    )
```

```python
import functools

import jax
import jax.numpy as jnp
from jax import lax
from jax.experimental import pallas as pl
from jax.experimental.pallas import tpu as pltpu
from jax.sharding import PartitionSpec as P

HEAD_SIZE = 64
EPSILON = 1e-05
ROPE_BASE = 130000.0
CHUNKS = 4
ORDER = (0, 3, 1, 2)
RIDING = 3

f32 = jnp.float32
bf16 = jnp.bfloat16


def rms_scale(values):
    return lax.rsqrt(jnp.mean(values * values, axis=-1, keepdims=True) + EPSILON)


def dot(left, right):
    return jnp.dot(left, right, preferred_element_type=f32)


def dot_rows(left, right):
    return lax.dot_general(left, right, (((1,), (1,)), ((), ())), preferred_element_type=f32)


def dot_tokens(left, right):
    return lax.dot_general(left, right, (((0,), (0,)), ((), ())), preferred_element_type=f32)


def tables_kernel(places_ref, _, cos_ref, sin_ref):
    half = HEAD_SIZE // 2
    width = cos_ref.shape[1]
    narrow = min(width, 128)
    lane = lax.broadcasted_iota(jnp.int32, (1, narrow), 1) % half
    inverse = jnp.exp(-(2.0 * lane.astype(f32) / HEAD_SIZE) * jnp.log(f32(ROPE_BASE)))
    angles = places_ref[...].astype(f32) * inverse
    cosine, sine = jnp.cos(angles), jnp.sin(angles)
    for start in range(0, width, narrow):
        cos_ref[:, start : start + narrow] = cosine
        sin_ref[:, start : start + narrow] = sine


def rope_tables(places, lanes, earlier):
    tokens = places.shape[0]
    tile = min(512, tokens)
    return pl.pallas_call(
        tables_kernel,
        grid=(tokens // tile,),
        in_specs=[pl.BlockSpec((tile, 1), lambda i: (i, 0)), ANYWHERE],
        out_specs=[pl.BlockSpec((tile, lanes), lambda i: (i, 0))] * 2,
        out_shape=[jax.ShapeDtypeStruct((tokens, lanes), f32)] * 2,
        cost_estimate=pl.CostEstimate(
            flops=100 * tokens * lanes, bytes_accessed=8 * tokens * lanes, transcendentals=0
        ),
    )(places.reshape(tokens, 1), earlier)


def other_half(values):
    half = HEAD_SIZE // 2
    lanes = values.shape[-1]
    if lanes == HEAD_SIZE:
        return jnp.concatenate([-values[:, half:], values[:, :half]], axis=1)
    lane = lax.broadcasted_iota(jnp.int32, values.shape, 1)
    return jnp.where(
        lane % HEAD_SIZE < half,
        -pltpu.roll(values, lanes - half, 1),
        pltpu.roll(values, half, 1),
    )


def rotate(values, cosine, sine):
    return values * cosine + other_half(values) * sine


def rotate_back(gradient, cosine, sine):
    return gradient * cosine - other_half(gradient * sine)


MESH = pl.DeviceIdType.MESH


def greet(line=False):
    barrier = pltpu.get_barrier_semaphore()
    partners = [{"ctx": partner} for partner in neighbours()]
    size = lax.axis_size("fsdp")
    if line:
        z = lax.axis_index("fsdp")
        partners += [{"fsdp": (z + shift) % size} for shift in range(1, size)]
    for partner in partners:
        pl.semaphore_signal(barrier, inc=1, device_id=partner, device_id_type=MESH)
    pl.semaphore_wait(barrier, len(partners))


def flipped(place, bits):
    for bit in (1, 2, 4):
        if bits & bit:
            place = place + bit - 2 * bit * ((place // bit) % 2)
    return place


def neighbours():
    me = lax.axis_index("ctx")
    return [flipped(me, bit) for bit in (1, 2, 4)]


class Gather:
    SEMAPHORES = (
        pltpu.SemaphoreType.DMA((2,)),
        pltpu.SemaphoreType.DMA((14,)),
        pltpu.SemaphoreType.DMA((14,)),
    )

    def __init__(self, own, out, local, sent, came):
        sibling, by_x, by_y = neighbours()
        routes = [
            (by_x, own.at[0], out.at[0, 0, 1]),
            (by_y, own.at[1], out.at[0, 1, 2]),
            (by_x, own.at[1], out.at[0, 1, 1]),
            (by_y, own.at[0], out.at[0, 0, 2]),
            (by_y, out.at[0, 0, 1], out.at[0, 0, 3]),
            (by_x, out.at[0, 1, 2], out.at[0, 1, 3]),
        ]
        for h in range(2):
            routes.append((sibling, own.at[h], out.at[1, h, 0]))
        for h, q in ((0, 1), (1, 2), (1, 1), (0, 2), (0, 3), (1, 3)):
            routes.append((sibling, out.at[0, h, q], out.at[1, h, q]))
        self.copies = [
            pltpu.make_async_remote_copy(
                src_ref=source,
                dst_ref=target,
                send_sem=sent.at[index],
                recv_sem=came.at[index],
                device_id={"ctx": partner},
                device_id_type=MESH,
            )
            for index, (partner, source, target) in enumerate(routes)
        ]
        self.kept = [
            pltpu.make_async_copy(own.at[h], out.at[0, h, 0], local.at[h]) for h in range(2)
        ]

    def send(self):
        for index in (0, 1, 2, 3, 6, 7):
            self.copies[index].start()
        for copy in self.kept:
            copy.start()

    def pass_on(self):
        self.copies[0].wait_recv()
        self.copies[4].start()
        self.copies[8].start()
        self.copies[1].wait_recv()
        self.copies[5].start()
        self.copies[9].start()

    def pass_seconds(self):
        self.copies[2].wait_recv()
        self.copies[10].start()
        self.copies[3].wait_recv()
        self.copies[11].start()

    def finish(self):
        self.copies[4].wait_recv()
        self.copies[12].start()
        self.copies[5].wait_recv()
        self.copies[13].start()
        for copy in self.copies[6:]:
            copy.wait_recv()
        for copy in self.copies:
            copy.wait_send()
        for copy in self.kept:
            copy.wait()

    def ride(self, step, steps):
        for turn, phase in ((0, self.send), (steps // 2, self.pass_on), (steps - 1, self.pass_seconds)):
            pl.when(step == turn)(phase)


class LineGather:
    SEMAPHORES = (
        pltpu.SemaphoreType.DMA((1,)),
        pltpu.SemaphoreType.DMA((3,)),
        pltpu.SemaphoreType.DMA((3,)),
    )

    def __init__(self, own, out, local, sent, came):
        z = lax.axis_index("fsdp")
        size = own.shape[0]

        def rows(place):
            return out.at[pl.ds(pl.multiple_of(place * size, size), size)]

        held = z // 2 + 2 * (z % 2)
        routes = [
            ((z + 1) % 4, own, rows(z)),
            ((z + 3) % 4, own, rows(z)),
            (2 * (1 - z % 2) + z // 2, rows(held), rows(held)),
        ]
        if lax.axis_size("fsdp") == 1:
            routes = []
        copies = [
            pltpu.make_async_remote_copy(
                src_ref=source,
                dst_ref=target,
                send_sem=sent.at[index],
                recv_sem=came.at[index],
                device_id={"fsdp": partner},
                device_id_type=MESH,
            )
            for index, (partner, source, target) in enumerate(routes)
        ]
        self.first, self.second = copies[:2], copies[2:]
        self.kept = pltpu.make_async_copy(own, rows(z), local.at[0])

    def send(self):
        for copy in (*self.first, self.kept):
            copy.start()

    def pass_on(self):
        for copy in self.first:
            copy.wait_recv()
        self.kept.wait()
        for copy in self.second:
            copy.start()

    def finish(self):
        for copy in self.second:
            copy.wait_recv()
        for copy in (*self.first, *self.second):
            copy.wait_send()

    def ride(self, step, steps):
        pl.when(step == 0)(self.send)
        pl.when(step == steps - 1)(self.pass_on)


def line_shape(own):
    return jax.ShapeDtypeStruct((lax.axis_size("fsdp") * own.shape[0], own.shape[1]), own.dtype)


class LineSum:
    @staticmethod
    def scratch(shape, width):
        _, n, rows, _ = shape
        return [
            pltpu.VMEM((6, n, rows, width), bf16),
            pltpu.SemaphoreType.DMA((3,)),
            pltpu.SemaphoreType.DMA((3,)),
            pltpu.SemaphoreType.DMA((3,)),
        ]

    def __init__(self, laid, first, out, held, local, sent, came):
        self.z = z = lax.axis_index("fsdp")
        self.size = lax.axis_size("fsdp")
        width = held.shape[-1]
        self.held, self.out = held, out

        def block(shift):
            return laid.at[(z + shift) % self.size, :, :, pl.ds(first, width)]

        def move(index, source, target, partner):
            return pltpu.make_async_remote_copy(
                src_ref=source,
                dst_ref=target,
                send_sem=sent.at[index],
                recv_sem=came.at[index],
                device_id={"fsdp": partner},
                device_id_type=MESH,
            )

        self.loads = [
            pltpu.make_async_copy(block(shift), held.at[index], local.at[index])
            for index, shift in enumerate((0, 1, 3))
        ]
        if self.size == 1:
            return
        self.far = move(0, block(2), held.at[3], 2 * (z % 2) + 1 - z // 2)
        self.up = move(1, held.at[1], held.at[4], (z + 1) % 4)
        self.down = move(2, held.at[2], held.at[5], (z + 3) % 4)

    def send(self):
        for load in self.loads:
            load.start()
        if self.size > 1:
            self.far.start()

    def pass_on(self):
        for load in self.loads:
            load.wait()
        if self.size > 1:
            self.far.wait_recv()
            for index, place, copy in ((1, 1, self.up), (2, 2, self.down)):

                @pl.when(self.z == place)
                def _():
                    added = self.held[index].astype(f32) + self.held[3].astype(f32)
                    self.held[index] = added.astype(bf16)

                copy.start()

    def finish(self):
        total = self.held[0].astype(f32)
        if self.size > 1:
            self.up.wait_recv()
            self.down.wait_recv()
            ends = jnp.where((self.z == 0) | (self.z == 3), 1.0, 0.0)
            total += self.held[4].astype(f32) + self.held[5].astype(f32)
            total += ends * self.held[3].astype(f32)
            for copy in (self.far, self.up, self.down):
                copy.wait_send()
        self.out[...] = total.astype(bf16)


def gathered_shape(own):
    return jax.ShapeDtypeStruct((2, 2, 4) + own.shape[1:], own.dtype)


ANYWHERE = pl.BlockSpec(memory_space=pl.ANY)
STAGED = pl.BlockSpec(memory_space=pltpu.VMEM)


def talking(identity):
    return pltpu.CompilerParams(
        collective_id=identity, has_side_effects=True, vmem_limit_bytes=56 * 1024 * 1024
    )


def gather_kernel(count, lines, *refs):
    sources, targets, refs = refs[: count + lines], refs[count + lines : 2 * (count + lines)], refs[2 * (count + lines) :]
    moves = [
        (Gather if i < count else LineGather)(sources[i], targets[i], *refs[3 * i : 3 * i + 3])
        for i in range(count + lines)
    ]
    gathers, lines = moves[:count], moves[count:]
    greet(line=True)
    gathers[0].send()
    for line in lines:
        line.send()
    gathers[0].pass_on()
    for gather in gathers[1:]:
        gather.send()
    gathers[0].pass_seconds()
    for line in lines:
        line.pass_on()
    gathers[0].finish()
    for gather in gathers[1:]:
        gather.pass_on()
        gather.pass_seconds()
        gather.finish()
    for line in lines:
        line.finish()


def gather_in_plane(owns, lines, identity):
    size = sum(own.size * own.dtype.itemsize for own in owns)
    count = len(owns) + len(lines)
    return pl.pallas_call(
        functools.partial(gather_kernel, len(owns), len(lines)),
        in_specs=[STAGED] * count,
        out_specs=[ANYWHERE] * count,
        out_shape=[gathered_shape(own) for own in owns] + [line_shape(own) for own in lines],
        scratch_shapes=list(Gather.SEMAPHORES) * len(owns) + list(LineGather.SEMAPHORES) * len(lines),
        compiler_params=talking(identity),
        cost_estimate=pl.CostEstimate(
            flops=0, bytes_accessed=16 * size, transcendentals=0, remote_bytes_transferred=7 * size
        ),
    )(*owns, *lines)


class Plane:
    def __init__(self, size):
        self.size = size
        self.relative = size == 8

    def swap(self, value, bits):
        return lax.ppermute(value, "ctx", [(i, i ^ bits) for i in range(self.size)])

    def gather(self, owns):
        wholes = [lax.all_gather(own, "ctx", axis=1, tiled=False) for own in owns]
        s, n, r, d = wholes[0].shape
        return [whole.reshape(s, n // 2, 2, r, d).transpose(2, 0, 1, 3, 4) for whole in wholes]

    def scatter(self, odd, even):
        if not self.relative:
            both = jnp.stack([even, odd], axis=2)
            s, q, p, r, d = both.shape
            return lax.psum_scatter(
                both.reshape(s, q * p, r, d), "ctx", scatter_dimension=1, tiled=False
            ).astype(f32)
        half = odd.shape[0] // 2
        came = self.swap(odd, 1)
        both = (even.astype(f32) + came.astype(f32)).astype(bf16)
        far_x, far_y = self.swap(both[:half, 3], 2), self.swap(both[half:, 3], 4)
        direct_x, direct_y = self.swap(both[:half, 1], 2), self.swap(both[half:, 2], 4)
        to_x = (both[half:, 1].astype(f32) + far_y.astype(f32)).astype(bf16)
        to_y = (both[:half, 2].astype(f32) + far_x.astype(f32)).astype(bf16)
        later_x, later_y = self.swap(to_x, 2), self.swap(to_y, 4)
        from_x = jnp.concatenate([direct_x, later_x], axis=0).astype(f32)
        from_y = jnp.concatenate([later_y, direct_y], axis=0).astype(f32)
        return both[:, 0].astype(f32) + from_x + from_y

    def order(self, places):
        s, n, r = places.shape
        if self.relative:
            me = lax.axis_index("ctx")
            bits = places.reshape(s, 2, 2, 2, r)
            for axis, bit in ((1, 4), (2, 2), (3, 1)):
                bits = jnp.where((me & bit) != 0, jnp.flip(bits, axis), bits)
            places = bits.reshape(s, n, r)
        return places.reshape(s, n // 2, 2, r).transpose(2, 0, 1, 3)


def zero_of(value):
    first = lax.slice(value, (0,) * value.ndim, (1,) * value.ndim).reshape(()).astype(f32)
    return (first != first).astype(jnp.int32)


def after(value, earlier):
    return jnp.where(zero_of(earlier) == 0, value, jnp.zeros_like(value))


def gather_rows(own):
    return lax.all_gather(own, "fsdp", axis=0, tiled=True)


def by_owners(partial, n, rows):
    depth, columns = partial.shape
    return partial.astype(bf16).reshape(n, depth // (n * rows), rows, columns).transpose(1, 0, 2, 3)


def sum_rows(laid):
    groups, n, rows, columns = laid.shape
    return lax.psum_scatter(
        laid.reshape(groups * n * rows, columns), "fsdp", scatter_dimension=0, tiled=True
    ).reshape(n, rows, columns)


def to_owners(sums):
    return lax.all_to_all(sums, "ctx", split_axis=0, concat_axis=0, tiled=True)


PARAMS = pltpu.CompilerParams(vmem_limit_bytes=56 * 1024 * 1024)


def whole_spec(shape):
    return pl.BlockSpec(shape, lambda i: (0,) * len(shape), pipeline_mode=pl.Buffered(1))


def tile_spec(tile, width):
    return pl.BlockSpec((tile, width), lambda i: (i, 0))


def project_kernel(x_ref, gain_ref, cos_ref, sin_ref, w_ref, low_ref, q_ref, k_ref, v_ref):
    x = x_ref[...].astype(f32)
    low = (x * rms_scale(x) * gain_ref[...]).astype(bf16)
    low_ref[...] = low
    lanes = q_ref.shape[-1]
    projected = dot(low, w_ref[...])
    cosine, sine = cos_ref[...], sin_ref[...]
    q_ref[...] = rotate(projected[:, :lanes], cosine, sine).astype(bf16)
    k_ref[...] = rotate(projected[:, lanes : 2 * lanes], cosine, sine).astype(bf16)
    v_ref[...] = projected[:, 2 * lanes :].astype(bf16)


def project(x, gain, cosine, sine, weight):
    tokens, d = x.shape
    lanes = cosine.shape[1]
    tile = min(512, tokens)
    return pl.pallas_call(
        project_kernel,
        grid=(tokens // tile,),
        in_specs=[tile_spec(tile, d), whole_spec((1, d))]
        + [tile_spec(tile, lanes)] * 2
        + [whole_spec(weight.shape)],
        out_specs=[tile_spec(tile, d)] + [tile_spec(tile, lanes)] * 3,
        out_shape=[jax.ShapeDtypeStruct((tokens, d), bf16)]
        + [jax.ShapeDtypeStruct((tokens, lanes), bf16)] * 3,
        compiler_params=PARAMS,
        cost_estimate=pl.CostEstimate(
            flops=6 * tokens * d * lanes, bytes_accessed=6 * tokens * d, transcendentals=0
        ),
    )(x, gain.reshape(1, d), cosine, sine, weight)


def residual_kernel(x_ref, att_ref, gain_ref, w_ref, low_ref, res_ref):
    n, _, width = w_ref.shape
    for c in range(n):
        columns = slice(c * width, (c + 1) * width)
        res_ref[:, columns] = x_ref[:, columns].astype(f32) + dot(att_ref[...], w_ref[c])
    residual = res_ref[...]
    low_ref[...] = (residual * rms_scale(residual) * gain_ref[...]).astype(bf16)


def residuals(x, attended, gain, out_blocks):
    tokens, d = x.shape
    tile = min(512, tokens)
    return pl.pallas_call(
        residual_kernel,
        grid=(tokens // tile,),
        in_specs=[tile_spec(tile, d), tile_spec(tile, d), whole_spec((1, d)), whole_spec(out_blocks.shape)],
        out_specs=[tile_spec(tile, d), tile_spec(tile, d)],
        out_shape=[jax.ShapeDtypeStruct((tokens, d), bf16), jax.ShapeDtypeStruct((tokens, d), f32)],
        compiler_params=PARAMS,
        cost_estimate=pl.CostEstimate(
            flops=2 * tokens * d * d, bytes_accessed=10 * tokens * d, transcendentals=0
        ),
    )(x, attended, gain.reshape(1, d), out_blocks)


def gathered_residual_kernel(x_ref, gain_ref, w_ref, *refs):
    parts, (own_ref, low_ref, res_ref, all_ref, att, total) = refs[:8], refs[8:14]
    line = LineGather(own_ref, all_ref, *refs[14:])
    step, steps = pl.program_id(0) * pl.num_programs(1) + pl.program_id(1), 8
    pl.when(step == 0)(lambda: greet(line=True))
    line.ride(step, steps)
    width = w_ref.shape[-1]
    shape = low_ref.shape

    def columns(index):
        return pl.ds(pl.multiple_of(flipped(lax.axis_index("ctx"), index) * width, width), width)

    for index, part in enumerate(parts):
        att[:, columns(index)] = part[...].reshape(-1, width)
    attended = att[...]
    for index in range(8):
        total[:, columns(index)] = dot(attended, w_ref[index % 2, :, index // 2].reshape(-1, width))
    residual = total[...] + x_ref[...].reshape(attended.shape).astype(f32)
    res_ref[...] = residual.reshape(shape)
    low_ref[...] = (residual * rms_scale(residual) * gain_ref[...]).astype(bf16).reshape(shape)
    pl.when(step == steps - 1)(line.finish)


def gathered_residuals(x, attended, gain, out_blocks, own, identity):
    _, s, q, r, d = x.shape
    width = attended.shape[-1]
    tile = pl.BlockSpec((1, s, 1, r, d), lambda p, t: (p, 0, t, 0, 0))

    def sent(index):
        odd, other = index % 2, index // 2
        return pl.BlockSpec(
            (1, 1, 1, s, 1, r, width),
            lambda p, t: (odd, (p + odd) % 2, other, 0, flipped(t, other), 0, 0),
        )

    def fixed(shape):
        return pl.BlockSpec(shape, lambda p, t: (0,) * len(shape), pipeline_mode=pl.Buffered(1))

    return pl.pallas_call(
        gathered_residual_kernel,
        grid=(2, q),
        in_specs=[tile, fixed((1, d)), fixed(out_blocks.shape)]
        + [sent(i) for i in range(8)]
        + [STAGED],
        out_specs=[tile, tile, ANYWHERE],
        out_shape=[
            jax.ShapeDtypeStruct(x.shape, bf16),
            jax.ShapeDtypeStruct(x.shape, f32),
            line_shape(own),
        ],
        scratch_shapes=[
            pltpu.VMEM((s * r, d), bf16),
            pltpu.VMEM((s * r, d), f32),
            *LineGather.SEMAPHORES,
        ],
        compiler_params=talking(identity),
        cost_estimate=pl.CostEstimate(
            flops=2 * x.size * d, bytes_accessed=10 * x.size, transcendentals=0
        ),
    )(x, gain.reshape(1, d), out_blocks, *[attended] * 8, own)


def hidden_kernel(skipped, low_ref, cot_ref, w_gate, w_up, w_down, *refs):
    hidden_ref, gate_ref, up_ref = refs[skipped:]
    low = low_ref[...]
    gate, upward = dot(low, w_gate[...]), dot(low, w_up[...])
    grad_hidden = dot(cot_ref[...], w_down[...])
    sigmoid = jax.nn.sigmoid(gate)
    hidden_ref[...] = (gate * sigmoid * upward).astype(bf16)
    gate_ref[...] = (grad_hidden * upward * sigmoid * (1.0 + gate * (1.0 - sigmoid))).astype(bf16)
    up_ref[...] = (grad_hidden * gate * sigmoid).astype(bf16)


def block_specs(weights):
    return [
        pl.BlockSpec((array.shape[0], width), lambda i, pick=pick: (0, pick), pipeline_mode=pl.Buffered(1))
        for array, width, pick in weights
    ]


def arrays(weights):
    return [array for array, _, _ in weights]


def hidden_part(second_low, cot, weights, earlier=()):
    tokens, d = second_low.shape
    step = weights[0][1]
    tile = min(512, tokens)
    return pl.pallas_call(
        functools.partial(hidden_kernel, len(earlier)),
        grid=(tokens // tile,),
        in_specs=[tile_spec(tile, d)] * 2 + block_specs(weights) + [ANYWHERE] * len(earlier),
        out_specs=[tile_spec(tile, step)] * 3,
        out_shape=[jax.ShapeDtypeStruct((tokens, step), bf16)] * 3,
        compiler_params=PARAMS,
        cost_estimate=pl.CostEstimate(
            flops=6 * tokens * d * step, bytes_accessed=4 * tokens * d, transcendentals=tokens * step
        ),
    )(second_low, cot, *arrays(weights), *earlier)


def back_kernel(count, *refs):
    lefts, weights = refs[:count], refs[count : 2 * count]
    total = None
    for left, weight in zip(lefts, weights):
        part = dot_rows(left[...], weight[...])
        total = part if total is None else total + part
    refs[2 * count][...] = total.astype(bf16)


def taken(weights):
    return [
        (array, width, pick)
        if width % 128 == 0
        else (lax.slice_in_dim(array, pick * width, (pick + 1) * width, axis=1), width, 0)
        for array, width, pick in weights
    ]


def back(lefts, weights, first, tokens):
    d = weights[0][0].shape[0]
    tile = min(256, tokens)
    start = first // tile
    weights = taken(weights)
    return pl.pallas_call(
        functools.partial(back_kernel, len(lefts)),
        grid=(tokens // tile,),
        in_specs=[pl.BlockSpec((tile, left.shape[1]), lambda i: (i + start, 0)) for left in lefts]
        + block_specs(weights),
        out_specs=tile_spec(tile, d),
        out_shape=jax.ShapeDtypeStruct((tokens, d), bf16),
        compiler_params=PARAMS,
        cost_estimate=pl.CostEstimate(
            flops=2 * tokens * d * sum(left.shape[1] for left in lefts),
            bytes_accessed=4 * tokens * d,
            transcendentals=0,
        ),
    )(*lefts, *arrays(weights))


FAR, BY_X, BY_Y, OWN = 3, 1, 2, 0
TURNS = ((1, FAR), (1, BY_X), (0, FAR), (1, BY_Y), (0, BY_X), (1, OWN), (0, BY_Y), (0, OWN))
PARITIES = sum(p << t for t, (p, _) in enumerate(TURNS))
PLACES = sum(q << (2 * t) for t, (_, q) in enumerate(TURNS))


def norm_back(grad, x, base, gain):
    scale = rms_scale(x)
    weighted = gain * grad
    mean = jnp.mean(weighted * x, axis=-1, keepdims=True)
    return base + scale * weighted - x * (scale * scale * scale) * mean, grad * x * scale


def back_scatter_kernel(count, skipped, riding, *refs):
    lefts, weights, refs = refs[:count], refs[count : 2 * count], refs[2 * count + skipped :]
    laid, refs = refs[:riding], refs[riding:]
    based = len(refs) - riding - (15 if riding else 11) == 6
    base_ref, refs = (refs[0], refs[1:]) if based else (None, refs)
    x_ref, gain_ref, grad_ref, low_ref, sum_ref = refs[:5]
    lines, refs = refs[5 : 5 + riding], refs[5 + riding :]
    given, got, sums, own, far, from_x, from_y, send_odd, came_odd, sent, came = refs[:11]
    lines = [LineSum(laid[0], 0, out, *refs[11:]) for out in lines]
    sibling, by_x, by_y = neighbours()
    greet(line=riding > 0)
    for line in lines:
        line.send()
    s, r, d = own.shape
    half = s // 2

    def move(partner, source, target, send_sem, recv_sem):
        return pltpu.make_async_remote_copy(
            src_ref=source,
            dst_ref=target,
            send_sem=send_sem,
            recv_sem=recv_sem,
            device_id={"ctx": partner},
            device_id_type=MESH,
        )

    def odd_copy(q):
        return move(sibling, given.at[q], got.at[q], send_odd.at[q], came_odd.at[q])

    low_half, high_half = pl.ds(0, half), pl.ds(half, half)
    far_x = move(by_x, sums.at[FAR, low_half], far.at[low_half], sent.at[0], came.at[0])
    far_y = move(by_y, sums.at[FAR, high_half], far.at[high_half], sent.at[1], came.at[1])
    first_x = move(by_x, sums.at[BY_X, low_half], from_x.at[low_half], sent.at[2], came.at[2])
    first_y = move(by_y, sums.at[BY_Y, high_half], from_y.at[high_half], sent.at[3], came.at[3])
    last_x = move(by_x, sums.at[BY_X, high_half], from_x.at[high_half], sent.at[4], came.at[4])
    last_y = move(by_y, sums.at[BY_Y, low_half], from_y.at[low_half], sent.at[5], came.at[5])

    def turn(t, _):
        p = lax.shift_right_logical(jnp.int32(PARITIES), t) % 2
        q = lax.shift_right_logical(jnp.int32(PLACES), 2 * t) % 4
        total = None
        for left, weight in zip(lefts, weights):
            width = left.shape[-1]
            part = dot_rows(left[p, :, q].reshape(s * r, width), weight[...])
            total = part if total is None else total + part
        total = total.reshape(s, r, d)

        @pl.when(p == 1)
        def _():
            given[q] = total.astype(bf16)
            odd_copy(q).start()

        @pl.when(p == 0)
        def _():
            odd_copy(q).wait_recv()
            both = total + got[q].astype(f32)

            @pl.when(q == OWN)
            def _():
                own[...] = both

            @pl.when(q != OWN)
            def _():
                sums[q] = both.astype(bf16)

            @pl.when(q == FAR)
            def _():
                far_x.start()
                far_y.start()

            @pl.when(q == BY_X)
            def _():
                first_x.start()

            @pl.when(q == BY_Y)
            def _():
                first_y.start()

        return 0

    lax.fori_loop(0, len(TURNS), turn, 0)
    for line in lines:
        line.pass_on()
    far_x.wait_recv()
    sums[BY_Y, low_half] = (sums[BY_Y, low_half].astype(f32) + far[low_half].astype(f32)).astype(bf16)
    last_y.start()
    far_y.wait_recv()
    sums[BY_X, high_half] = (sums[BY_X, high_half].astype(f32) + far[high_half].astype(f32)).astype(bf16)
    last_x.start()
    first_x.wait_recv()
    first_y.wait_recv()
    own[low_half] += from_x[low_half].astype(f32)
    own[high_half] += from_y[high_half].astype(f32)
    last_y.wait_recv()
    own[low_half] += from_y[low_half].astype(f32)
    last_x.wait_recv()
    own[high_half] += from_x[high_half].astype(f32)

    sum_ref[...] = jnp.zeros_like(sum_ref)
    slab = min(32, r)

    def finish(index, _):
        at = (index // (r // slab), pl.ds(pl.multiple_of((index % (r // slab)) * slab, slab), slab))
        base = base_ref[at].astype(f32) if based else 0.0
        grad, terms = norm_back(own[at], x_ref[at].astype(f32), base, gain_ref[...])
        grad_ref[at] = grad
        low_ref[at] = grad.astype(bf16)
        sum_ref[...] += jnp.sum(terms, axis=0, keepdims=True)
        return 0

    lax.fori_loop(0, s * (r // slab), finish, 0)
    for line in lines:
        line.finish()
    for copy in (far_x, far_y, first_x, first_y, last_x, last_y):
        copy.wait_send()
    for q in range(4):
        odd_copy(q).wait_send()


def back_scatter(lefts, weights, shape, identity, x, base, gain, earlier=(), last=False, laid=None):
    s, q, r, d = shape
    width = sum(left.shape[-1] for left in lefts)
    weights = taken(weights)
    lefts = [left.reshape(2, s, q, r, left.shape[-1]) for left in lefts]

    def fixed(whole):
        return pl.BlockSpec(whole, lambda i: (0,) * len(whole), pipeline_mode=pl.Buffered(1))

    operands = [*lefts, *arrays(weights), *earlier]
    in_specs = [fixed(left.shape) for left in lefts] + block_specs(weights)
    in_specs += [ANYWHERE] * len(earlier)
    riding = laid is not None
    based = base is not None
    operands += [laid] * riding + [base] * based + [x, gain.reshape(1, d)]
    in_specs += [ANYWHERE] * riding + [fixed((s, r, d))] * (1 + based) + [fixed((1, d))]
    out_specs = [fixed((s, r, d)), fixed((s, r, d)), fixed((1, d))]
    out_shape = [
        jax.ShapeDtypeStruct((s, r, d), f32),
        jax.ShapeDtypeStruct((s, r, d), bf16),
        jax.ShapeDtypeStruct((1, d), f32),
    ]
    line_scratch = []
    if riding:
        part = (laid.shape[1], laid.shape[2], laid.shape[3] // 2)
        out_specs.append(fixed(part))
        out_shape.append(jax.ShapeDtypeStruct(part, bf16))
        line_scratch = LineSum.scratch(laid.shape, part[2])
    dma = pltpu.SemaphoreType.DMA
    return pl.pallas_call(
        functools.partial(back_scatter_kernel, len(lefts), len(earlier), int(riding)),
        grid=(1,),
        in_specs=in_specs,
        out_specs=out_specs,
        out_shape=out_shape,
        scratch_shapes=[
            pltpu.VMEM((4, s, r, d), bf16),
            pltpu.VMEM((4, s, r, d), bf16),
            pltpu.VMEM((4, s, r, d), bf16),
            pltpu.VMEM((s, r, d), f32),
            pltpu.VMEM((s, r, d), bf16),
            pltpu.VMEM((s, r, d), bf16),
            pltpu.VMEM((s, r, d), bf16),
            dma((4,)),
            dma((4,)),
            dma((6,)),
            dma((6,)),
            *line_scratch,
        ],
        compiler_params=talking(identity),
        cost_estimate=pl.CostEstimate(
            flops=1 if last else 16 * s * r * d * width,
            bytes_accessed=1 if last else 16 * s * r * d,
            transcendentals=0,
            remote_bytes_transferred=1 if last else 14 * s * r * d,
        ),
    )(*operands)


def token_sums_kernel(counts, *refs):
    out_ref = refs[-1]
    start = 0
    for count in counts:
        left, rights, refs = refs[0], refs[1 : 1 + count], refs[1 + count :]
        for right in rights:
            width = right.shape[1]
            part = dot_tokens(left[...], right[...]).astype(bf16)
            groups, owners, rows, _ = out_ref.shape
            part = part.reshape(owners, groups, rows, width)
            for owner in range(owners):
                out_ref[:, owner, :, start : start + width] = part[owner]
            start += width


def token_sums(pairs, n, rows, earlier=()):
    groups = pairs[0][0].shape[1] // (n * rows)
    operands, in_specs, width = [], [], 0
    for left, rights in pairs:
        operands += [left, *rights]
        in_specs.append(pl.BlockSpec((left.shape[0], 2 * groups * rows), lambda i: (0, i)))
        in_specs += [whole_spec(right.shape) for right in rights]
        width += sum(right.shape[1] for right in rights)
    tokens, d = pairs[0][0].shape
    return pl.pallas_call(
        functools.partial(token_sums_kernel, [len(rights) for _, rights in pairs]),
        grid=(n // 2,),
        in_specs=in_specs + [ANYWHERE] * len(earlier),
        out_specs=pl.BlockSpec((groups, 2, rows, width), lambda i: (0, i, 0, 0)),
        out_shape=jax.ShapeDtypeStruct((groups, n, rows, width), bf16),
        compiler_params=PARAMS,
        cost_estimate=pl.CostEstimate(
            flops=2 * tokens * d * width, bytes_accessed=4 * tokens * d, transcendentals=0
        ),
    )(*operands, *earlier)


def output_back_kernel(low_ref, att_ref, w_ref, *refs):
    grad_ref, sum_ref, total = refs[-3:]

    @pl.when(pl.program_id(0) == 0)
    def _():
        total[...] = jnp.zeros_like(total)

    low = low_ref[...]
    grad_ref[...] = dot_rows(low, w_ref[...]).astype(bf16)
    total[...] += dot_tokens(att_ref[...], low)

    @pl.when(pl.program_id(0) == pl.num_programs(0) - 1)
    def _():
        groups, n, rows, width = sum_ref.shape
        for group in range(groups):
            for c in range(n):
                part = total[group * rows : (group + 1) * rows, c * width : (c + 1) * width]
                sum_ref[group, c] = part.astype(bf16)


def output_back(grad_low, attended_low, out_rows, n, rows, earlier=()):
    tokens, d = grad_low.shape
    lanes = attended_low.shape[1]
    sums = (lanes // rows, n, rows, d // n)
    tile = min(512, tokens)
    return pl.pallas_call(
        output_back_kernel,
        grid=(tokens // tile,),
        in_specs=[tile_spec(tile, d), tile_spec(tile, lanes), whole_spec((lanes, d))]
        + [ANYWHERE] * len(earlier),
        out_specs=[tile_spec(tile, lanes), pl.BlockSpec(sums, lambda i: (0, 0, 0, 0))],
        out_shape=[
            jax.ShapeDtypeStruct((tokens, lanes), bf16),
            jax.ShapeDtypeStruct(sums, bf16),
        ],
        scratch_shapes=[pltpu.VMEM((lanes, d), f32)],
        compiler_params=PARAMS,
        cost_estimate=pl.CostEstimate(
            flops=4 * tokens * d * lanes, bytes_accessed=2 * tokens * d, transcendentals=0
        ),
    )(grad_low, attended_low, out_rows, *earlier)


def gather_and_sum_kernel(hiddens, skipped, low_ref, gate_ref, up_ref, cot_ref, *refs):
    lefts, weights = refs[:hiddens], refs[hiddens : 2 * hiddens]
    refs = refs[2 * hiddens :]
    own_ref, refs = refs[0], refs[1 + skipped :]
    sum_ref, out_ref, all_ref = refs[:3]
    gather = Gather(own_ref, all_ref, *refs[3:])
    step, steps = pl.program_id(0), 8
    pl.when(step == 0)(greet)
    gather.ride(step, steps)
    tile = lefts[0].shape[0] // steps
    token_sums_kernel([2, 1], low_ref, gate_ref, up_ref, cot_ref, lefts[-1], sum_ref)
    rows = pl.ds(pl.multiple_of(step * tile, tile), tile)
    total = None
    for left, weight in zip(lefts, weights):
        part = dot_rows(left[rows, :], weight[...])
        total = part if total is None else total + part
    out_ref[...] = total.astype(bf16)
    pl.when(step == steps - 1)(gather.finish)


def gather_and_sum(own, second_low, grads, cot, hiddens, weights, rows, identity, earlier=()):
    tokens, d = second_low.shape
    step = hiddens[0].shape[1]
    groups = d // (8 * rows)
    column = pl.BlockSpec((tokens, groups * rows), lambda i: (0, i))
    return pl.pallas_call(
        functools.partial(gather_and_sum_kernel, len(hiddens), len(earlier)),
        grid=(8,),
        in_specs=[column, whole_spec(grads[0].shape), whole_spec(grads[1].shape), column]
        + [whole_spec(hidden.shape) for hidden in hiddens]
        + block_specs(weights)
        + [STAGED]
        + [ANYWHERE] * len(earlier),
        out_specs=[
            pl.BlockSpec((groups, 1, rows, 3 * step), lambda i: (0, i, 0, 0)),
            tile_spec(tokens // 8, d),
            ANYWHERE,
        ],
        out_shape=[
            jax.ShapeDtypeStruct((groups, 8, rows, 3 * step), bf16),
            jax.ShapeDtypeStruct((tokens, d), bf16),
            gathered_shape(own),
        ],
        scratch_shapes=list(Gather.SEMAPHORES),
        compiler_params=talking(identity),
        cost_estimate=pl.CostEstimate(
            flops=14 * tokens * d * step, bytes_accessed=12 * tokens * d, transcendentals=0
        ),
    )(second_low, *grads, cot, *hiddens, *arrays(weights), own, *earlier)


def spread_kernel(count, *refs):
    parts, out_ref, last_ref = refs[:count], refs[count], refs[count + 1]
    senders, _, width = parts[0].shape

    def write(target):
        for sender in range(senders):
            for index, part in enumerate(parts):
                start = (sender * count + index) * width
                target[:, start : start + width] = part[sender].astype(f32)

    pl.when(pl.program_id(0) < 2)(lambda: write(out_ref))
    pl.when(pl.program_id(0) == 2)(lambda: write(last_ref))


def spread(parts, width):
    n, rows, _ = parts[0][0].shape
    count = len(parts)
    pair = min(n, 4)
    wide = pair * count * width
    turns = n // pair
    return pl.pallas_call(
        functools.partial(spread_kernel, count),
        grid=(3, turns),
        in_specs=[
            pl.BlockSpec((pair, rows, width), lambda third, i, place=place: (i, 0, 3 * place + third))
            for _, place in parts
        ],
        out_specs=[
            pl.BlockSpec((rows, wide), lambda third, i: (0, jnp.minimum(third * turns + i, 2 * turns - 1))),
            pl.BlockSpec((rows, wide), lambda third, i: (0, jnp.maximum(third - 1, 0) * i)),
        ],
        out_shape=[
            jax.ShapeDtypeStruct((rows, 2 * n * count * width), f32),
            jax.ShapeDtypeStruct((rows, n * count * width), f32),
        ],
        compiler_params=PARAMS,
        cost_estimate=pl.CostEstimate(
            flops=0, bytes_accessed=18 * n * rows * count * width, transcendentals=0
        ),
    )(*[whole for whole, _ in parts])


def spread_all_kernel(part_ref, _, out_ref):
    senders, _, width = part_ref.shape
    for sender in range(senders):
        out_ref[:, sender * width : (sender + 1) * width] = part_ref[sender].astype(f32)


def spread_all(part, width, earlier):
    n, rows, _ = part.shape
    return pl.pallas_call(
        spread_all_kernel,
        grid=(3,),
        in_specs=[pl.BlockSpec((n, rows, width), lambda i: (0, 0, i)), ANYWHERE],
        out_specs=pl.BlockSpec((rows, n * width), lambda i: (0, i)),
        out_shape=jax.ShapeDtypeStruct((rows, 3 * n * width), f32),
        compiler_params=PARAMS,
        cost_estimate=pl.CostEstimate(
            flops=0, bytes_accessed=18 * n * rows * width, transcendentals=0
        ),
    )(part, earlier)


class PlaneSum:
    @staticmethod
    def scratch(shape):
        _, s, q, r, d = shape
        dma = pltpu.SemaphoreType.DMA
        block = pltpu.VMEM((s, r, d), bf16)
        blocks = pltpu.VMEM((q, s, r, d), bf16)
        return [blocks, blocks, block, block, block, dma((4,)), dma((4,)), dma((4,)), dma((6,)), dma((6,))]

    def __init__(self, parts, out, held, got, far, from_x, from_y, local, send_odd, came_odd, sent, came):
        self.out, self.held, self.got = out, held, got
        self.far, self.from_x, self.from_y = far, from_x, from_y
        sibling, by_x, by_y = neighbours()
        half = far.shape[0] // 2
        self.low, self.high = low, high = pl.ds(0, half), pl.ds(half, half)

        def move(partner, source, target, send_sem, recv_sem):
            return pltpu.make_async_remote_copy(
                src_ref=source,
                dst_ref=target,
                send_sem=send_sem,
                recv_sem=recv_sem,
                device_id={"ctx": partner},
                device_id_type=MESH,
            )

        self.loads = [pltpu.make_async_copy(parts.at[0, :, q], held.at[q], local.at[q]) for q in range(4)]
        self.odd = [
            move(sibling, parts.at[1, :, q], got.at[q], send_odd.at[q], came_odd.at[q]) for q in range(4)
        ]
        routes = [
            (by_x, held.at[FAR, low], far.at[low]),
            (by_y, held.at[FAR, high], far.at[high]),
            (by_x, held.at[BY_X, low], from_x.at[low]),
            (by_y, held.at[BY_Y, high], from_y.at[high]),
            (by_x, held.at[BY_X, high], from_x.at[high]),
            (by_y, held.at[BY_Y, low], from_y.at[low]),
        ]
        self.copies = [
            move(partner, source, target, sent.at[index], came.at[index])
            for index, (partner, source, target) in enumerate(routes)
        ]

    def send(self):
        for q in (FAR, BY_X, BY_Y, OWN):
            self.odd[q].start()
            self.loads[q].start()

    def join(self, q):
        self.loads[q].wait()
        self.odd[q].wait_recv()
        self.held[q] = (self.held[q].astype(f32) + self.got[q].astype(f32)).astype(bf16)

    def send_far(self):
        self.join(FAR)
        self.copies[0].start()
        self.copies[1].start()

    def send_first(self):
        self.join(BY_X)
        self.copies[2].start()
        self.join(BY_Y)
        self.copies[3].start()
        self.join(OWN)

    def send_last(self):
        for arrived, q, part, copy in ((1, BY_X, self.high, 4), (0, BY_Y, self.low, 5)):
            self.copies[arrived].wait_recv()
            added = self.held[q, part].astype(f32) + self.far[part].astype(f32)
            self.held[q, part] = added.astype(bf16)
            self.copies[copy].start()

    def finish(self):
        for copy in self.copies[2:]:
            copy.wait_recv()
        for copy in (*self.copies, *self.odd):
            copy.wait_send()
        total = self.held[OWN].astype(f32) + self.from_x[...].astype(f32) + self.from_y[...].astype(f32)
        self.out[...] = total

    def ride(self, step, steps):
        turns = (0, self.send), (steps // 8, self.send_far), (steps // 4, self.send_first)
        for turn, phase in (*turns, (steps // 2, self.send_last)):
            pl.when(step == turn)(phase)


def only(values, head, heads):
    if heads == 1:
        return values
    lane = lax.broadcasted_iota(jnp.int32, values.shape, 1)
    inside = (lane >= head * HEAD_SIZE) & (lane < (head + 1) * HEAD_SIZE)
    return jnp.where(inside, values, jnp.zeros_like(values))


def forward_kernel(heads, q_spot, k_spot, q_ref, k_ref, v_ref, *refs):
    if len(refs) > 2:
        own_ref, line_ref, low_ref, total_ref, all_ref, line_all_ref = refs[:6]
        gather = Gather(own_ref, all_ref, *refs[6:9])
        line = LineGather(line_ref, line_all_ref, *refs[9:])
        steps = pl.num_programs(0) * pl.num_programs(1) * pl.num_programs(2)
        step = (pl.program_id(0) * pl.num_programs(1) + pl.program_id(1)) * pl.num_programs(2)
        step += pl.program_id(2)
        pl.when(step == 0)(lambda: greet(line=True))
        gather.ride(step, steps)
        line.ride(step, steps)
    else:
        low_ref, total_ref = refs
    lanes = q_ref.shape[-1]
    queries = q_ref[0, 0] * bf16(HEAD_SIZE**-0.5)
    keys = k_ref[:, 0].reshape(-1, lanes)
    values = v_ref[:, 0].reshape(-1, lanes)
    allowed = k_spot[0] <= q_spot[0, 0]
    attended = jnp.zeros(queries.shape, f32)
    for head in range(heads):
        scores = dot_rows(keys, only(queries, head, heads))
        scores = jnp.where(allowed, scores, -1e30)
        highest = jnp.max(scores, axis=0, keepdims=True)
        raised = jnp.exp(scores - highest)
        summed = jnp.sum(raised, axis=0, keepdims=True)
        probs = (raised * (1.0 / summed)).astype(bf16)
        total_ref[0, 0, head : head + 1, :] = highest + jnp.log(summed)
        attended += dot_tokens(probs, only(values, head, heads))
    low_ref[0, 0] = attended.astype(bf16)
    if len(refs) > 2:
        pl.when(step == steps - 1)(line.finish)
        pl.when(step == steps - 1)(gather.finish)


def backward_kernel(
    heads, q_spot, k_spot, q_ref, k_ref, v_ref, grad_ref, total_ref, qc_ref, qs_ref, kc_ref, ks_ref, *refs
):
    if len(refs) > 5:
        parts, laid, dq_ref, dk_ref, dv_ref, out_ref, line_ref, dk_sum, dv_sum = refs[:9]
        summing = PlaneSum(parts, out_ref, *refs[9:-4])
        line = LineSum(laid, laid.shape[-1] // 2, line_ref, *refs[-4:])
    else:
        dq_ref, dk_ref, dv_ref, dk_sum, dv_sum = refs
    lanes = q_ref.shape[-1]
    scale = HEAD_SIZE**-0.5
    step = pl.program_id(1) * pl.num_programs(2) + pl.program_id(2)
    if len(refs) > 5:
        turn = pl.program_id(0) * pl.num_programs(1) * pl.num_programs(2) + step
        turns = pl.num_programs(0) * pl.num_programs(1) * pl.num_programs(2)
        pl.when(turn == 0)(lambda: greet(line=True))
        summing.ride(turn, turns)
        pl.when(turn == 0)(line.send)
        pl.when(turn == turns // 2)(line.pass_on)

    @pl.when(step == 0)
    def _():
        dk_sum[...] = jnp.zeros_like(dk_sum)
        dv_sum[...] = jnp.zeros_like(dv_sum)

    queries = q_ref[0, 0] * bf16(scale)
    grads = grad_ref[0, 0]
    keys = k_ref[:, 0].reshape(-1, lanes)
    values = v_ref[:, 0].reshape(-1, lanes)
    allowed = k_spot[0] <= q_spot[0, 0]
    grad_q = jnp.zeros(queries.shape, f32)
    for head in range(heads):
        query = only(queries, head, heads)
        grad = only(grads, head, heads)
        scores = jnp.where(allowed, dot_rows(keys, query), -1e30)
        probs = jnp.exp(scores - total_ref[0, 0, head : head + 1, :])
        dv_sum[...] += dot(probs.astype(bf16), grad)
        weighted = probs * dot_rows(values, grad)
        delta = jnp.sum(weighted, axis=0, keepdims=True)
        grad_scores = (weighted - probs * delta).astype(bf16)
        dk_sum[...] += dot(grad_scores, query)
        grad_q += dot_tokens(grad_scores, only(keys, head, heads))
    dq_ref[0, 0] = rotate_back(grad_q * scale, qc_ref[0, 0], qs_ref[0, 0]).astype(bf16)

    @pl.when(step == pl.num_programs(1) * pl.num_programs(2) - 1)
    def _():
        shape = (dk_ref.shape[0],) + dk_ref.shape[2:]
        cosine = kc_ref[:, 0].reshape(-1, lanes)
        sine = ks_ref[:, 0].reshape(-1, lanes)
        dk_ref[:, 0] = rotate_back(dk_sum[...], cosine, sine).astype(bf16).reshape(shape)
        dv_ref[:, 0] = dv_sum[...].astype(bf16).reshape(shape)

    if len(refs) > 5:
        pl.when(turn == turns - 1)(summing.finish)
        pl.when(turn == turns - 1)(line.finish)


def attention_specs(shape, heads):
    p, s, rows, lanes = shape
    tile = min(256, rows)
    one = pl.BlockSpec((1, 1, tile, lanes), lambda i, j, t: (j, i, t, 0))
    side = pl.BlockSpec((p, 1, rows, lanes), lambda i, j, t: (0, i, 0, 0))
    stat = pl.BlockSpec((1, 1, heads, tile), lambda i, j, t: (j, i, 0, t))
    q_spot = pl.BlockSpec((1, 1, 1, tile), lambda i, j, t: (j, i, 0, t))
    k_spot = pl.BlockSpec((1, p * rows, 1), lambda i, j, t: (i, 0, 0))
    return (s, p, rows // tile), one, side, stat, q_spot, k_spot


def attend(q_spot, k_spot, queries, keys, values, own=None, line=None, identity=None):
    p, s, rows, lanes = queries.shape
    heads = lanes // HEAD_SIZE
    grid, one, side, stat, q_spec, k_spec = attention_specs(queries.shape, heads)
    pairs = p * rows * s * p * rows
    out_shape = [
        jax.ShapeDtypeStruct(queries.shape, bf16),
        jax.ShapeDtypeStruct((p, s, heads, rows), f32),
    ]
    riding = own is not None
    return pl.pallas_call(
        functools.partial(forward_kernel, heads),
        grid=grid,
        in_specs=[q_spec, k_spec, one, side, side] + [STAGED] * (2 * riding),
        out_specs=[one, stat] + [ANYWHERE] * (2 * riding),
        out_shape=out_shape + ([gathered_shape(own), line_shape(line)] if riding else []),
        scratch_shapes=[*Gather.SEMAPHORES, *LineGather.SEMAPHORES] if riding else [],
        compiler_params=talking(identity) if riding else PARAMS,
        cost_estimate=pl.CostEstimate(
            flops=pairs * heads * 2048, bytes_accessed=queries.size * 14, transcendentals=pairs * heads
        ),
    )(q_spot, k_spot, queries, keys, values, *([own, line] if riding else []))


def attend_back(
    q_spot, k_spot, queries, keys, values, grads, totals, cosine, sine, parts=None, laid=None, identity=None
):
    p, s, rows, lanes = queries.shape
    heads = lanes // HEAD_SIZE
    grid, one, side, stat, q_spec, k_spec = attention_specs(queries.shape, heads)
    pairs = p * rows * s * p * rows
    in_specs = [q_spec, k_spec, one, side, side, one, stat, one, one, side, side]
    out_specs = [one, side, side]
    out_shape = [jax.ShapeDtypeStruct(queries.shape, bf16)] * 3
    scratch = [pltpu.VMEM((p * rows, lanes), f32)] * 2
    operands = [q_spot, k_spot, queries, keys, values, grads, totals, cosine, sine, cosine, sine]
    if parts is not None:
        own = (parts.shape[1], *parts.shape[3:])
        part = (*laid.shape[1:3], laid.shape[3] // 2)
        operands += [parts, laid]
        in_specs += [ANYWHERE] * 2
        for shape, kind in ((own, f32), (part, bf16)):
            out_specs.append(pl.BlockSpec(shape, lambda i, j, t: (0, 0, 0), pipeline_mode=pl.Buffered(1)))
            out_shape.append(jax.ShapeDtypeStruct(shape, kind))
        scratch += [*PlaneSum.scratch(parts.shape), *LineSum.scratch(laid.shape, part[2])]
    return pl.pallas_call(
        functools.partial(backward_kernel, heads),
        grid=grid,
        in_specs=in_specs,
        out_specs=out_specs,
        out_shape=out_shape,
        scratch_shapes=scratch,
        compiler_params=PARAMS if parts is None else talking(identity),
        cost_estimate=pl.CostEstimate(
            flops=pairs * heads * 5120, bytes_accessed=queries.size * 20, transcendentals=pairs * heads
        ),
    )(*operands)


def on_device(
    plane,
    inputs,
    positions,
    first_gain,
    attention_weight,
    output_weight,
    second_gain,
    gate_up_weight,
    down_weight,
    cotangent,
):
    s, r, d = inputs.shape
    n = plane.size
    ff = down_weight.shape[1]
    me = lax.axis_index("ctx")
    lanes = d // n
    mine = ff // n
    step = mine // CHUNKS
    tokens = s * r * n
    rows = d // (n * lax.axis_size("fsdp"))
    half = tokens // 2
    group = (2, s, n // 2 * r)
    blocks = (s, n // 2, r, d)

    def columns(weight, start, width):
        return lax.dynamic_slice_in_dim(weight, start, width, 1)

    qkv = jnp.concatenate(
        [columns(attention_weight, part * d + me * lanes, lanes) for part in range(3)], axis=1
    )
    out_own = columns(output_weight, me * lanes, lanes)
    if plane.relative:
        whole_inputs, cot, qkv, out_own = gather_in_plane([inputs, cotangent], [qkv, out_own], 1)
    else:
        whole_inputs, cot = plane.gather([inputs, cotangent])
        qkv, out_own = gather_rows(qkv), gather_rows(out_own)

    def chunk_parts(chunk, earlier):
        start = (me + zero_of(earlier)) * mine + chunk * step
        return [
            columns(gate_up_weight, start, step),
            columns(gate_up_weight, ff + start, step),
            columns(down_weight, start, step),
        ]

    ffn = {}
    for chunk in range(CHUNKS):
        if chunk != RIDING or not plane.relative:
            whole = gather_rows(jnp.concatenate(chunk_parts(chunk, qkv), axis=1))
            ffn[chunk] = [(whole, step, part) for part in range(3)]

    places = plane.order(positions.reshape(s, n, r)).reshape(group)
    q_spot = places[:, :, None, :]
    k_spot = places.transpose(1, 0, 2).reshape(s, n * r, 1)
    cosine, sine = rope_tables(places.reshape(tokens), lanes, whole_inputs)
    normed_low, queries, keys, values = project(
        whole_inputs.reshape(tokens, d), first_gain, cosine, sine, qkv
    )
    queries, keys, values, cosine, sine = (
        part.reshape(*group, lanes) for part in (queries, keys, values, cosine, sine)
    )
    if plane.relative:
        riders = chunk_parts(RIDING, qkv)
        attended_low, totals, out_blocks, gate = attend(
            q_spot, k_spot, queries, keys, values, out_own.reshape(2, d // 2, lanes), riders[0], 2
        )
        attended_whole, upward = gather_in_plane(
            [attended_low.reshape(2, half, lanes)], riders[1:2], 3
        )
        second_low, residual, down = gathered_residuals(
            whole_inputs,
            attended_whole.reshape(2, 2, 4, s, 4, r, lanes),
            second_gain,
            out_blocks,
            riders[2],
            4,
        )
        ffn[RIDING] = [(whole, step, 0) for whole in (gate, upward, down)]
        second_low = second_low.reshape(tokens, d)
        residual = residual[0, :, 0]
    else:
        attended_low, totals = attend(q_spot, k_spot, queries, keys, values)
        out_blocks = lax.all_gather(out_own, "ctx", axis=0, tiled=False)
        attended_whole = lax.all_gather(
            attended_low.reshape(tokens, lanes), "ctx", axis=1, tiled=True
        )
        second_low, residual = residuals(
            whole_inputs.reshape(tokens, d), attended_whole, second_gain, out_blocks
        )
        residual = lax.dynamic_index_in_dim(residual.reshape(2, *blocks), me % 2, 0, keepdims=False)
        residual = lax.dynamic_index_in_dim(residual, me // 2, 1, keepdims=False)
    cot = cot.reshape(tokens, d)
    attended_low = attended_low.reshape(tokens, lanes)

    if plane.relative:
        out_rows = lax.dynamic_slice(
            out_blocks, (0, me // 4, 0, (me % 4) * lanes, 0), (2, 1, 4, lanes, lanes)
        ).reshape(2, 2, 2, lanes, lanes)
        for axis, bit in ((0, 1), (1, 4), (2, 2)):
            out_rows = jnp.where((me & bit) != 0, jnp.flip(out_rows, axis), out_rows)
        out_rows = out_rows.transpose(3, 1, 2, 0, 4).reshape(lanes, d)
    else:
        out_rows = lax.dynamic_slice_in_dim(out_blocks, me * lanes, lanes, 1)
        out_rows = out_rows.transpose(1, 0, 2).reshape(lanes, d)

    def summed(pairs, earlier=()):
        if plane.relative:
            return token_sums(pairs, n, rows, earlier)
        partial = [dot_tokens(left, right) for left, rights in pairs for right in rights]
        return by_owners(jnp.concatenate(partial, axis=1), n, rows)

    hiddens, grads, partials, sums = [], [], [], []
    for chunk in ORDER:
        hidden, *grad_gate_up = hidden_part(
            second_low, cot, taken(ffn[chunk]), partials[-1:] or [out_rows]
        )
        hiddens.append(hidden)
        grads.append(grad_gate_up)
        if len(hiddens) < CHUNKS or not plane.relative:
            partials.append(summed([(second_low, grad_gate_up), (cot, [hidden])]))
            if len(hiddens) < CHUNKS - 1 or not plane.relative:
                sums.append(sum_rows(partials[-1]))

    def apart(lefts, weights):
        odd, even = back(lefts, weights, half, half), back(lefts, weights, 0, half)
        return plane.scatter(odd.reshape(blocks), even.reshape(blocks))

    def norm_step(identity, lefts, weights, x, base, gain, earlier, last=False, laid=None):
        if plane.relative:
            return back_scatter(lefts, weights, blocks, identity, x, base, gain, earlier, last, laid)
        base = 0.0 if base is None else base.astype(f32)
        grad, terms = norm_back(apart(lefts, weights), x.astype(f32), base, gain)
        return grad, grad.astype(bf16), jnp.sum(terms, axis=(0, 1))

    grad_residual, grad_residual_low, second_gain_part, *left_sums = norm_step(
        5,
        [grad for pair in grads for grad in pair],
        [weight for chunk in ORDER for weight in ffn[chunk][:2]],
        residual,
        cotangent,
        second_gain,
        partials[-1:],
        laid=partials[-1] if plane.relative else None,
    )
    downs = [ffn[chunk][2] for chunk in ORDER]
    if plane.relative:
        last, output_parts, grad_low = gather_and_sum(
            grad_residual_low,
            second_low,
            grads[-1],
            cot,
            hiddens,
            downs,
            rows,
            6,
            sums[:1],
        )
    else:
        last = partials[-1]
        sums.pop()
        (grad_low,) = plane.gather([grad_residual_low])
    grad_low = grad_low.reshape(tokens, d)

    grad_attended, out_part = output_back(
        grad_low, attended_low, out_rows, n, rows
    )
    last = sum_rows(last)
    early = to_owners(after(jnp.concatenate(sums[:2], axis=2), grad_attended))
    operands = (q_spot, k_spot, queries, keys, values, grad_attended.reshape(*group, lanes))
    operands += (totals, cosine, sine)
    if plane.relative:
        *grad_projected, output, right_sums = attend_back(
            *operands, output_parts.reshape(2, *blocks), partials[-1], 8
        )
        output = residual + output
        sums += [*left_sums, right_sums]
    else:
        grad_projected = attend_back(*operands)
        output = residual + apart(hiddens, downs)
    grad_projected = [part.reshape(tokens, lanes) for part in grad_projected]
    attention_parts = summed([(normed_low, grad_projected)], [early])
    attention_sums = sum_rows(attention_parts)
    grad_output_weight = sum_rows(after(out_part, attention_parts))
    grad_input, _, first_gain_part = norm_step(
        7,
        grad_projected,
        [(qkv, lanes, part) for part in range(3)],
        inputs,
        None,
        first_gain,
        [attention_parts],
        True,
    )
    grad_input = grad_residual + grad_input
    late = to_owners(jnp.concatenate([*sums[2:], last], axis=2))
    attention_sums = to_owners(after(attention_sums, grad_input))
    gains = jnp.stack([first_gain_part.reshape(d), second_gain_part.reshape(d)])
    gains = after(gains.reshape(2, d // rows, rows).transpose(1, 0, 2), attention_sums)
    gains = jnp.sum(
        lax.all_to_all(gains, ("ctx", "fsdp"), split_axis=0, concat_axis=0, tiled=True), axis=0
    )
    places = [ORDER.index(chunk) for chunk in range(CHUNKS)]
    sums = [(early, place) if place < 2 else (late, place - 2) for place in places]
    if plane.relative:
        grad_gate_up, grad_down = spread(sums, step)
        grad_attention = spread_all(attention_sums, lanes, grad_down)
    else:
        parts = [whole[:, :, 3 * step * place : 3 * step * (place + 1)] for whole, place in sums]
        whole = jnp.stack([part.reshape(n, rows, 3, step) for part in parts], axis=3)
        whole = whole.transpose(1, 2, 0, 3, 4).reshape(rows, 3, ff).astype(f32)
        grad_gate_up, grad_down = whole[:, :2].reshape(rows, 2 * ff), whole[:, 2]
        grad_attention = attention_sums.reshape(n, rows, 3, lanes).transpose(1, 2, 0, 3)
        grad_attention = grad_attention.reshape(rows, 3 * d).astype(f32)
    return (
        output,
        grad_input,
        grad_attention,
        after(grad_output_weight, grad_attention).transpose(1, 0, 2).reshape(rows, d).astype(f32),
        grad_gate_up,
        grad_down,
        gains[0],
        gains[1],
    )


def solution(mesh):
    plane = Plane(mesh.shape["ctx"])
    return jax.shard_map(
        functools.partial(on_device, plane),
        mesh=mesh,
        in_specs=(
            P("fsdp", "ctx", None),
            P("fsdp", None),
            P(),
            P("fsdp", None),
            P("fsdp", None),
            P(),
            P("fsdp", None),
            P("fsdp", None),
            P("fsdp", "ctx", None),
        ),
        out_specs=(
            P("fsdp", "ctx", None),
            P("fsdp", "ctx", None),
            P(("ctx", "fsdp"), None),
            P(("ctx", "fsdp"), None),
            P(("ctx", "fsdp"), None),
            P(("ctx", "fsdp"), None),
            P(("ctx", "fsdp")),
            P(("ctx", "fsdp")),
        ),
        check_vma=False,
    )
```

```python
import functools

import jax
import jax.numpy as jnp
from jax import lax
from jax.experimental import pallas as pl
from jax.experimental.pallas import tpu as pltpu
from jax.sharding import PartitionSpec as P

HEAD_SIZE = 64
EPSILON = 1e-05
ROPE_BASE = 130000.0
CHUNKS = 4
ORDER = (0, 3, 1, 2)
RIDING = 3

f32 = jnp.float32
bf16 = jnp.bfloat16


def rms_scale(values):
    return lax.rsqrt(jnp.mean(values * values, axis=-1, keepdims=True) + EPSILON)


def dot(left, right):
    return jnp.dot(left, right, preferred_element_type=f32)


def dot_rows(left, right):
    return lax.dot_general(left, right, (((1,), (1,)), ((), ())), preferred_element_type=f32)


def dot_tokens(left, right):
    return lax.dot_general(left, right, (((0,), (0,)), ((), ())), preferred_element_type=f32)


def tables_kernel(places_ref, _, cos_ref, sin_ref):
    half = HEAD_SIZE // 2
    width = cos_ref.shape[1]
    narrow = min(width, 128)
    lane = lax.broadcasted_iota(jnp.int32, (1, narrow), 1) % half
    inverse = jnp.exp(-(2.0 * lane.astype(f32) / HEAD_SIZE) * jnp.log(f32(ROPE_BASE)))
    angles = places_ref[...].astype(f32) * inverse
    cosine, sine = jnp.cos(angles), jnp.sin(angles)
    for start in range(0, width, narrow):
        cos_ref[:, start : start + narrow] = cosine
        sin_ref[:, start : start + narrow] = sine


def rope_tables(places, lanes, earlier):
    tokens = places.shape[0]
    tile = min(512, tokens)
    return pl.pallas_call(
        tables_kernel,
        grid=(tokens // tile,),
        in_specs=[pl.BlockSpec((tile, 1), lambda i: (i, 0)), ANYWHERE],
        out_specs=[pl.BlockSpec((tile, lanes), lambda i: (i, 0))] * 2,
        out_shape=[jax.ShapeDtypeStruct((tokens, lanes), f32)] * 2,
        cost_estimate=pl.CostEstimate(
            flops=100 * tokens * lanes, bytes_accessed=8 * tokens * lanes, transcendentals=0
        ),
    )(places.reshape(tokens, 1), earlier)


def other_half(values):
    half = HEAD_SIZE // 2
    lanes = values.shape[-1]
    if lanes == HEAD_SIZE:
        return jnp.concatenate([-values[:, half:], values[:, :half]], axis=1)
    lane = lax.broadcasted_iota(jnp.int32, values.shape, 1)
    return jnp.where(
        lane % HEAD_SIZE < half,
        -pltpu.roll(values, lanes - half, 1),
        pltpu.roll(values, half, 1),
    )


def rotate(values, cosine, sine):
    return values * cosine + other_half(values) * sine


def rotate_back(gradient, cosine, sine):
    return gradient * cosine - other_half(gradient * sine)


MESH = pl.DeviceIdType.MESH


def greet(line=False):
    barrier = pltpu.get_barrier_semaphore()
    partners = [{"ctx": partner} for partner in neighbours()]
    size = lax.axis_size("fsdp")
    if line:
        z = lax.axis_index("fsdp")
        partners += [{"fsdp": (z + shift) % size} for shift in range(1, size)]
    for partner in partners:
        pl.semaphore_signal(barrier, inc=1, device_id=partner, device_id_type=MESH)
    pl.semaphore_wait(barrier, len(partners))


def flipped(place, bits):
    for bit in (1, 2, 4):
        if bits & bit:
            place = place + bit - 2 * bit * ((place // bit) % 2)
    return place


def neighbours():
    me = lax.axis_index("ctx")
    return [flipped(me, bit) for bit in (1, 2, 4)]


class Gather:
    SEMAPHORES = (
        pltpu.SemaphoreType.DMA((2,)),
        pltpu.SemaphoreType.DMA((14,)),
        pltpu.SemaphoreType.DMA((14,)),
    )

    def __init__(self, own, out, local, sent, came):
        sibling, by_x, by_y = neighbours()
        routes = [
            (by_x, own.at[0], out.at[0, 0, 1]),
            (by_y, own.at[1], out.at[0, 1, 2]),
            (by_x, own.at[1], out.at[0, 1, 1]),
            (by_y, own.at[0], out.at[0, 0, 2]),
            (by_y, out.at[0, 0, 1], out.at[0, 0, 3]),
            (by_x, out.at[0, 1, 2], out.at[0, 1, 3]),
        ]
        for h in range(2):
            routes.append((sibling, own.at[h], out.at[1, h, 0]))
        for h, q in ((0, 1), (1, 2), (1, 1), (0, 2), (0, 3), (1, 3)):
            routes.append((sibling, out.at[0, h, q], out.at[1, h, q]))
        self.copies = [
            pltpu.make_async_remote_copy(
                src_ref=source,
                dst_ref=target,
                send_sem=sent.at[index],
                recv_sem=came.at[index],
                device_id={"ctx": partner},
                device_id_type=MESH,
            )
            for index, (partner, source, target) in enumerate(routes)
        ]
        self.kept = [
            pltpu.make_async_copy(own.at[h], out.at[0, h, 0], local.at[h]) for h in range(2)
        ]

    def send(self):
        for index in (0, 1, 2, 3, 6, 7):
            self.copies[index].start()
        for copy in self.kept:
            copy.start()

    def pass_on(self):
        self.copies[0].wait_recv()
        self.copies[4].start()
        self.copies[8].start()
        self.copies[1].wait_recv()
        self.copies[5].start()
        self.copies[9].start()

    def pass_seconds(self):
        self.copies[2].wait_recv()
        self.copies[10].start()
        self.copies[3].wait_recv()
        self.copies[11].start()

    def finish(self):
        self.copies[4].wait_recv()
        self.copies[12].start()
        self.copies[5].wait_recv()
        self.copies[13].start()
        for copy in self.copies[6:]:
            copy.wait_recv()
        for copy in self.copies:
            copy.wait_send()
        for copy in self.kept:
            copy.wait()

    def ride(self, step, steps):
        for turn, phase in ((0, self.send), (steps // 2, self.pass_on), (steps - 1, self.pass_seconds)):
            pl.when(step == turn)(phase)


class LineGather:
    SEMAPHORES = (
        pltpu.SemaphoreType.DMA((1,)),
        pltpu.SemaphoreType.DMA((3,)),
        pltpu.SemaphoreType.DMA((3,)),
    )

    def __init__(self, own, out, local, sent, came):
        z = lax.axis_index("fsdp")
        size = own.shape[0]

        def rows(place):
            return out.at[pl.ds(pl.multiple_of(place * size, size), size)]

        held = z // 2 + 2 * (z % 2)
        routes = [
            ((z + 1) % 4, own, rows(z)),
            ((z + 3) % 4, own, rows(z)),
            (2 * (1 - z % 2) + z // 2, rows(held), rows(held)),
        ]
        if lax.axis_size("fsdp") == 1:
            routes = []
        copies = [
            pltpu.make_async_remote_copy(
                src_ref=source,
                dst_ref=target,
                send_sem=sent.at[index],
                recv_sem=came.at[index],
                device_id={"fsdp": partner},
                device_id_type=MESH,
            )
            for index, (partner, source, target) in enumerate(routes)
        ]
        self.first, self.second = copies[:2], copies[2:]
        self.kept = pltpu.make_async_copy(own, rows(z), local.at[0])

    def send(self):
        for copy in (*self.first, self.kept):
            copy.start()

    def pass_on(self):
        for copy in self.first:
            copy.wait_recv()
        self.kept.wait()
        for copy in self.second:
            copy.start()

    def finish(self):
        for copy in self.second:
            copy.wait_recv()
        for copy in (*self.first, *self.second):
            copy.wait_send()

    def ride(self, step, steps):
        pl.when(step == 0)(self.send)
        pl.when(step == steps - 1)(self.pass_on)


def line_shape(own):
    return jax.ShapeDtypeStruct((lax.axis_size("fsdp") * own.shape[0], own.shape[1]), own.dtype)


class LineSum:
    @staticmethod
    def scratch(shape, width):
        _, n, rows, _ = shape
        return [
            pltpu.VMEM((6, n, rows, width), bf16),
            pltpu.SemaphoreType.DMA((3,)),
            pltpu.SemaphoreType.DMA((3,)),
            pltpu.SemaphoreType.DMA((3,)),
        ]

    def __init__(self, laid, first, out, held, local, sent, came):
        self.z = z = lax.axis_index("fsdp")
        self.size = lax.axis_size("fsdp")
        width = held.shape[-1]
        self.held, self.out = held, out

        def block(shift):
            return laid.at[(z + shift) % self.size, :, :, pl.ds(first, width)]

        def move(index, source, target, partner):
            return pltpu.make_async_remote_copy(
                src_ref=source,
                dst_ref=target,
                send_sem=sent.at[index],
                recv_sem=came.at[index],
                device_id={"fsdp": partner},
                device_id_type=MESH,
            )

        self.loads = [
            pltpu.make_async_copy(block(shift), held.at[index], local.at[index])
            for index, shift in enumerate((0, 1, 3))
        ]
        if self.size == 1:
            return
        self.far = move(0, block(2), held.at[3], 2 * (z % 2) + 1 - z // 2)
        self.up = move(1, held.at[1], held.at[4], (z + 1) % 4)
        self.down = move(2, held.at[2], held.at[5], (z + 3) % 4)

    def send(self):
        for load in self.loads:
            load.start()
        if self.size > 1:
            self.far.start()

    def pass_on(self):
        for load in self.loads:
            load.wait()
        if self.size > 1:
            self.far.wait_recv()
            for index, place, copy in ((1, 1, self.up), (2, 2, self.down)):

                @pl.when(self.z == place)
                def _():
                    added = self.held[index].astype(f32) + self.held[3].astype(f32)
                    self.held[index] = added.astype(bf16)

                copy.start()

    def finish(self):
        total = self.held[0].astype(f32)
        if self.size > 1:
            self.up.wait_recv()
            self.down.wait_recv()
            ends = jnp.where((self.z == 0) | (self.z == 3), 1.0, 0.0)
            total += self.held[4].astype(f32) + self.held[5].astype(f32)
            total += ends * self.held[3].astype(f32)
            for copy in (self.far, self.up, self.down):
                copy.wait_send()
        self.out[...] = total.astype(bf16)


def gathered_shape(own):
    return jax.ShapeDtypeStruct((2, 2, 4) + own.shape[1:], own.dtype)


ANYWHERE = pl.BlockSpec(memory_space=pl.ANY)
STAGED = pl.BlockSpec(memory_space=pltpu.VMEM)


def talking(identity):
    return pltpu.CompilerParams(
        collective_id=identity, has_side_effects=True, vmem_limit_bytes=56 * 1024 * 1024
    )


def gather_kernel(count, lines, *refs):
    sources, targets, refs = refs[: count + lines], refs[count + lines : 2 * (count + lines)], refs[2 * (count + lines) :]
    moves = [
        (Gather if i < count else LineGather)(sources[i], targets[i], *refs[3 * i : 3 * i + 3])
        for i in range(count + lines)
    ]
    gathers, lines = moves[:count], moves[count:]
    greet(line=True)
    gathers[0].send()
    for line in lines:
        line.send()
    gathers[0].pass_on()
    for gather in gathers[1:]:
        gather.send()
    gathers[0].pass_seconds()
    for line in lines:
        line.pass_on()
    gathers[0].finish()
    for gather in gathers[1:]:
        gather.pass_on()
        gather.pass_seconds()
        gather.finish()
    for line in lines:
        line.finish()


def gather_in_plane(owns, lines, identity):
    size = sum(own.size * own.dtype.itemsize for own in owns)
    count = len(owns) + len(lines)
    return pl.pallas_call(
        functools.partial(gather_kernel, len(owns), len(lines)),
        in_specs=[STAGED] * count,
        out_specs=[ANYWHERE] * count,
        out_shape=[gathered_shape(own) for own in owns] + [line_shape(own) for own in lines],
        scratch_shapes=list(Gather.SEMAPHORES) * len(owns) + list(LineGather.SEMAPHORES) * len(lines),
        compiler_params=talking(identity),
        cost_estimate=pl.CostEstimate(
            flops=0, bytes_accessed=16 * size, transcendentals=0, remote_bytes_transferred=7 * size
        ),
    )(*owns, *lines)


class Plane:
    def __init__(self, size):
        self.size = size
        self.relative = size == 8

    def swap(self, value, bits):
        return lax.ppermute(value, "ctx", [(i, i ^ bits) for i in range(self.size)])

    def gather(self, owns):
        wholes = [lax.all_gather(own, "ctx", axis=1, tiled=False) for own in owns]
        s, n, r, d = wholes[0].shape
        return [whole.reshape(s, n // 2, 2, r, d).transpose(2, 0, 1, 3, 4) for whole in wholes]

    def scatter(self, odd, even):
        if not self.relative:
            both = jnp.stack([even, odd], axis=2)
            s, q, p, r, d = both.shape
            return lax.psum_scatter(
                both.reshape(s, q * p, r, d), "ctx", scatter_dimension=1, tiled=False
            ).astype(f32)
        half = odd.shape[0] // 2
        came = self.swap(odd, 1)
        both = (even.astype(f32) + came.astype(f32)).astype(bf16)
        far_x, far_y = self.swap(both[:half, 3], 2), self.swap(both[half:, 3], 4)
        direct_x, direct_y = self.swap(both[:half, 1], 2), self.swap(both[half:, 2], 4)
        to_x = (both[half:, 1].astype(f32) + far_y.astype(f32)).astype(bf16)
        to_y = (both[:half, 2].astype(f32) + far_x.astype(f32)).astype(bf16)
        later_x, later_y = self.swap(to_x, 2), self.swap(to_y, 4)
        from_x = jnp.concatenate([direct_x, later_x], axis=0).astype(f32)
        from_y = jnp.concatenate([later_y, direct_y], axis=0).astype(f32)
        return both[:, 0].astype(f32) + from_x + from_y

    def order(self, places):
        s, n, r = places.shape
        if self.relative:
            me = lax.axis_index("ctx")
            bits = places.reshape(s, 2, 2, 2, r)
            for axis, bit in ((1, 4), (2, 2), (3, 1)):
                bits = jnp.where((me & bit) != 0, jnp.flip(bits, axis), bits)
            places = bits.reshape(s, n, r)
        return places.reshape(s, n // 2, 2, r).transpose(2, 0, 1, 3)


def zero_of(value):
    first = lax.slice(value, (0,) * value.ndim, (1,) * value.ndim).reshape(()).astype(f32)
    return (first != first).astype(jnp.int32)


def after(value, earlier):
    return jnp.where(zero_of(earlier) == 0, value, jnp.zeros_like(value))


def gather_rows(own):
    return lax.all_gather(own, "fsdp", axis=0, tiled=True)


def by_owners(partial, n, rows):
    depth, columns = partial.shape
    return partial.astype(bf16).reshape(n, depth // (n * rows), rows, columns).transpose(1, 0, 2, 3)


def sum_rows(laid):
    groups, n, rows, columns = laid.shape
    return lax.psum_scatter(
        laid.reshape(groups * n * rows, columns), "fsdp", scatter_dimension=0, tiled=True
    ).reshape(n, rows, columns)


def line_total(value):
    size = lax.axis_size("fsdp")
    bit = 1
    while bit < size:
        value = value + lax.ppermute(value, "fsdp", [(i, i ^ bit) for i in range(size)])
        bit = 2 * bit
    return lax.dynamic_index_in_dim(value, lax.axis_index("fsdp"), value.ndim - 1, keepdims=False)


def to_owners(sums):
    return lax.all_to_all(sums, "ctx", split_axis=0, concat_axis=0, tiled=True)


PARAMS = pltpu.CompilerParams(vmem_limit_bytes=56 * 1024 * 1024)


def whole_spec(shape):
    return pl.BlockSpec(shape, lambda i: (0,) * len(shape), pipeline_mode=pl.Buffered(1))


def tile_spec(tile, width):
    return pl.BlockSpec((tile, width), lambda i: (i, 0))


def project_kernel(x_ref, gain_ref, cos_ref, sin_ref, w_ref, low_ref, q_ref, k_ref, v_ref):
    x = x_ref[...].astype(f32)
    low = (x * rms_scale(x) * gain_ref[...]).astype(bf16)
    low_ref[...] = low
    lanes = q_ref.shape[-1]
    projected = dot(low, w_ref[...])
    cosine, sine = cos_ref[...], sin_ref[...]
    q_ref[...] = rotate(projected[:, :lanes], cosine, sine).astype(bf16)
    k_ref[...] = rotate(projected[:, lanes : 2 * lanes], cosine, sine).astype(bf16)
    v_ref[...] = projected[:, 2 * lanes :].astype(bf16)


def project(x, gain, cosine, sine, weight):
    tokens, d = x.shape
    lanes = cosine.shape[1]
    tile = min(512, tokens)
    return pl.pallas_call(
        project_kernel,
        grid=(tokens // tile,),
        in_specs=[tile_spec(tile, d), whole_spec((1, d))]
        + [tile_spec(tile, lanes)] * 2
        + [whole_spec(weight.shape)],
        out_specs=[tile_spec(tile, d)] + [tile_spec(tile, lanes)] * 3,
        out_shape=[jax.ShapeDtypeStruct((tokens, d), bf16)]
        + [jax.ShapeDtypeStruct((tokens, lanes), bf16)] * 3,
        compiler_params=PARAMS,
        cost_estimate=pl.CostEstimate(
            flops=6 * tokens * d * lanes, bytes_accessed=6 * tokens * d, transcendentals=0
        ),
    )(x, gain.reshape(1, d), cosine, sine, weight)


def residual_kernel(x_ref, att_ref, gain_ref, w_ref, low_ref, res_ref):
    n, _, width = w_ref.shape
    for c in range(n):
        columns = slice(c * width, (c + 1) * width)
        res_ref[:, columns] = x_ref[:, columns].astype(f32) + dot(att_ref[...], w_ref[c])
    residual = res_ref[...]
    low_ref[...] = (residual * rms_scale(residual) * gain_ref[...]).astype(bf16)


def residuals(x, attended, gain, out_blocks):
    tokens, d = x.shape
    tile = min(512, tokens)
    return pl.pallas_call(
        residual_kernel,
        grid=(tokens // tile,),
        in_specs=[tile_spec(tile, d), tile_spec(tile, d), whole_spec((1, d)), whole_spec(out_blocks.shape)],
        out_specs=[tile_spec(tile, d), tile_spec(tile, d)],
        out_shape=[jax.ShapeDtypeStruct((tokens, d), bf16), jax.ShapeDtypeStruct((tokens, d), f32)],
        compiler_params=PARAMS,
        cost_estimate=pl.CostEstimate(
            flops=2 * tokens * d * d, bytes_accessed=10 * tokens * d, transcendentals=0
        ),
    )(x, attended, gain.reshape(1, d), out_blocks)


def gathered_residual_kernel(x_ref, gain_ref, w_ref, *refs):
    parts, (own_ref, low_ref, res_ref, all_ref, att, total) = refs[:8], refs[8:14]
    line = LineGather(own_ref, all_ref, *refs[14:])
    step, steps = pl.program_id(0) * pl.num_programs(1) + pl.program_id(1), 8
    pl.when(step == 0)(lambda: greet(line=True))
    line.ride(step, steps)
    width = w_ref.shape[-1]
    shape = low_ref.shape

    def columns(index):
        return pl.ds(pl.multiple_of(flipped(lax.axis_index("ctx"), index) * width, width), width)

    for index, part in enumerate(parts):
        att[:, columns(index)] = part[...].reshape(-1, width)
    attended = att[...]
    for index in range(8):
        total[:, columns(index)] = dot(attended, w_ref[index % 2, :, index // 2].reshape(-1, width))
    residual = total[...] + x_ref[...].reshape(attended.shape).astype(f32)
    res_ref[...] = residual.reshape(shape)
    low_ref[...] = (residual * rms_scale(residual) * gain_ref[...]).astype(bf16).reshape(shape)
    pl.when(step == steps - 1)(line.finish)


def gathered_residuals(x, attended, gain, out_blocks, own, identity):
    _, s, q, r, d = x.shape
    width = attended.shape[-1]
    tile = pl.BlockSpec((1, s, 1, r, d), lambda p, t: (p, 0, t, 0, 0))

    def sent(index):
        odd, other = index % 2, index // 2
        return pl.BlockSpec(
            (1, 1, 1, s, 1, r, width),
            lambda p, t: (odd, (p + odd) % 2, other, 0, flipped(t, other), 0, 0),
        )

    def fixed(shape):
        return pl.BlockSpec(shape, lambda p, t: (0,) * len(shape), pipeline_mode=pl.Buffered(1))

    return pl.pallas_call(
        gathered_residual_kernel,
        grid=(2, q),
        in_specs=[tile, fixed((1, d)), fixed(out_blocks.shape)]
        + [sent(i) for i in range(8)]
        + [STAGED],
        out_specs=[tile, tile, ANYWHERE],
        out_shape=[
            jax.ShapeDtypeStruct(x.shape, bf16),
            jax.ShapeDtypeStruct(x.shape, f32),
            line_shape(own),
        ],
        scratch_shapes=[
            pltpu.VMEM((s * r, d), bf16),
            pltpu.VMEM((s * r, d), f32),
            *LineGather.SEMAPHORES,
        ],
        compiler_params=talking(identity),
        cost_estimate=pl.CostEstimate(
            flops=2 * x.size * d, bytes_accessed=10 * x.size, transcendentals=0
        ),
    )(x, gain.reshape(1, d), out_blocks, *[attended] * 8, own)


def hidden_kernel(skipped, low_ref, cot_ref, w_gate, w_up, w_down, *refs):
    hidden_ref, gate_ref, up_ref = refs[skipped:]
    low = low_ref[...]
    gate, upward = dot(low, w_gate[...]), dot(low, w_up[...])
    grad_hidden = dot(cot_ref[...], w_down[...])
    sigmoid = jax.nn.sigmoid(gate)
    hidden_ref[...] = (gate * sigmoid * upward).astype(bf16)
    gate_ref[...] = (grad_hidden * upward * sigmoid * (1.0 + gate * (1.0 - sigmoid))).astype(bf16)
    up_ref[...] = (grad_hidden * gate * sigmoid).astype(bf16)


def block_specs(weights):
    return [
        pl.BlockSpec((array.shape[0], width), lambda i, pick=pick: (0, pick), pipeline_mode=pl.Buffered(1))
        for array, width, pick in weights
    ]


def arrays(weights):
    return [array for array, _, _ in weights]


def hidden_part(second_low, cot, weights, earlier=()):
    tokens, d = second_low.shape
    step = weights[0][1]
    tile = min(512, tokens)
    return pl.pallas_call(
        functools.partial(hidden_kernel, len(earlier)),
        grid=(tokens // tile,),
        in_specs=[tile_spec(tile, d)] * 2 + block_specs(weights) + [ANYWHERE] * len(earlier),
        out_specs=[tile_spec(tile, step)] * 3,
        out_shape=[jax.ShapeDtypeStruct((tokens, step), bf16)] * 3,
        compiler_params=PARAMS,
        cost_estimate=pl.CostEstimate(
            flops=6 * tokens * d * step, bytes_accessed=4 * tokens * d, transcendentals=tokens * step
        ),
    )(second_low, cot, *arrays(weights), *earlier)


def back_kernel(count, *refs):
    lefts, weights = refs[:count], refs[count : 2 * count]
    total = None
    for left, weight in zip(lefts, weights):
        part = dot_rows(left[...], weight[...])
        total = part if total is None else total + part
    refs[2 * count][...] = total.astype(bf16)


def taken(weights):
    return [
        (array, width, pick)
        if width % 128 == 0
        else (lax.slice_in_dim(array, pick * width, (pick + 1) * width, axis=1), width, 0)
        for array, width, pick in weights
    ]


def back(lefts, weights, first, tokens):
    d = weights[0][0].shape[0]
    tile = min(256, tokens)
    start = first // tile
    weights = taken(weights)
    return pl.pallas_call(
        functools.partial(back_kernel, len(lefts)),
        grid=(tokens // tile,),
        in_specs=[pl.BlockSpec((tile, left.shape[1]), lambda i: (i + start, 0)) for left in lefts]
        + block_specs(weights),
        out_specs=tile_spec(tile, d),
        out_shape=jax.ShapeDtypeStruct((tokens, d), bf16),
        compiler_params=PARAMS,
        cost_estimate=pl.CostEstimate(
            flops=2 * tokens * d * sum(left.shape[1] for left in lefts),
            bytes_accessed=4 * tokens * d,
            transcendentals=0,
        ),
    )(*lefts, *arrays(weights))


FAR, BY_X, BY_Y, OWN = 3, 1, 2, 0
TURNS = ((1, FAR), (1, BY_X), (0, FAR), (1, BY_Y), (0, BY_X), (1, OWN), (0, BY_Y), (0, OWN))
PARITIES = sum(p << t for t, (p, _) in enumerate(TURNS))
PLACES = sum(q << (2 * t) for t, (_, q) in enumerate(TURNS))


def norm_back(grad, x, base, gain):
    scale = rms_scale(x)
    weighted = gain * grad
    mean = jnp.mean(weighted * x, axis=-1, keepdims=True)
    return base + scale * weighted - x * (scale * scale * scale) * mean, grad * x * scale


def back_scatter_kernel(count, skipped, riding, *refs):
    lefts, weights, refs = refs[:count], refs[count : 2 * count], refs[2 * count + skipped :]
    laid, refs = refs[:riding], refs[riding:]
    based = len(refs) - riding - (15 if riding else 11) == 6
    base_ref, refs = (refs[0], refs[1:]) if based else (None, refs)
    x_ref, gain_ref, grad_ref, low_ref, sum_ref = refs[:5]
    lines, refs = refs[5 : 5 + riding], refs[5 + riding :]
    given, got, sums, own, far, from_x, from_y, send_odd, came_odd, sent, came = refs[:11]
    lines = [LineSum(laid[0], 0, out, *refs[11:]) for out in lines]
    sibling, by_x, by_y = neighbours()
    greet(line=riding > 0)
    for line in lines:
        line.send()
    s, r, d = own.shape
    half = s // 2

    def move(partner, source, target, send_sem, recv_sem):
        return pltpu.make_async_remote_copy(
            src_ref=source,
            dst_ref=target,
            send_sem=send_sem,
            recv_sem=recv_sem,
            device_id={"ctx": partner},
            device_id_type=MESH,
        )

    def odd_copy(q):
        return move(sibling, given.at[q], got.at[q], send_odd.at[q], came_odd.at[q])

    low_half, high_half = pl.ds(0, half), pl.ds(half, half)
    far_x = move(by_x, sums.at[FAR, low_half], far.at[low_half], sent.at[0], came.at[0])
    far_y = move(by_y, sums.at[FAR, high_half], far.at[high_half], sent.at[1], came.at[1])
    first_x = move(by_x, sums.at[BY_X, low_half], from_x.at[low_half], sent.at[2], came.at[2])
    first_y = move(by_y, sums.at[BY_Y, high_half], from_y.at[high_half], sent.at[3], came.at[3])
    last_x = move(by_x, sums.at[BY_X, high_half], from_x.at[high_half], sent.at[4], came.at[4])
    last_y = move(by_y, sums.at[BY_Y, low_half], from_y.at[low_half], sent.at[5], came.at[5])

    def turn(t, _):
        p = lax.shift_right_logical(jnp.int32(PARITIES), t) % 2
        q = lax.shift_right_logical(jnp.int32(PLACES), 2 * t) % 4
        total = None
        for left, weight in zip(lefts, weights):
            width = left.shape[-1]
            part = dot_rows(left[p, :, q].reshape(s * r, width), weight[...])
            total = part if total is None else total + part
        total = total.reshape(s, r, d)

        @pl.when(p == 1)
        def _():
            given[q] = total.astype(bf16)
            odd_copy(q).start()

        @pl.when(p == 0)
        def _():
            odd_copy(q).wait_recv()
            both = total + got[q].astype(f32)

            @pl.when(q == OWN)
            def _():
                own[...] = both

            @pl.when(q != OWN)
            def _():
                sums[q] = both.astype(bf16)

            @pl.when(q == FAR)
            def _():
                far_x.start()
                far_y.start()

            @pl.when(q == BY_X)
            def _():
                first_x.start()

            @pl.when(q == BY_Y)
            def _():
                first_y.start()

        return 0

    lax.fori_loop(0, len(TURNS), turn, 0)
    for line in lines:
        line.pass_on()
    far_x.wait_recv()
    sums[BY_Y, low_half] = (sums[BY_Y, low_half].astype(f32) + far[low_half].astype(f32)).astype(bf16)
    last_y.start()
    far_y.wait_recv()
    sums[BY_X, high_half] = (sums[BY_X, high_half].astype(f32) + far[high_half].astype(f32)).astype(bf16)
    last_x.start()
    first_x.wait_recv()
    first_y.wait_recv()
    own[low_half] += from_x[low_half].astype(f32)
    own[high_half] += from_y[high_half].astype(f32)
    last_y.wait_recv()
    own[low_half] += from_y[low_half].astype(f32)
    last_x.wait_recv()
    own[high_half] += from_x[high_half].astype(f32)

    sum_ref[...] = jnp.zeros_like(sum_ref)
    slab = min(32, r)

    def finish(index, _):
        at = (index // (r // slab), pl.ds(pl.multiple_of((index % (r // slab)) * slab, slab), slab))
        base = base_ref[at].astype(f32) if based else 0.0
        grad, terms = norm_back(own[at], x_ref[at].astype(f32), base, gain_ref[...])
        grad_ref[at] = grad
        low_ref[at] = grad.astype(bf16)
        sum_ref[...] += jnp.sum(terms, axis=0, keepdims=True)
        return 0

    lax.fori_loop(0, s * (r // slab), finish, 0)
    for line in lines:
        line.finish()
    for copy in (far_x, far_y, first_x, first_y, last_x, last_y):
        copy.wait_send()
    for q in range(4):
        odd_copy(q).wait_send()


def back_scatter(lefts, weights, shape, identity, x, base, gain, earlier=(), last=False, laid=None):
    s, q, r, d = shape
    width = sum(left.shape[-1] for left in lefts)
    weights = taken(weights)
    lefts = [left.reshape(2, s, q, r, left.shape[-1]) for left in lefts]

    def fixed(whole):
        return pl.BlockSpec(whole, lambda i: (0,) * len(whole), pipeline_mode=pl.Buffered(1))

    operands = [*lefts, *arrays(weights), *earlier]
    in_specs = [fixed(left.shape) for left in lefts] + block_specs(weights)
    in_specs += [ANYWHERE] * len(earlier)
    riding = laid is not None
    based = base is not None
    operands += [laid] * riding + [base] * based + [x, gain.reshape(1, d)]
    in_specs += [ANYWHERE] * riding + [fixed((s, r, d))] * (1 + based) + [fixed((1, d))]
    out_specs = [fixed((s, r, d)), fixed((s, r, d)), fixed((1, d))]
    out_shape = [
        jax.ShapeDtypeStruct((s, r, d), f32),
        jax.ShapeDtypeStruct((s, r, d), bf16),
        jax.ShapeDtypeStruct((1, d), f32),
    ]
    line_scratch = []
    if riding:
        part = (laid.shape[1], laid.shape[2], laid.shape[3] // 2)
        out_specs.append(fixed(part))
        out_shape.append(jax.ShapeDtypeStruct(part, bf16))
        line_scratch = LineSum.scratch(laid.shape, part[2])
    dma = pltpu.SemaphoreType.DMA
    return pl.pallas_call(
        functools.partial(back_scatter_kernel, len(lefts), len(earlier), int(riding)),
        grid=(1,),
        in_specs=in_specs,
        out_specs=out_specs,
        out_shape=out_shape,
        scratch_shapes=[
            pltpu.VMEM((4, s, r, d), bf16),
            pltpu.VMEM((4, s, r, d), bf16),
            pltpu.VMEM((4, s, r, d), bf16),
            pltpu.VMEM((s, r, d), f32),
            pltpu.VMEM((s, r, d), bf16),
            pltpu.VMEM((s, r, d), bf16),
            pltpu.VMEM((s, r, d), bf16),
            dma((4,)),
            dma((4,)),
            dma((6,)),
            dma((6,)),
            *line_scratch,
        ],
        compiler_params=talking(identity),
        cost_estimate=pl.CostEstimate(
            flops=1 if last else 16 * s * r * d * width,
            bytes_accessed=1 if last else 16 * s * r * d,
            transcendentals=0,
            remote_bytes_transferred=1 if last else 14 * s * r * d,
        ),
    )(*operands)


def weighted_sums_kernel(counts, *refs):
    inputs = sum(counts) + len(counts)
    weight_ref, (out_ref, sum_ref) = refs[inputs], refs[-2:]
    sum_ref[...] = jnp.zeros_like(sum_ref)
    token_sums_kernel(counts, *refs[:inputs], out_ref, weighted=(weight_ref, sum_ref))


def token_sums_kernel(counts, *refs, weighted=None):
    out_ref = refs[-1]
    start = 0
    for count in counts:
        left, rights, refs = refs[0], refs[1 : 1 + count], refs[1 + count :]
        for right in rights:
            width = right.shape[1]
            part = dot_tokens(left[...], right[...])
            if weighted is not None:
                weight = weighted[0][:, start : start + width].astype(f32)
                weighted[1][...] += jnp.sum(part * weight, axis=1, keepdims=True)
            part = part.astype(bf16)
            groups, owners, rows, _ = out_ref.shape
            part = part.reshape(owners, groups, rows, width)
            for owner in range(owners):
                out_ref[:, owner, :, start : start + width] = part[owner]
            start += width


def token_sums(pairs, n, rows, earlier=(), weight=None):
    groups = pairs[0][0].shape[1] // (n * rows)
    operands, in_specs, width = [], [], 0
    for left, rights in pairs:
        operands += [left, *rights]
        in_specs.append(pl.BlockSpec((left.shape[0], 2 * groups * rows), lambda i: (0, i)))
        in_specs += [whole_spec(right.shape) for right in rights]
        width += sum(right.shape[1] for right in rights)
    tokens, d = pairs[0][0].shape
    out_specs = [pl.BlockSpec((groups, 2, rows, width), lambda i: (0, i, 0, 0))]
    out_shape = [jax.ShapeDtypeStruct((groups, n, rows, width), bf16)]
    if weight is not None:
        side = 2 * groups * rows
        operands.append(weight)
        in_specs.append(pl.BlockSpec((side, width), lambda i: (i, 0)))
        out_specs.append(pl.BlockSpec((side, 1), lambda i: (i, 0)))
        out_shape.append(jax.ShapeDtypeStruct((d, 1), f32))
    return pl.pallas_call(
        functools.partial(
            token_sums_kernel if weight is None else weighted_sums_kernel, [len(rights) for _, rights in pairs]
        ),
        grid=(n // 2,),
        in_specs=in_specs + [ANYWHERE] * len(earlier),
        out_specs=out_specs,
        out_shape=out_shape,
        compiler_params=PARAMS,
        cost_estimate=pl.CostEstimate(
            flops=2 * tokens * d * width, bytes_accessed=4 * tokens * d, transcendentals=0
        ),
    )(*operands, *earlier)


def output_back_kernel(low_ref, att_ref, w_ref, *refs):
    grad_ref, sum_ref, total = refs[-3:]

    @pl.when(pl.program_id(0) == 0)
    def _():
        total[...] = jnp.zeros_like(total)

    low = low_ref[...]
    grad_ref[...] = dot_rows(low, w_ref[...]).astype(bf16)
    total[...] += dot_tokens(att_ref[...], low)

    @pl.when(pl.program_id(0) == pl.num_programs(0) - 1)
    def _():
        groups, n, rows, width = sum_ref.shape
        for group in range(groups):
            for c in range(n):
                part = total[group * rows : (group + 1) * rows, c * width : (c + 1) * width]
                sum_ref[group, c] = part.astype(bf16)


def output_back(grad_low, attended_low, out_rows, n, rows, earlier=()):
    tokens, d = grad_low.shape
    lanes = attended_low.shape[1]
    sums = (lanes // rows, n, rows, d // n)
    tile = min(512, tokens)
    return pl.pallas_call(
        output_back_kernel,
        grid=(tokens // tile,),
        in_specs=[tile_spec(tile, d), tile_spec(tile, lanes), whole_spec((lanes, d))]
        + [ANYWHERE] * len(earlier),
        out_specs=[tile_spec(tile, lanes), pl.BlockSpec(sums, lambda i: (0, 0, 0, 0))],
        out_shape=[
            jax.ShapeDtypeStruct((tokens, lanes), bf16),
            jax.ShapeDtypeStruct(sums, bf16),
        ],
        scratch_shapes=[pltpu.VMEM((lanes, d), f32)],
        compiler_params=PARAMS,
        cost_estimate=pl.CostEstimate(
            flops=4 * tokens * d * lanes, bytes_accessed=2 * tokens * d, transcendentals=0
        ),
    )(grad_low, attended_low, out_rows, *earlier)


def gather_and_sum_kernel(hiddens, skipped, low_ref, gate_ref, up_ref, cot_ref, *refs):
    lefts, weights = refs[:hiddens], refs[hiddens : 2 * hiddens]
    refs = refs[2 * hiddens :]
    own_ref, refs = refs[0], refs[1 + skipped :]
    sum_ref, out_ref, all_ref = refs[:3]
    gather = Gather(own_ref, all_ref, *refs[3:])
    step, steps = pl.program_id(0), 8
    pl.when(step == 0)(greet)
    gather.ride(step, steps)
    tile = lefts[0].shape[0] // steps
    token_sums_kernel([2, 1], low_ref, gate_ref, up_ref, cot_ref, lefts[-1], sum_ref)
    rows = pl.ds(pl.multiple_of(step * tile, tile), tile)
    total = None
    for left, weight in zip(lefts, weights):
        part = dot_rows(left[rows, :], weight[...])
        total = part if total is None else total + part
    out_ref[...] = total.astype(bf16)
    pl.when(step == steps - 1)(gather.finish)


def gather_and_sum(own, second_low, grads, cot, hiddens, weights, rows, identity, earlier=()):
    tokens, d = second_low.shape
    step = hiddens[0].shape[1]
    groups = d // (8 * rows)
    column = pl.BlockSpec((tokens, groups * rows), lambda i: (0, i))
    return pl.pallas_call(
        functools.partial(gather_and_sum_kernel, len(hiddens), len(earlier)),
        grid=(8,),
        in_specs=[column, whole_spec(grads[0].shape), whole_spec(grads[1].shape), column]
        + [whole_spec(hidden.shape) for hidden in hiddens]
        + block_specs(weights)
        + [STAGED]
        + [ANYWHERE] * len(earlier),
        out_specs=[
            pl.BlockSpec((groups, 1, rows, 3 * step), lambda i: (0, i, 0, 0)),
            tile_spec(tokens // 8, d),
            ANYWHERE,
        ],
        out_shape=[
            jax.ShapeDtypeStruct((groups, 8, rows, 3 * step), bf16),
            jax.ShapeDtypeStruct((tokens, d), bf16),
            gathered_shape(own),
        ],
        scratch_shapes=list(Gather.SEMAPHORES),
        compiler_params=talking(identity),
        cost_estimate=pl.CostEstimate(
            flops=14 * tokens * d * step, bytes_accessed=12 * tokens * d, transcendentals=0
        ),
    )(second_low, *grads, cot, *hiddens, *arrays(weights), own, *earlier)


def spread_kernel(count, *refs):
    parts, out_ref, last_ref = refs[:count], refs[count], refs[count + 1]
    senders, _, width = parts[0].shape

    def write(target):
        for sender in range(senders):
            for index, part in enumerate(parts):
                start = (sender * count + index) * width
                target[:, start : start + width] = part[sender].astype(f32)

    pl.when(pl.program_id(0) < 2)(lambda: write(out_ref))
    pl.when(pl.program_id(0) == 2)(lambda: write(last_ref))


def spread(parts, width):
    n, rows, _ = parts[0][0].shape
    count = len(parts)
    pair = min(n, 4)
    wide = pair * count * width
    turns = n // pair
    return pl.pallas_call(
        functools.partial(spread_kernel, count),
        grid=(3, turns),
        in_specs=[
            pl.BlockSpec((pair, rows, width), lambda third, i, place=place: (i, 0, 3 * place + third))
            for _, place in parts
        ],
        out_specs=[
            pl.BlockSpec((rows, wide), lambda third, i: (0, jnp.minimum(third * turns + i, 2 * turns - 1))),
            pl.BlockSpec((rows, wide), lambda third, i: (0, jnp.maximum(third - 1, 0) * i)),
        ],
        out_shape=[
            jax.ShapeDtypeStruct((rows, 2 * n * count * width), f32),
            jax.ShapeDtypeStruct((rows, n * count * width), f32),
        ],
        compiler_params=PARAMS,
        cost_estimate=pl.CostEstimate(
            flops=0, bytes_accessed=18 * n * rows * count * width, transcendentals=0
        ),
    )(*[whole for whole, _ in parts])


def spread_all_kernel(part_ref, _, out_ref):
    senders, _, width = part_ref.shape
    for sender in range(senders):
        out_ref[:, sender * width : (sender + 1) * width] = part_ref[sender].astype(f32)


def spread_all(part, width, earlier):
    n, rows, _ = part.shape
    return pl.pallas_call(
        spread_all_kernel,
        grid=(3,),
        in_specs=[pl.BlockSpec((n, rows, width), lambda i: (0, 0, i)), ANYWHERE],
        out_specs=pl.BlockSpec((rows, n * width), lambda i: (0, i)),
        out_shape=jax.ShapeDtypeStruct((rows, 3 * n * width), f32),
        compiler_params=PARAMS,
        cost_estimate=pl.CostEstimate(
            flops=0, bytes_accessed=18 * n * rows * width, transcendentals=0
        ),
    )(part, earlier)


class PlaneSum:
    @staticmethod
    def scratch(shape):
        _, s, q, r, d = shape
        dma = pltpu.SemaphoreType.DMA
        block = pltpu.VMEM((s, r, d), bf16)
        blocks = pltpu.VMEM((q, s, r, d), bf16)
        return [blocks, blocks, block, block, block, dma((4,)), dma((4,)), dma((4,)), dma((6,)), dma((6,))]

    def __init__(self, parts, out, held, got, far, from_x, from_y, local, send_odd, came_odd, sent, came):
        self.out, self.held, self.got = out, held, got
        self.far, self.from_x, self.from_y = far, from_x, from_y
        sibling, by_x, by_y = neighbours()
        half = far.shape[0] // 2
        self.low, self.high = low, high = pl.ds(0, half), pl.ds(half, half)

        def move(partner, source, target, send_sem, recv_sem):
            return pltpu.make_async_remote_copy(
                src_ref=source,
                dst_ref=target,
                send_sem=send_sem,
                recv_sem=recv_sem,
                device_id={"ctx": partner},
                device_id_type=MESH,
            )

        self.loads = [pltpu.make_async_copy(parts.at[0, :, q], held.at[q], local.at[q]) for q in range(4)]
        self.odd = [
            move(sibling, parts.at[1, :, q], got.at[q], send_odd.at[q], came_odd.at[q]) for q in range(4)
        ]
        routes = [
            (by_x, held.at[FAR, low], far.at[low]),
            (by_y, held.at[FAR, high], far.at[high]),
            (by_x, held.at[BY_X, low], from_x.at[low]),
            (by_y, held.at[BY_Y, high], from_y.at[high]),
            (by_x, held.at[BY_X, high], from_x.at[high]),
            (by_y, held.at[BY_Y, low], from_y.at[low]),
        ]
        self.copies = [
            move(partner, source, target, sent.at[index], came.at[index])
            for index, (partner, source, target) in enumerate(routes)
        ]

    def send(self):
        for q in (FAR, BY_X, BY_Y, OWN):
            self.odd[q].start()
            self.loads[q].start()

    def join(self, q):
        self.loads[q].wait()
        self.odd[q].wait_recv()
        self.held[q] = (self.held[q].astype(f32) + self.got[q].astype(f32)).astype(bf16)

    def send_far(self):
        self.join(FAR)
        self.copies[0].start()
        self.copies[1].start()

    def send_first(self):
        self.join(BY_X)
        self.copies[2].start()
        self.join(BY_Y)
        self.copies[3].start()
        self.join(OWN)

    def send_last(self):
        for arrived, q, part, copy in ((1, BY_X, self.high, 4), (0, BY_Y, self.low, 5)):
            self.copies[arrived].wait_recv()
            added = self.held[q, part].astype(f32) + self.far[part].astype(f32)
            self.held[q, part] = added.astype(bf16)
            self.copies[copy].start()

    def finish(self):
        for copy in self.copies[2:]:
            copy.wait_recv()
        for copy in (*self.copies, *self.odd):
            copy.wait_send()
        total = self.held[OWN].astype(f32) + self.from_x[...].astype(f32) + self.from_y[...].astype(f32)
        self.out[...] = total

    def ride(self, step, steps):
        turns = (0, self.send), (steps // 8, self.send_far), (steps // 4, self.send_first)
        for turn, phase in (*turns, (steps // 2, self.send_last)):
            pl.when(step == turn)(phase)


def only(values, head, heads):
    if heads == 1:
        return values
    lane = lax.broadcasted_iota(jnp.int32, values.shape, 1)
    inside = (lane >= head * HEAD_SIZE) & (lane < (head + 1) * HEAD_SIZE)
    return jnp.where(inside, values, jnp.zeros_like(values))


def forward_kernel(heads, q_spot, k_spot, q_ref, k_ref, v_ref, *refs):
    if len(refs) > 2:
        own_ref, line_ref, low_ref, total_ref, all_ref, line_all_ref = refs[:6]
        gather = Gather(own_ref, all_ref, *refs[6:9])
        line = LineGather(line_ref, line_all_ref, *refs[9:])
        steps = pl.num_programs(0) * pl.num_programs(1) * pl.num_programs(2)
        step = (pl.program_id(0) * pl.num_programs(1) + pl.program_id(1)) * pl.num_programs(2)
        step += pl.program_id(2)
        pl.when(step == 0)(lambda: greet(line=True))
        gather.ride(step, steps)
        line.ride(step, steps)
    else:
        low_ref, total_ref = refs
    lanes = q_ref.shape[-1]
    queries = q_ref[0, 0] * bf16(HEAD_SIZE**-0.5)
    keys = k_ref[:, 0].reshape(-1, lanes)
    values = v_ref[:, 0].reshape(-1, lanes)
    allowed = k_spot[0] <= q_spot[0, 0]
    attended = jnp.zeros(queries.shape, f32)
    for head in range(heads):
        scores = dot_rows(keys, only(queries, head, heads))
        scores = jnp.where(allowed, scores, -1e30)
        highest = jnp.max(scores, axis=0, keepdims=True)
        raised = jnp.exp(scores - highest)
        summed = jnp.sum(raised, axis=0, keepdims=True)
        probs = (raised * (1.0 / summed)).astype(bf16)
        total_ref[0, 0, head : head + 1, :] = highest + jnp.log(summed)
        attended += dot_tokens(probs, only(values, head, heads))
    low_ref[0, 0] = attended.astype(bf16)
    if len(refs) > 2:
        pl.when(step == steps - 1)(line.finish)
        pl.when(step == steps - 1)(gather.finish)


def backward_kernel(
    heads, q_spot, k_spot, q_ref, k_ref, v_ref, grad_ref, total_ref, qc_ref, qs_ref, kc_ref, ks_ref, *refs
):
    if len(refs) > 5:
        parts, laid, dq_ref, dk_ref, dv_ref, out_ref, line_ref, dk_sum, dv_sum = refs[:9]
        summing = PlaneSum(parts, out_ref, *refs[9:-4])
        line = LineSum(laid, laid.shape[-1] // 2, line_ref, *refs[-4:])
    else:
        dq_ref, dk_ref, dv_ref, dk_sum, dv_sum = refs
    lanes = q_ref.shape[-1]
    scale = HEAD_SIZE**-0.5
    step = pl.program_id(1) * pl.num_programs(2) + pl.program_id(2)
    if len(refs) > 5:
        turn = pl.program_id(0) * pl.num_programs(1) * pl.num_programs(2) + step
        turns = pl.num_programs(0) * pl.num_programs(1) * pl.num_programs(2)
        pl.when(turn == 0)(lambda: greet(line=True))
        summing.ride(turn, turns)
        pl.when(turn == 0)(line.send)
        pl.when(turn == turns // 2)(line.pass_on)

    @pl.when(step == 0)
    def _():
        dk_sum[...] = jnp.zeros_like(dk_sum)
        dv_sum[...] = jnp.zeros_like(dv_sum)

    queries = q_ref[0, 0] * bf16(scale)
    grads = grad_ref[0, 0]
    keys = k_ref[:, 0].reshape(-1, lanes)
    values = v_ref[:, 0].reshape(-1, lanes)
    allowed = k_spot[0] <= q_spot[0, 0]
    grad_q = jnp.zeros(queries.shape, f32)
    for head in range(heads):
        query = only(queries, head, heads)
        grad = only(grads, head, heads)
        scores = jnp.where(allowed, dot_rows(keys, query), -1e30)
        probs = jnp.exp(scores - total_ref[0, 0, head : head + 1, :])
        dv_sum[...] += dot(probs.astype(bf16), grad)
        weighted = probs * dot_rows(values, grad)
        delta = jnp.sum(weighted, axis=0, keepdims=True)
        grad_scores = (weighted - probs * delta).astype(bf16)
        dk_sum[...] += dot(grad_scores, query)
        grad_q += dot_tokens(grad_scores, only(keys, head, heads))
    dq_ref[0, 0] = rotate_back(grad_q * scale, qc_ref[0, 0], qs_ref[0, 0]).astype(bf16)

    @pl.when(step == pl.num_programs(1) * pl.num_programs(2) - 1)
    def _():
        shape = (dk_ref.shape[0],) + dk_ref.shape[2:]
        cosine = kc_ref[:, 0].reshape(-1, lanes)
        sine = ks_ref[:, 0].reshape(-1, lanes)
        dk_ref[:, 0] = rotate_back(dk_sum[...], cosine, sine).astype(bf16).reshape(shape)
        dv_ref[:, 0] = dv_sum[...].astype(bf16).reshape(shape)

    if len(refs) > 5:
        pl.when(turn == turns - 1)(summing.finish)
        pl.when(turn == turns - 1)(line.finish)


def attention_specs(shape, heads):
    p, s, rows, lanes = shape
    tile = min(256, rows)
    one = pl.BlockSpec((1, 1, tile, lanes), lambda i, j, t: (j, i, t, 0))
    side = pl.BlockSpec((p, 1, rows, lanes), lambda i, j, t: (0, i, 0, 0))
    stat = pl.BlockSpec((1, 1, heads, tile), lambda i, j, t: (j, i, 0, t))
    q_spot = pl.BlockSpec((1, 1, 1, tile), lambda i, j, t: (j, i, 0, t))
    k_spot = pl.BlockSpec((1, p * rows, 1), lambda i, j, t: (i, 0, 0))
    return (s, p, rows // tile), one, side, stat, q_spot, k_spot


def attend(q_spot, k_spot, queries, keys, values, own=None, line=None, identity=None):
    p, s, rows, lanes = queries.shape
    heads = lanes // HEAD_SIZE
    grid, one, side, stat, q_spec, k_spec = attention_specs(queries.shape, heads)
    pairs = p * rows * s * p * rows
    out_shape = [
        jax.ShapeDtypeStruct(queries.shape, bf16),
        jax.ShapeDtypeStruct((p, s, heads, rows), f32),
    ]
    riding = own is not None
    return pl.pallas_call(
        functools.partial(forward_kernel, heads),
        grid=grid,
        in_specs=[q_spec, k_spec, one, side, side] + [STAGED] * (2 * riding),
        out_specs=[one, stat] + [ANYWHERE] * (2 * riding),
        out_shape=out_shape + ([gathered_shape(own), line_shape(line)] if riding else []),
        scratch_shapes=[*Gather.SEMAPHORES, *LineGather.SEMAPHORES] if riding else [],
        compiler_params=talking(identity) if riding else PARAMS,
        cost_estimate=pl.CostEstimate(
            flops=pairs * heads * 2048, bytes_accessed=queries.size * 14, transcendentals=pairs * heads
        ),
    )(q_spot, k_spot, queries, keys, values, *([own, line] if riding else []))


def attend_back(
    q_spot, k_spot, queries, keys, values, grads, totals, cosine, sine, parts=None, laid=None, identity=None
):
    p, s, rows, lanes = queries.shape
    heads = lanes // HEAD_SIZE
    grid, one, side, stat, q_spec, k_spec = attention_specs(queries.shape, heads)
    pairs = p * rows * s * p * rows
    in_specs = [q_spec, k_spec, one, side, side, one, stat, one, one, side, side]
    out_specs = [one, side, side]
    out_shape = [jax.ShapeDtypeStruct(queries.shape, bf16)] * 3
    scratch = [pltpu.VMEM((p * rows, lanes), f32)] * 2
    operands = [q_spot, k_spot, queries, keys, values, grads, totals, cosine, sine, cosine, sine]
    if parts is not None:
        own = (parts.shape[1], *parts.shape[3:])
        part = (*laid.shape[1:3], laid.shape[3] // 2)
        operands += [parts, laid]
        in_specs += [ANYWHERE] * 2
        for shape, kind in ((own, f32), (part, bf16)):
            out_specs.append(pl.BlockSpec(shape, lambda i, j, t: (0, 0, 0), pipeline_mode=pl.Buffered(1)))
            out_shape.append(jax.ShapeDtypeStruct(shape, kind))
        scratch += [*PlaneSum.scratch(parts.shape), *LineSum.scratch(laid.shape, part[2])]
    return pl.pallas_call(
        functools.partial(backward_kernel, heads),
        grid=grid,
        in_specs=in_specs,
        out_specs=out_specs,
        out_shape=out_shape,
        scratch_shapes=scratch,
        compiler_params=PARAMS if parts is None else talking(identity),
        cost_estimate=pl.CostEstimate(
            flops=pairs * heads * 5120, bytes_accessed=queries.size * 20, transcendentals=pairs * heads
        ),
    )(*operands)


def on_device(
    plane,
    inputs,
    positions,
    first_gain,
    attention_weight,
    output_weight,
    second_gain,
    gate_up_weight,
    down_weight,
    cotangent,
):
    s, r, d = inputs.shape
    n = plane.size
    ff = down_weight.shape[1]
    me = lax.axis_index("ctx")
    lanes = d // n
    mine = ff // n
    step = mine // CHUNKS
    tokens = s * r * n
    rows = d // (n * lax.axis_size("fsdp"))
    half = tokens // 2
    group = (2, s, n // 2 * r)
    blocks = (s, n // 2, r, d)

    def columns(weight, start, width):
        return lax.dynamic_slice_in_dim(weight, start, width, 1)

    qkv = jnp.concatenate(
        [columns(attention_weight, part * d + me * lanes, lanes) for part in range(3)], axis=1
    )
    out_own = columns(output_weight, me * lanes, lanes)
    if plane.relative:
        whole_inputs, cot, qkv, out_own = gather_in_plane([inputs, cotangent], [qkv, out_own], 1)
    else:
        whole_inputs, cot = plane.gather([inputs, cotangent])
        qkv, out_own = gather_rows(qkv), gather_rows(out_own)

    def chunk_parts(chunk, earlier):
        start = (me + zero_of(earlier)) * mine + chunk * step
        return [
            columns(gate_up_weight, start, step),
            columns(gate_up_weight, ff + start, step),
            columns(down_weight, start, step),
        ]

    ffn = {}
    for chunk in range(CHUNKS):
        if chunk != RIDING or not plane.relative:
            whole = gather_rows(jnp.concatenate(chunk_parts(chunk, qkv), axis=1))
            ffn[chunk] = [(whole, step, part) for part in range(3)]

    places = plane.order(positions.reshape(s, n, r)).reshape(group)
    q_spot = places[:, :, None, :]
    k_spot = places.transpose(1, 0, 2).reshape(s, n * r, 1)
    cosine, sine = rope_tables(places.reshape(tokens), lanes, whole_inputs)
    normed_low, queries, keys, values = project(
        whole_inputs.reshape(tokens, d), first_gain, cosine, sine, qkv
    )
    queries, keys, values, cosine, sine = (
        part.reshape(*group, lanes) for part in (queries, keys, values, cosine, sine)
    )
    if plane.relative:
        riders = chunk_parts(RIDING, qkv)
        attended_low, totals, out_blocks, gate = attend(
            q_spot, k_spot, queries, keys, values, out_own.reshape(2, d // 2, lanes), riders[0], 2
        )
        attended_whole, upward = gather_in_plane(
            [attended_low.reshape(2, half, lanes)], riders[1:2], 3
        )
        second_low, residual, down = gathered_residuals(
            whole_inputs,
            attended_whole.reshape(2, 2, 4, s, 4, r, lanes),
            second_gain,
            out_blocks,
            riders[2],
            4,
        )
        ffn[RIDING] = [(whole, step, 0) for whole in (gate, upward, down)]
        second_low = second_low.reshape(tokens, d)
        residual = residual[0, :, 0]
    else:
        attended_low, totals = attend(q_spot, k_spot, queries, keys, values)
        out_blocks = lax.all_gather(out_own, "ctx", axis=0, tiled=False)
        attended_whole = lax.all_gather(
            attended_low.reshape(tokens, lanes), "ctx", axis=1, tiled=True
        )
        second_low, residual = residuals(
            whole_inputs.reshape(tokens, d), attended_whole, second_gain, out_blocks
        )
        residual = lax.dynamic_index_in_dim(residual.reshape(2, *blocks), me % 2, 0, keepdims=False)
        residual = lax.dynamic_index_in_dim(residual, me // 2, 1, keepdims=False)
    cot = cot.reshape(tokens, d)
    attended_low = attended_low.reshape(tokens, lanes)

    if plane.relative:
        out_rows = lax.dynamic_slice(
            out_blocks, (0, me // 4, 0, (me % 4) * lanes, 0), (2, 1, 4, lanes, lanes)
        ).reshape(2, 2, 2, lanes, lanes)
        for axis, bit in ((0, 1), (1, 4), (2, 2)):
            out_rows = jnp.where((me & bit) != 0, jnp.flip(out_rows, axis), out_rows)
        out_rows = out_rows.transpose(3, 1, 2, 0, 4).reshape(lanes, d)
    else:
        out_rows = lax.dynamic_slice_in_dim(out_blocks, me * lanes, lanes, 1)
        out_rows = out_rows.transpose(1, 0, 2).reshape(lanes, d)

    def summed(pairs, earlier=(), weight=None):
        if plane.relative:
            return token_sums(pairs, n, rows, earlier, weight)
        partial = [dot_tokens(left, right) for left, rights in pairs for right in rights]
        partial = jnp.concatenate(partial, axis=1)
        laid = [by_owners(partial, n, rows)]
        return laid if weight is None else [*laid, jnp.sum(partial * weight, axis=1)]

    hiddens, grads, partials, sums = [], [], [], []
    for chunk in ORDER:
        hidden, *grad_gate_up = hidden_part(
            second_low, cot, taken(ffn[chunk]), partials[-1:] or [out_rows]
        )
        hiddens.append(hidden)
        grads.append(grad_gate_up)
        if len(hiddens) < CHUNKS or not plane.relative:
            partials += summed([(second_low, grad_gate_up), (cot, [hidden])])
            if len(hiddens) < CHUNKS - 1 or not plane.relative:
                sums.append(sum_rows(partials[-1]))

    def apart(lefts, weights):
        odd, even = back(lefts, weights, half, half), back(lefts, weights, 0, half)
        return plane.scatter(odd.reshape(blocks), even.reshape(blocks))

    def norm_step(identity, lefts, weights, x, base, gain, earlier, last=False, laid=None):
        if plane.relative:
            return back_scatter(lefts, weights, blocks, identity, x, base, gain, earlier, last, laid)
        base = 0.0 if base is None else base.astype(f32)
        grad, terms = norm_back(apart(lefts, weights), x.astype(f32), base, gain)
        return grad, grad.astype(bf16), jnp.sum(terms, axis=(0, 1))

    grad_residual, grad_residual_low, second_gain_part, *left_sums = norm_step(
        5,
        [grad for pair in grads for grad in pair],
        [weight for chunk in ORDER for weight in ffn[chunk][:2]],
        residual,
        cotangent,
        second_gain,
        partials[-1:],
        laid=partials[-1] if plane.relative else None,
    )
    downs = [ffn[chunk][2] for chunk in ORDER]
    if plane.relative:
        last, output_parts, grad_low = gather_and_sum(
            grad_residual_low,
            second_low,
            grads[-1],
            cot,
            hiddens,
            downs,
            rows,
            6,
            sums[:1],
        )
    else:
        last = partials[-1]
        sums.pop()
        (grad_low,) = plane.gather([grad_residual_low])
    grad_low = grad_low.reshape(tokens, d)

    grad_attended, out_part = output_back(
        grad_low, attended_low, out_rows, n, rows
    )
    last = sum_rows(last)
    early = to_owners(after(jnp.concatenate(sums[:2], axis=2), grad_attended))
    operands = (q_spot, k_spot, queries, keys, values, grad_attended.reshape(*group, lanes))
    operands += (totals, cosine, sine)
    if plane.relative:
        *grad_projected, output, right_sums = attend_back(
            *operands, output_parts.reshape(2, *blocks), partials[-1], 8
        )
        output = residual + output
        sums += [*left_sums, right_sums]
    else:
        grad_projected = attend_back(*operands)
        output = residual + apart(hiddens, downs)
    grad_projected = [part.reshape(tokens, lanes) for part in grad_projected]
    attention_parts, first_gain_part = summed([(normed_low, grad_projected)], [early], qkv)
    first_gain_part = first_gain_part.reshape(d) / first_gain
    attention_sums = sum_rows(attention_parts)
    grad_output_weight = sum_rows(after(out_part, attention_parts))
    grad_input, *_ = norm_step(
        7,
        grad_projected,
        [(qkv, lanes, part) for part in range(3)],
        inputs,
        None,
        first_gain,
        [attention_parts],
        True,
    )
    grad_input = grad_residual + grad_input
    gains = jnp.stack([first_gain_part, second_gain_part.reshape(d)]).astype(bf16)
    gains = gains.reshape(2, n, -1, rows).transpose(1, 3, 0, 2).reshape(n, rows, -1)
    count = gains.shape[-1]
    gains = jnp.pad(gains, ((0, 0), (0, 0), (0, 128 - count)))
    late = to_owners(jnp.concatenate([*sums[2:], last, gains], axis=2))
    gains = jnp.sum(late[:, :, -128 : count - 128].astype(f32), axis=0).reshape(rows, 2, -1)
    gains = line_total(gains)
    attention_sums = to_owners(after(attention_sums, grad_input))
    places = [ORDER.index(chunk) for chunk in range(CHUNKS)]
    sums = [(early, place) if place < 2 else (late, place - 2) for place in places]
    if plane.relative:
        grad_gate_up, grad_down = spread(sums, step)
        grad_attention = spread_all(attention_sums, lanes, grad_down)
    else:
        parts = [whole[:, :, 3 * step * place : 3 * step * (place + 1)] for whole, place in sums]
        whole = jnp.stack([part.reshape(n, rows, 3, step) for part in parts], axis=3)
        whole = whole.transpose(1, 2, 0, 3, 4).reshape(rows, 3, ff).astype(f32)
        grad_gate_up, grad_down = whole[:, :2].reshape(rows, 2 * ff), whole[:, 2]
        grad_attention = attention_sums.reshape(n, rows, 3, lanes).transpose(1, 2, 0, 3)
        grad_attention = grad_attention.reshape(rows, 3 * d).astype(f32)
    return (
        output,
        grad_input,
        grad_attention,
        after(grad_output_weight, grad_attention).transpose(1, 0, 2).reshape(rows, d).astype(f32),
        grad_gate_up,
        grad_down,
        gains[:, 0],
        gains[:, 1],
    )


def solution(mesh):
    plane = Plane(mesh.shape["ctx"])
    return jax.shard_map(
        functools.partial(on_device, plane),
        mesh=mesh,
        in_specs=(
            P("fsdp", "ctx", None),
            P("fsdp", None),
            P(),
            P("fsdp", None),
            P("fsdp", None),
            P(),
            P("fsdp", None),
            P("fsdp", None),
            P("fsdp", "ctx", None),
        ),
        out_specs=(
            P("fsdp", "ctx", None),
            P("fsdp", "ctx", None),
            P(("ctx", "fsdp"), None),
            P(("ctx", "fsdp"), None),
            P(("ctx", "fsdp"), None),
            P(("ctx", "fsdp"), None),
            P(("ctx", "fsdp")),
            P(("ctx", "fsdp")),
        ),
        check_vma=False,
    )
```

```python
import functools

import jax
import jax.numpy as jnp
from jax import lax
from jax.experimental import pallas as pl
from jax.experimental.pallas import tpu as pltpu
from jax.sharding import PartitionSpec as P

HEAD_SIZE = 64
EPSILON = 1e-05
ROPE_BASE = 130000.0
CHUNKS = 4
ORDER = (0, 3, 1, 2)
RIDING = 3

f32 = jnp.float32
bf16 = jnp.bfloat16


def rms_scale(values):
    return lax.rsqrt(jnp.mean(values * values, axis=-1, keepdims=True) + EPSILON)


def dot(left, right):
    return jnp.dot(left, right, preferred_element_type=f32)


def dot_rows(left, right):
    return lax.dot_general(left, right, (((1,), (1,)), ((), ())), preferred_element_type=f32)


def dot_tokens(left, right):
    return lax.dot_general(left, right, (((0,), (0,)), ((), ())), preferred_element_type=f32)


def tables_kernel(places_ref, _, cos_ref, sin_ref):
    half = HEAD_SIZE // 2
    width = cos_ref.shape[1]
    narrow = min(width, 128)
    lane = lax.broadcasted_iota(jnp.int32, (1, narrow), 1) % half
    inverse = jnp.exp(-(2.0 * lane.astype(f32) / HEAD_SIZE) * jnp.log(f32(ROPE_BASE)))
    angles = places_ref[...].astype(f32) * inverse
    cosine, sine = jnp.cos(angles), jnp.sin(angles)
    for start in range(0, width, narrow):
        cos_ref[:, start : start + narrow] = cosine
        sin_ref[:, start : start + narrow] = sine


def rope_tables(places, lanes, earlier):
    tokens = places.shape[0]
    tile = min(512, tokens)
    return pl.pallas_call(
        tables_kernel,
        grid=(tokens // tile,),
        in_specs=[pl.BlockSpec((tile, 1), lambda i: (i, 0)), ANYWHERE],
        out_specs=[pl.BlockSpec((tile, lanes), lambda i: (i, 0))] * 2,
        out_shape=[jax.ShapeDtypeStruct((tokens, lanes), f32)] * 2,
        cost_estimate=pl.CostEstimate(
            flops=100 * tokens * lanes, bytes_accessed=8 * tokens * lanes, transcendentals=0
        ),
    )(places.reshape(tokens, 1), earlier)


def other_half(values):
    half = HEAD_SIZE // 2
    lanes = values.shape[-1]
    if lanes == HEAD_SIZE:
        return jnp.concatenate([-values[:, half:], values[:, :half]], axis=1)
    lane = lax.broadcasted_iota(jnp.int32, values.shape, 1)
    return jnp.where(
        lane % HEAD_SIZE < half,
        -pltpu.roll(values, lanes - half, 1),
        pltpu.roll(values, half, 1),
    )


def rotate(values, cosine, sine):
    return values * cosine + other_half(values) * sine


def rotate_back(gradient, cosine, sine):
    return gradient * cosine - other_half(gradient * sine)


MESH = pl.DeviceIdType.MESH


def greet(line=False):
    barrier = pltpu.get_barrier_semaphore()
    partners = [{"ctx": partner} for partner in neighbours()]
    size = lax.axis_size("fsdp")
    if line:
        z = lax.axis_index("fsdp")
        partners += [{"fsdp": (z + shift) % size} for shift in range(1, size)]
    for partner in partners:
        pl.semaphore_signal(barrier, inc=1, device_id=partner, device_id_type=MESH)
    pl.semaphore_wait(barrier, len(partners))


def flipped(place, bits):
    for bit in (1, 2, 4):
        if bits & bit:
            place = place + bit - 2 * bit * ((place // bit) % 2)
    return place


def neighbours():
    me = lax.axis_index("ctx")
    return [flipped(me, bit) for bit in (1, 2, 4)]


class Gather:
    SEMAPHORES = (
        pltpu.SemaphoreType.DMA((2,)),
        pltpu.SemaphoreType.DMA((14,)),
        pltpu.SemaphoreType.DMA((14,)),
    )

    def __init__(self, own, out, local, sent, came):
        sibling, by_x, by_y = neighbours()
        routes = [
            (by_x, own.at[0], out.at[0, 0, 1]),
            (by_y, own.at[1], out.at[0, 1, 2]),
            (by_x, own.at[1], out.at[0, 1, 1]),
            (by_y, own.at[0], out.at[0, 0, 2]),
            (by_y, out.at[0, 0, 1], out.at[0, 0, 3]),
            (by_x, out.at[0, 1, 2], out.at[0, 1, 3]),
        ]
        for h in range(2):
            routes.append((sibling, own.at[h], out.at[1, h, 0]))
        for h, q in ((0, 1), (1, 2), (1, 1), (0, 2), (0, 3), (1, 3)):
            routes.append((sibling, out.at[0, h, q], out.at[1, h, q]))
        self.copies = [
            pltpu.make_async_remote_copy(
                src_ref=source,
                dst_ref=target,
                send_sem=sent.at[index],
                recv_sem=came.at[index],
                device_id={"ctx": partner},
                device_id_type=MESH,
            )
            for index, (partner, source, target) in enumerate(routes)
        ]
        self.kept = [
            pltpu.make_async_copy(own.at[h], out.at[0, h, 0], local.at[h]) for h in range(2)
        ]

    def send(self):
        for index in (0, 1, 2, 3, 6, 7):
            self.copies[index].start()
        for copy in self.kept:
            copy.start()

    def pass_on(self):
        self.copies[0].wait_recv()
        self.copies[4].start()
        self.copies[8].start()
        self.copies[1].wait_recv()
        self.copies[5].start()
        self.copies[9].start()

    def pass_seconds(self):
        self.copies[2].wait_recv()
        self.copies[10].start()
        self.copies[3].wait_recv()
        self.copies[11].start()

    def finish(self):
        self.copies[4].wait_recv()
        self.copies[12].start()
        self.copies[5].wait_recv()
        self.copies[13].start()
        for copy in self.copies[6:]:
            copy.wait_recv()
        for copy in self.copies:
            copy.wait_send()
        for copy in self.kept:
            copy.wait()

    def ride(self, step, steps):
        for turn, phase in ((0, self.send), (steps // 2, self.pass_on), (steps - 1, self.pass_seconds)):
            pl.when(step == turn)(phase)


class LineGather:
    SEMAPHORES = (
        pltpu.SemaphoreType.DMA((1,)),
        pltpu.SemaphoreType.DMA((3,)),
        pltpu.SemaphoreType.DMA((3,)),
    )

    def __init__(self, own, out, local, sent, came):
        z = lax.axis_index("fsdp")
        size = own.shape[0]

        def rows(place):
            return out.at[pl.ds(pl.multiple_of(place * size, size), size)]

        held = z // 2 + 2 * (z % 2)
        routes = [
            ((z + 1) % 4, own, rows(z)),
            ((z + 3) % 4, own, rows(z)),
            (2 * (1 - z % 2) + z // 2, rows(held), rows(held)),
        ]
        if lax.axis_size("fsdp") == 1:
            routes = []
        copies = [
            pltpu.make_async_remote_copy(
                src_ref=source,
                dst_ref=target,
                send_sem=sent.at[index],
                recv_sem=came.at[index],
                device_id={"fsdp": partner},
                device_id_type=MESH,
            )
            for index, (partner, source, target) in enumerate(routes)
        ]
        self.first, self.second = copies[:2], copies[2:]
        self.kept = pltpu.make_async_copy(own, rows(z), local.at[0])

    def send(self):
        for copy in (*self.first, self.kept):
            copy.start()

    def pass_on(self):
        for copy in self.first:
            copy.wait_recv()
        self.kept.wait()
        for copy in self.second:
            copy.start()

    def finish(self):
        for copy in self.second:
            copy.wait_recv()
        for copy in (*self.first, *self.second):
            copy.wait_send()

    def ride(self, step, steps):
        pl.when(step == 0)(self.send)
        pl.when(step == steps - 1)(self.pass_on)


def line_shape(own):
    return jax.ShapeDtypeStruct((lax.axis_size("fsdp") * own.shape[0], own.shape[1]), own.dtype)


class LineSum:
    @staticmethod
    def scratch(shape, width):
        _, n, rows, _ = shape
        return [
            pltpu.VMEM((6, n, rows, width), bf16),
            pltpu.SemaphoreType.DMA((3,)),
            pltpu.SemaphoreType.DMA((3,)),
            pltpu.SemaphoreType.DMA((3,)),
        ]

    def __init__(self, laid, first, out, held, local, sent, came):
        self.z = z = lax.axis_index("fsdp")
        self.size = lax.axis_size("fsdp")
        width = held.shape[-1]
        self.held, self.out = held, out

        def block(shift):
            return laid.at[(z + shift) % self.size, :, :, pl.ds(first, width)]

        def move(index, source, target, partner):
            return pltpu.make_async_remote_copy(
                src_ref=source,
                dst_ref=target,
                send_sem=sent.at[index],
                recv_sem=came.at[index],
                device_id={"fsdp": partner},
                device_id_type=MESH,
            )

        self.loads = [
            pltpu.make_async_copy(block(shift), held.at[index], local.at[index])
            for index, shift in enumerate((0, 1, 3))
        ]
        if self.size == 1:
            return
        self.far = move(0, block(2), held.at[3], 2 * (z % 2) + 1 - z // 2)
        self.up = move(1, held.at[1], held.at[4], (z + 1) % 4)
        self.down = move(2, held.at[2], held.at[5], (z + 3) % 4)

    def send(self):
        for load in self.loads:
            load.start()
        if self.size > 1:
            self.far.start()

    def pass_on(self):
        for load in self.loads:
            load.wait()
        if self.size > 1:
            self.far.wait_recv()
            for index, place, copy in ((1, 1, self.up), (2, 2, self.down)):

                @pl.when(self.z == place)
                def _():
                    added = self.held[index].astype(f32) + self.held[3].astype(f32)
                    self.held[index] = added.astype(bf16)

                copy.start()

    def finish(self):
        total = self.held[0].astype(f32)
        if self.size > 1:
            self.up.wait_recv()
            self.down.wait_recv()
            ends = jnp.where((self.z == 0) | (self.z == 3), 1.0, 0.0)
            total += self.held[4].astype(f32) + self.held[5].astype(f32)
            total += ends * self.held[3].astype(f32)
            for copy in (self.far, self.up, self.down):
                copy.wait_send()
        self.out[...] = total.astype(bf16)


def gathered_shape(own):
    return jax.ShapeDtypeStruct((2, 2, 4) + own.shape[1:], own.dtype)


ANYWHERE = pl.BlockSpec(memory_space=pl.ANY)
STAGED = pl.BlockSpec(memory_space=pltpu.VMEM)


def talking(identity):
    return pltpu.CompilerParams(
        collective_id=identity, has_side_effects=True, vmem_limit_bytes=56 * 1024 * 1024
    )


def gather_kernel(count, lines, *refs):
    sources, targets, refs = refs[: count + lines], refs[count + lines : 2 * (count + lines)], refs[2 * (count + lines) :]
    moves = [
        (Gather if i < count else LineGather)(sources[i], targets[i], *refs[3 * i : 3 * i + 3])
        for i in range(count + lines)
    ]
    gathers, lines = moves[:count], moves[count:]
    greet(line=True)
    gathers[0].send()
    for line in lines:
        line.send()
    gathers[0].pass_on()
    for gather in gathers[1:]:
        gather.send()
    gathers[0].pass_seconds()
    for line in lines:
        line.pass_on()
    gathers[0].finish()
    for gather in gathers[1:]:
        gather.pass_on()
        gather.pass_seconds()
        gather.finish()
    for line in lines:
        line.finish()


def gather_in_plane(owns, lines, identity):
    size = sum(own.size * own.dtype.itemsize for own in owns)
    count = len(owns) + len(lines)
    return pl.pallas_call(
        functools.partial(gather_kernel, len(owns), len(lines)),
        in_specs=[STAGED] * count,
        out_specs=[ANYWHERE] * count,
        out_shape=[gathered_shape(own) for own in owns] + [line_shape(own) for own in lines],
        scratch_shapes=list(Gather.SEMAPHORES) * len(owns) + list(LineGather.SEMAPHORES) * len(lines),
        compiler_params=talking(identity),
        cost_estimate=pl.CostEstimate(
            flops=0, bytes_accessed=16 * size, transcendentals=0, remote_bytes_transferred=7 * size
        ),
    )(*owns, *lines)


class Plane:
    def __init__(self, size):
        self.size = size
        self.relative = size == 8

    def swap(self, value, bits):
        return lax.ppermute(value, "ctx", [(i, i ^ bits) for i in range(self.size)])

    def gather(self, owns):
        wholes = [lax.all_gather(own, "ctx", axis=1, tiled=False) for own in owns]
        s, n, r, d = wholes[0].shape
        return [whole.reshape(s, n // 2, 2, r, d).transpose(2, 0, 1, 3, 4) for whole in wholes]

    def scatter(self, odd, even):
        if not self.relative:
            both = jnp.stack([even, odd], axis=2)
            s, q, p, r, d = both.shape
            return lax.psum_scatter(
                both.reshape(s, q * p, r, d), "ctx", scatter_dimension=1, tiled=False
            ).astype(f32)
        half = odd.shape[0] // 2
        came = self.swap(odd, 1)
        both = (even.astype(f32) + came.astype(f32)).astype(bf16)
        far_x, far_y = self.swap(both[:half, 3], 2), self.swap(both[half:, 3], 4)
        direct_x, direct_y = self.swap(both[:half, 1], 2), self.swap(both[half:, 2], 4)
        to_x = (both[half:, 1].astype(f32) + far_y.astype(f32)).astype(bf16)
        to_y = (both[:half, 2].astype(f32) + far_x.astype(f32)).astype(bf16)
        later_x, later_y = self.swap(to_x, 2), self.swap(to_y, 4)
        from_x = jnp.concatenate([direct_x, later_x], axis=0).astype(f32)
        from_y = jnp.concatenate([later_y, direct_y], axis=0).astype(f32)
        return both[:, 0].astype(f32) + from_x + from_y

    def order(self, places):
        s, n, r = places.shape
        if self.relative:
            me = lax.axis_index("ctx")
            bits = places.reshape(s, 2, 2, 2, r)
            for axis, bit in ((1, 4), (2, 2), (3, 1)):
                bits = jnp.where((me & bit) != 0, jnp.flip(bits, axis), bits)
            places = bits.reshape(s, n, r)
        return places.reshape(s, n // 2, 2, r).transpose(2, 0, 1, 3)


def zero_of(value):
    first = lax.slice(value, (0,) * value.ndim, (1,) * value.ndim).reshape(()).astype(f32)
    return (first != first).astype(jnp.int32)


def after(value, earlier):
    return jnp.where(zero_of(earlier) == 0, value, jnp.zeros_like(value))


def gather_rows(own):
    return lax.all_gather(own, "fsdp", axis=0, tiled=True)


def by_owners(partial, n, rows):
    depth, columns = partial.shape
    return partial.astype(bf16).reshape(n, depth // (n * rows), rows, columns).transpose(1, 0, 2, 3)


def sum_rows(laid):
    groups, n, rows, columns = laid.shape
    return lax.psum_scatter(
        laid.reshape(groups * n * rows, columns), "fsdp", scatter_dimension=0, tiled=True
    ).reshape(n, rows, columns)


def line_total(value):
    size = lax.axis_size("fsdp")
    bit = 1
    while bit < size:
        value = value + lax.ppermute(value, "fsdp", [(i, i ^ bit) for i in range(size)])
        bit = 2 * bit
    return lax.dynamic_index_in_dim(value, lax.axis_index("fsdp"), value.ndim - 1, keepdims=False)


def to_owners(sums):
    return lax.all_to_all(sums, "ctx", split_axis=0, concat_axis=0, tiled=True)


PARAMS = pltpu.CompilerParams(vmem_limit_bytes=56 * 1024 * 1024)


def whole_spec(shape):
    return pl.BlockSpec(shape, lambda i: (0,) * len(shape), pipeline_mode=pl.Buffered(1))


def tile_spec(tile, width):
    return pl.BlockSpec((tile, width), lambda i: (i, 0))


def project_kernel(x_ref, gain_ref, cos_ref, sin_ref, w_ref, low_ref, q_ref, k_ref, v_ref):
    x = x_ref[...].astype(f32)
    low = (x * rms_scale(x) * gain_ref[...]).astype(bf16)
    low_ref[...] = low
    lanes = q_ref.shape[-1]
    projected = dot(low, w_ref[...])
    cosine, sine = cos_ref[...], sin_ref[...]
    q_ref[...] = rotate(projected[:, :lanes], cosine, sine).astype(bf16)
    k_ref[...] = rotate(projected[:, lanes : 2 * lanes], cosine, sine).astype(bf16)
    v_ref[...] = projected[:, 2 * lanes :].astype(bf16)


def project(x, gain, cosine, sine, weight):
    tokens, d = x.shape
    lanes = cosine.shape[1]
    tile = min(512, tokens)
    return pl.pallas_call(
        project_kernel,
        grid=(tokens // tile,),
        in_specs=[tile_spec(tile, d), whole_spec((1, d))]
        + [tile_spec(tile, lanes)] * 2
        + [whole_spec(weight.shape)],
        out_specs=[tile_spec(tile, d)] + [tile_spec(tile, lanes)] * 3,
        out_shape=[jax.ShapeDtypeStruct((tokens, d), bf16)]
        + [jax.ShapeDtypeStruct((tokens, lanes), bf16)] * 3,
        compiler_params=PARAMS,
        cost_estimate=pl.CostEstimate(
            flops=6 * tokens * d * lanes, bytes_accessed=6 * tokens * d, transcendentals=0
        ),
    )(x, gain.reshape(1, d), cosine, sine, weight)


def residual_kernel(x_ref, att_ref, gain_ref, w_ref, low_ref, res_ref):
    n, _, width = w_ref.shape
    for c in range(n):
        columns = slice(c * width, (c + 1) * width)
        res_ref[:, columns] = x_ref[:, columns].astype(f32) + dot(att_ref[...], w_ref[c])
    residual = res_ref[...]
    low_ref[...] = (residual * rms_scale(residual) * gain_ref[...]).astype(bf16)


def residuals(x, attended, gain, out_blocks):
    tokens, d = x.shape
    tile = min(512, tokens)
    return pl.pallas_call(
        residual_kernel,
        grid=(tokens // tile,),
        in_specs=[tile_spec(tile, d), tile_spec(tile, d), whole_spec((1, d)), whole_spec(out_blocks.shape)],
        out_specs=[tile_spec(tile, d), tile_spec(tile, d)],
        out_shape=[jax.ShapeDtypeStruct((tokens, d), bf16), jax.ShapeDtypeStruct((tokens, d), f32)],
        compiler_params=PARAMS,
        cost_estimate=pl.CostEstimate(
            flops=2 * tokens * d * d, bytes_accessed=10 * tokens * d, transcendentals=0
        ),
    )(x, attended, gain.reshape(1, d), out_blocks)


def gathered_residual_kernel(x_ref, gain_ref, w_ref, *refs):
    parts, (own_ref, low_ref, res_ref, all_ref, att, total) = refs[:8], refs[8:14]
    line = LineGather(own_ref, all_ref, *refs[14:])
    step, steps = pl.program_id(0) * pl.num_programs(1) + pl.program_id(1), 8
    pl.when(step == 0)(lambda: greet(line=True))
    line.ride(step, steps)
    width = w_ref.shape[-1]
    shape = low_ref.shape

    def columns(index):
        return pl.ds(pl.multiple_of(flipped(lax.axis_index("ctx"), index) * width, width), width)

    for index, part in enumerate(parts):
        att[:, columns(index)] = part[...].reshape(-1, width)
    attended = att[...]
    for index in range(8):
        total[:, columns(index)] = dot(attended, w_ref[index % 2, :, index // 2].reshape(-1, width))
    residual = total[...] + x_ref[...].reshape(attended.shape).astype(f32)
    res_ref[...] = residual.reshape(shape)
    low_ref[...] = (residual * rms_scale(residual) * gain_ref[...]).astype(bf16).reshape(shape)
    pl.when(step == steps - 1)(line.finish)


def gathered_residuals(x, attended, gain, out_blocks, own, identity):
    _, s, q, r, d = x.shape
    width = attended.shape[-1]
    tile = pl.BlockSpec((1, s, 1, r, d), lambda p, t: (p, 0, t, 0, 0))

    def sent(index):
        odd, other = index % 2, index // 2
        return pl.BlockSpec(
            (1, 1, 1, s, 1, r, width),
            lambda p, t: (odd, (p + odd) % 2, other, 0, flipped(t, other), 0, 0),
        )

    def fixed(shape):
        return pl.BlockSpec(shape, lambda p, t: (0,) * len(shape), pipeline_mode=pl.Buffered(1))

    return pl.pallas_call(
        gathered_residual_kernel,
        grid=(2, q),
        in_specs=[tile, fixed((1, d)), fixed(out_blocks.shape)]
        + [sent(i) for i in range(8)]
        + [STAGED],
        out_specs=[tile, tile, ANYWHERE],
        out_shape=[
            jax.ShapeDtypeStruct(x.shape, bf16),
            jax.ShapeDtypeStruct(x.shape, f32),
            line_shape(own),
        ],
        scratch_shapes=[
            pltpu.VMEM((s * r, d), bf16),
            pltpu.VMEM((s * r, d), f32),
            *LineGather.SEMAPHORES,
        ],
        compiler_params=talking(identity),
        cost_estimate=pl.CostEstimate(
            flops=2 * x.size * d, bytes_accessed=10 * x.size, transcendentals=0
        ),
    )(x, gain.reshape(1, d), out_blocks, *[attended] * 8, own)


def hidden_kernel(skipped, low_ref, cot_ref, w_gate, w_up, w_down, *refs):
    hidden_ref, gate_ref, up_ref = refs[skipped:]
    low = low_ref[...]
    gate, upward = dot(low, w_gate[...]), dot(low, w_up[...])
    grad_hidden = dot(cot_ref[...], w_down[...])
    sigmoid = jax.nn.sigmoid(gate)
    hidden_ref[...] = (gate * sigmoid * upward).astype(bf16)
    gate_ref[...] = (grad_hidden * upward * sigmoid * (1.0 + gate * (1.0 - sigmoid))).astype(bf16)
    up_ref[...] = (grad_hidden * gate * sigmoid).astype(bf16)


def block_specs(weights):
    return [
        pl.BlockSpec((array.shape[0], width), lambda i, pick=pick: (0, pick), pipeline_mode=pl.Buffered(1))
        for array, width, pick in weights
    ]


def arrays(weights):
    return [array for array, _, _ in weights]


def hidden_part(second_low, cot, weights, earlier=()):
    tokens, d = second_low.shape
    step = weights[0][1]
    tile = min(512, tokens)
    return pl.pallas_call(
        functools.partial(hidden_kernel, len(earlier)),
        grid=(tokens // tile,),
        in_specs=[tile_spec(tile, d)] * 2 + block_specs(weights) + [ANYWHERE] * len(earlier),
        out_specs=[tile_spec(tile, step)] * 3,
        out_shape=[jax.ShapeDtypeStruct((tokens, step), bf16)] * 3,
        compiler_params=PARAMS,
        cost_estimate=pl.CostEstimate(
            flops=6 * tokens * d * step, bytes_accessed=4 * tokens * d, transcendentals=tokens * step
        ),
    )(second_low, cot, *arrays(weights), *earlier)


def back_kernel(count, *refs):
    lefts, weights = refs[:count], refs[count : 2 * count]
    total = None
    for left, weight in zip(lefts, weights):
        part = dot_rows(left[...], weight[...])
        total = part if total is None else total + part
    refs[2 * count][...] = total.astype(bf16)


def taken(weights):
    return [
        (array, width, pick)
        if width % 128 == 0
        else (lax.slice_in_dim(array, pick * width, (pick + 1) * width, axis=1), width, 0)
        for array, width, pick in weights
    ]


def back(lefts, weights, first, tokens):
    d = weights[0][0].shape[0]
    tile = min(256, tokens)
    start = first // tile
    weights = taken(weights)
    return pl.pallas_call(
        functools.partial(back_kernel, len(lefts)),
        grid=(tokens // tile,),
        in_specs=[pl.BlockSpec((tile, left.shape[1]), lambda i: (i + start, 0)) for left in lefts]
        + block_specs(weights),
        out_specs=tile_spec(tile, d),
        out_shape=jax.ShapeDtypeStruct((tokens, d), bf16),
        compiler_params=PARAMS,
        cost_estimate=pl.CostEstimate(
            flops=2 * tokens * d * sum(left.shape[1] for left in lefts),
            bytes_accessed=4 * tokens * d,
            transcendentals=0,
        ),
    )(*lefts, *arrays(weights))


FAR, BY_X, BY_Y, OWN = 3, 1, 2, 0
TURNS = ((1, FAR), (1, BY_X), (0, FAR), (1, BY_Y), (0, BY_X), (1, OWN), (0, BY_Y), (0, OWN))
PARITIES = sum(p << t for t, (p, _) in enumerate(TURNS))
PLACES = sum(q << (2 * t) for t, (_, q) in enumerate(TURNS))


def norm_back(grad, x, base, gain):
    scale = rms_scale(x)
    weighted = gain * grad
    mean = jnp.mean(weighted * x, axis=-1, keepdims=True)
    return base + scale * weighted - x * (scale * scale * scale) * mean, grad * x * scale


def back_scatter_kernel(count, skipped, riding, *refs):
    lefts, weights, refs = refs[:count], refs[count : 2 * count], refs[2 * count + skipped :]
    laid, refs = refs[:riding], refs[riding:]
    based = len(refs) - riding - (15 if riding else 11) == 6
    base_ref, refs = (refs[0], refs[1:]) if based else (None, refs)
    x_ref, gain_ref, grad_ref, low_ref, sum_ref = refs[:5]
    lines, refs = refs[5 : 5 + riding], refs[5 + riding :]
    given, got, sums, own, far, from_x, from_y, send_odd, came_odd, sent, came = refs[:11]
    lines = [LineSum(laid[0], 0, out, *refs[11:]) for out in lines]
    sibling, by_x, by_y = neighbours()
    greet(line=riding > 0)
    for line in lines:
        line.send()
    s, r, d = own.shape
    half = s // 2

    def move(partner, source, target, send_sem, recv_sem):
        return pltpu.make_async_remote_copy(
            src_ref=source,
            dst_ref=target,
            send_sem=send_sem,
            recv_sem=recv_sem,
            device_id={"ctx": partner},
            device_id_type=MESH,
        )

    def odd_copy(q):
        return move(sibling, given.at[q], got.at[q], send_odd.at[q], came_odd.at[q])

    low_half, high_half = pl.ds(0, half), pl.ds(half, half)
    far_x = move(by_x, sums.at[FAR, low_half], far.at[low_half], sent.at[0], came.at[0])
    far_y = move(by_y, sums.at[FAR, high_half], far.at[high_half], sent.at[1], came.at[1])
    first_x = move(by_x, sums.at[BY_X, low_half], from_x.at[low_half], sent.at[2], came.at[2])
    first_y = move(by_y, sums.at[BY_Y, high_half], from_y.at[high_half], sent.at[3], came.at[3])
    last_x = move(by_x, sums.at[BY_X, high_half], from_x.at[high_half], sent.at[4], came.at[4])
    last_y = move(by_y, sums.at[BY_Y, low_half], from_y.at[low_half], sent.at[5], came.at[5])

    def turn(t, _):
        p = lax.shift_right_logical(jnp.int32(PARITIES), t) % 2
        q = lax.shift_right_logical(jnp.int32(PLACES), 2 * t) % 4
        total = None
        for left, weight in zip(lefts, weights):
            width = left.shape[-1]
            part = dot_rows(left[p, :, q].reshape(s * r, width), weight[...])
            total = part if total is None else total + part
        total = total.reshape(s, r, d)

        @pl.when(p == 1)
        def _():
            given[q] = total.astype(bf16)
            odd_copy(q).start()

        @pl.when(p == 0)
        def _():
            odd_copy(q).wait_recv()
            both = total + got[q].astype(f32)

            @pl.when(q == OWN)
            def _():
                own[...] = both

            @pl.when(q != OWN)
            def _():
                sums[q] = both.astype(bf16)

            @pl.when(q == FAR)
            def _():
                far_x.start()
                far_y.start()

            @pl.when(q == BY_X)
            def _():
                first_x.start()

            @pl.when(q == BY_Y)
            def _():
                first_y.start()

        return 0

    lax.fori_loop(0, len(TURNS), turn, 0)
    for line in lines:
        line.pass_on()
    far_x.wait_recv()
    sums[BY_Y, low_half] = (sums[BY_Y, low_half].astype(f32) + far[low_half].astype(f32)).astype(bf16)
    last_y.start()
    far_y.wait_recv()
    sums[BY_X, high_half] = (sums[BY_X, high_half].astype(f32) + far[high_half].astype(f32)).astype(bf16)
    last_x.start()
    first_x.wait_recv()
    first_y.wait_recv()
    own[low_half] += from_x[low_half].astype(f32)
    own[high_half] += from_y[high_half].astype(f32)
    last_y.wait_recv()
    own[low_half] += from_y[low_half].astype(f32)
    last_x.wait_recv()
    own[high_half] += from_x[high_half].astype(f32)

    sum_ref[...] = jnp.zeros_like(sum_ref)
    slab = min(32, r)

    def finish(index, _):
        at = (index // (r // slab), pl.ds(pl.multiple_of((index % (r // slab)) * slab, slab), slab))
        base = base_ref[at].astype(f32) if based else 0.0
        grad, terms = norm_back(own[at], x_ref[at].astype(f32), base, gain_ref[...])
        grad_ref[at] = grad
        low_ref[at] = grad.astype(bf16)
        sum_ref[...] += jnp.sum(terms, axis=0, keepdims=True)
        return 0

    lax.fori_loop(0, s * (r // slab), finish, 0)
    for line in lines:
        line.finish()
    for copy in (far_x, far_y, first_x, first_y, last_x, last_y):
        copy.wait_send()
    for q in range(4):
        odd_copy(q).wait_send()


def back_scatter(lefts, weights, shape, identity, x, base, gain, earlier=(), last=False, laid=None):
    s, q, r, d = shape
    width = sum(left.shape[-1] for left in lefts)
    weights = taken(weights)
    lefts = [left.reshape(2, s, q, r, left.shape[-1]) for left in lefts]

    def fixed(whole):
        return pl.BlockSpec(whole, lambda i: (0,) * len(whole), pipeline_mode=pl.Buffered(1))

    operands = [*lefts, *arrays(weights), *earlier]
    in_specs = [fixed(left.shape) for left in lefts] + block_specs(weights)
    in_specs += [ANYWHERE] * len(earlier)
    riding = laid is not None
    based = base is not None
    operands += [laid] * riding + [base] * based + [x, gain.reshape(1, d)]
    in_specs += [ANYWHERE] * riding + [fixed((s, r, d))] * (1 + based) + [fixed((1, d))]
    out_specs = [fixed((s, r, d)), fixed((s, r, d)), fixed((1, d))]
    out_shape = [
        jax.ShapeDtypeStruct((s, r, d), f32),
        jax.ShapeDtypeStruct((s, r, d), bf16),
        jax.ShapeDtypeStruct((1, d), f32),
    ]
    line_scratch = []
    if riding:
        part = (laid.shape[1], laid.shape[2], laid.shape[3] // 3)
        out_specs.append(fixed(part))
        out_shape.append(jax.ShapeDtypeStruct(part, bf16))
        line_scratch = LineSum.scratch(laid.shape, part[2])
    dma = pltpu.SemaphoreType.DMA
    return pl.pallas_call(
        functools.partial(back_scatter_kernel, len(lefts), len(earlier), int(riding)),
        grid=(1,),
        in_specs=in_specs,
        out_specs=out_specs,
        out_shape=out_shape,
        scratch_shapes=[
            pltpu.VMEM((4, s, r, d), bf16),
            pltpu.VMEM((4, s, r, d), bf16),
            pltpu.VMEM((4, s, r, d), bf16),
            pltpu.VMEM((s, r, d), f32),
            pltpu.VMEM((s, r, d), bf16),
            pltpu.VMEM((s, r, d), bf16),
            pltpu.VMEM((s, r, d), bf16),
            dma((4,)),
            dma((4,)),
            dma((6,)),
            dma((6,)),
            *line_scratch,
        ],
        compiler_params=talking(identity),
        cost_estimate=pl.CostEstimate(
            flops=1 if last else 16 * s * r * d * width,
            bytes_accessed=1 if last else 16 * s * r * d,
            transcendentals=0,
            remote_bytes_transferred=1 if last else 14 * s * r * d,
        ),
    )(*operands)


def weighted_sums_kernel(counts, *refs):
    inputs = sum(counts) + len(counts)
    weight_ref, (out_ref, sum_ref) = refs[inputs], refs[-2:]
    sum_ref[...] = jnp.zeros_like(sum_ref)
    token_sums_kernel(counts, *refs[:inputs], out_ref, weighted=(weight_ref, sum_ref))


def token_sums_kernel(counts, *refs, weighted=None):
    out_ref = refs[-1]
    start = 0
    for count in counts:
        left, rights, refs = refs[0], refs[1 : 1 + count], refs[1 + count :]
        for right in rights:
            width = right.shape[1]
            part = dot_tokens(left[...], right[...])
            if weighted is not None:
                weight = weighted[0][:, start : start + width].astype(f32)
                weighted[1][...] += jnp.sum(part * weight, axis=1, keepdims=True)
            part = part.astype(bf16)
            groups, owners, rows, _ = out_ref.shape
            part = part.reshape(owners, groups, rows, width)
            for owner in range(owners):
                out_ref[:, owner, :, start : start + width] = part[owner]
            start += width


def token_sums(pairs, n, rows, earlier=(), weight=None):
    groups = pairs[0][0].shape[1] // (n * rows)
    operands, in_specs, width = [], [], 0
    for left, rights in pairs:
        operands += [left, *rights]
        in_specs.append(pl.BlockSpec((left.shape[0], 2 * groups * rows), lambda i: (0, i)))
        in_specs += [whole_spec(right.shape) for right in rights]
        width += sum(right.shape[1] for right in rights)
    tokens, d = pairs[0][0].shape
    out_specs = [pl.BlockSpec((groups, 2, rows, width), lambda i: (0, i, 0, 0))]
    out_shape = [jax.ShapeDtypeStruct((groups, n, rows, width), bf16)]
    if weight is not None:
        side = 2 * groups * rows
        operands.append(weight)
        in_specs.append(pl.BlockSpec((side, width), lambda i: (i, 0)))
        out_specs.append(pl.BlockSpec((side, 1), lambda i: (i, 0)))
        out_shape.append(jax.ShapeDtypeStruct((d, 1), f32))
    return pl.pallas_call(
        functools.partial(
            token_sums_kernel if weight is None else weighted_sums_kernel, [len(rights) for _, rights in pairs]
        ),
        grid=(n // 2,),
        in_specs=in_specs + [ANYWHERE] * len(earlier),
        out_specs=out_specs,
        out_shape=out_shape,
        compiler_params=PARAMS,
        cost_estimate=pl.CostEstimate(
            flops=2 * tokens * d * width, bytes_accessed=4 * tokens * d, transcendentals=0
        ),
    )(*operands, *earlier)


def output_back_kernel(low_ref, att_ref, w_ref, *refs):
    grad_ref, sum_ref, total = refs[-3:]

    @pl.when(pl.program_id(0) == 0)
    def _():
        total[...] = jnp.zeros_like(total)

    low = low_ref[...]
    grad_ref[...] = dot_rows(low, w_ref[...]).astype(bf16)
    total[...] += dot_tokens(att_ref[...], low)

    @pl.when(pl.program_id(0) == pl.num_programs(0) - 1)
    def _():
        groups, n, rows, width = sum_ref.shape
        for group in range(groups):
            for c in range(n):
                part = total[group * rows : (group + 1) * rows, c * width : (c + 1) * width]
                sum_ref[group, c] = part.astype(bf16)


def output_back(grad_low, attended_low, out_rows, n, rows, earlier=()):
    tokens, d = grad_low.shape
    lanes = attended_low.shape[1]
    sums = (lanes // rows, n, rows, d // n)
    tile = min(512, tokens)
    return pl.pallas_call(
        output_back_kernel,
        grid=(tokens // tile,),
        in_specs=[tile_spec(tile, d), tile_spec(tile, lanes), whole_spec((lanes, d))]
        + [ANYWHERE] * len(earlier),
        out_specs=[tile_spec(tile, lanes), pl.BlockSpec(sums, lambda i: (0, 0, 0, 0))],
        out_shape=[
            jax.ShapeDtypeStruct((tokens, lanes), bf16),
            jax.ShapeDtypeStruct(sums, bf16),
        ],
        scratch_shapes=[pltpu.VMEM((lanes, d), f32)],
        compiler_params=PARAMS,
        cost_estimate=pl.CostEstimate(
            flops=4 * tokens * d * lanes, bytes_accessed=2 * tokens * d, transcendentals=0
        ),
    )(grad_low, attended_low, out_rows, *earlier)


def gather_and_sum_kernel(hiddens, skipped, low_ref, gate_ref, up_ref, cot_ref, *refs):
    lefts, weights = refs[:hiddens], refs[hiddens : 2 * hiddens]
    refs = refs[2 * hiddens :]
    own_ref, laid_ref, refs = refs[0], refs[1], refs[2 + skipped :]
    sum_ref, out_ref, all_ref, line_ref = refs[:4]
    gather = Gather(own_ref, all_ref, *refs[4:7])
    line = LineSum(laid_ref, laid_ref.shape[-1] // 3, line_ref, *refs[7:])
    step, steps = pl.program_id(0), 8
    pl.when(step == 0)(lambda: greet(line=True))
    gather.ride(step, steps)
    pl.when(step == 0)(line.send)
    pl.when(step == steps // 2)(line.pass_on)
    tile = lefts[0].shape[0] // steps
    token_sums_kernel([2, 1], low_ref, gate_ref, up_ref, cot_ref, lefts[-1], sum_ref)
    rows = pl.ds(pl.multiple_of(step * tile, tile), tile)
    total = None
    for left, weight in zip(lefts, weights):
        part = dot_rows(left[rows, :], weight[...])
        total = part if total is None else total + part
    out_ref[...] = total.astype(bf16)
    pl.when(step == steps - 1)(gather.finish)
    pl.when(step == steps - 1)(line.finish)


def gather_and_sum(own, laid, second_low, grads, cot, hiddens, weights, rows, identity, earlier=()):
    tokens, d = second_low.shape
    step = hiddens[0].shape[1]
    groups = d // (8 * rows)
    column = pl.BlockSpec((tokens, groups * rows), lambda i: (0, i))
    part = (laid.shape[1], laid.shape[2], laid.shape[3] // 3)
    return pl.pallas_call(
        functools.partial(gather_and_sum_kernel, len(hiddens), len(earlier)),
        grid=(8,),
        in_specs=[column, whole_spec(grads[0].shape), whole_spec(grads[1].shape), column]
        + [whole_spec(hidden.shape) for hidden in hiddens]
        + block_specs(weights)
        + [STAGED]
        + [ANYWHERE] * (1 + len(earlier)),
        out_specs=[
            pl.BlockSpec((groups, 1, rows, 3 * step), lambda i: (0, i, 0, 0)),
            tile_spec(tokens // 8, d),
            ANYWHERE,
            whole_spec(part),
        ],
        out_shape=[
            jax.ShapeDtypeStruct((groups, 8, rows, 3 * step), bf16),
            jax.ShapeDtypeStruct((tokens, d), bf16),
            gathered_shape(own),
            jax.ShapeDtypeStruct(part, bf16),
        ],
        scratch_shapes=[*Gather.SEMAPHORES, *LineSum.scratch(laid.shape, part[2])],
        compiler_params=talking(identity),
        cost_estimate=pl.CostEstimate(
            flops=14 * tokens * d * step, bytes_accessed=12 * tokens * d, transcendentals=0
        ),
    )(second_low, *grads, cot, *hiddens, *arrays(weights), own, laid, *earlier)


def spread_kernel(count, *refs):
    parts, lasts, out_ref, last_ref = refs[:count], refs[count : 2 * count], refs[-2], refs[-1]
    senders, _, width = parts[0].shape

    def write(target, sources):
        for sender in range(senders):
            for index, part in enumerate(sources):
                start = (sender * count + index) * width
                target[:, start : start + width] = part[sender].astype(f32)

    pl.when(pl.program_id(0) < 2)(lambda: write(out_ref, parts))
    pl.when(pl.program_id(0) == 2)(lambda: write(last_ref, lasts))


def spread(parts, width):
    n, rows, _ = parts[0][0][0].shape
    count = len(parts)
    pair = min(n, 4)
    wide = pair * count * width
    turns = n // pair
    specs = [
        pl.BlockSpec(
            (pair, rows, width),
            lambda third, i, place=first[1]: (jnp.where(third < 2, i, turns - 1), 0, place + jnp.minimum(third, 1)),
        )
        for first, _, _ in parts
    ] + [
        pl.BlockSpec((pair, rows, width), lambda third, i, place=last[1]: (jnp.where(third < 2, 0, i), 0, place))
        for _, _, last in parts
    ]
    return pl.pallas_call(
        functools.partial(spread_kernel, count),
        grid=(3, turns),
        in_specs=specs,
        out_specs=[
            pl.BlockSpec((rows, wide), lambda third, i: (0, jnp.minimum(third * turns + i, 2 * turns - 1))),
            pl.BlockSpec((rows, wide), lambda third, i: (0, jnp.maximum(third - 1, 0) * i)),
        ],
        out_shape=[
            jax.ShapeDtypeStruct((rows, 2 * n * count * width), f32),
            jax.ShapeDtypeStruct((rows, n * count * width), f32),
        ],
        compiler_params=PARAMS,
        cost_estimate=pl.CostEstimate(
            flops=0, bytes_accessed=18 * n * rows * count * width, transcendentals=0
        ),
    )(*[first[0] for first, _, _ in parts], *[last[0] for _, _, last in parts])


def spread_all_kernel(part_ref, _, out_ref):
    senders, _, width = part_ref.shape
    for sender in range(senders):
        out_ref[:, sender * width : (sender + 1) * width] = part_ref[sender].astype(f32)


def spread_all(part, width, earlier):
    n, rows, _ = part.shape
    return pl.pallas_call(
        spread_all_kernel,
        grid=(3,),
        in_specs=[pl.BlockSpec((n, rows, width), lambda i: (0, 0, i)), ANYWHERE],
        out_specs=pl.BlockSpec((rows, n * width), lambda i: (0, i)),
        out_shape=jax.ShapeDtypeStruct((rows, 3 * n * width), f32),
        compiler_params=PARAMS,
        cost_estimate=pl.CostEstimate(
            flops=0, bytes_accessed=18 * n * rows * width, transcendentals=0
        ),
    )(part, earlier)


class PlaneSum:
    @staticmethod
    def scratch(shape):
        _, s, q, r, d = shape
        dma = pltpu.SemaphoreType.DMA
        block = pltpu.VMEM((s, r, d), bf16)
        blocks = pltpu.VMEM((q, s, r, d), bf16)
        return [blocks, blocks, block, block, block, dma((4,)), dma((4,)), dma((4,)), dma((6,)), dma((6,))]

    def __init__(self, parts, out, held, got, far, from_x, from_y, local, send_odd, came_odd, sent, came):
        self.out, self.held, self.got = out, held, got
        self.far, self.from_x, self.from_y = far, from_x, from_y
        sibling, by_x, by_y = neighbours()
        half = far.shape[0] // 2
        self.low, self.high = low, high = pl.ds(0, half), pl.ds(half, half)

        def move(partner, source, target, send_sem, recv_sem):
            return pltpu.make_async_remote_copy(
                src_ref=source,
                dst_ref=target,
                send_sem=send_sem,
                recv_sem=recv_sem,
                device_id={"ctx": partner},
                device_id_type=MESH,
            )

        self.loads = [pltpu.make_async_copy(parts.at[0, :, q], held.at[q], local.at[q]) for q in range(4)]
        self.odd = [
            move(sibling, parts.at[1, :, q], got.at[q], send_odd.at[q], came_odd.at[q]) for q in range(4)
        ]
        routes = [
            (by_x, held.at[FAR, low], far.at[low]),
            (by_y, held.at[FAR, high], far.at[high]),
            (by_x, held.at[BY_X, low], from_x.at[low]),
            (by_y, held.at[BY_Y, high], from_y.at[high]),
            (by_x, held.at[BY_X, high], from_x.at[high]),
            (by_y, held.at[BY_Y, low], from_y.at[low]),
        ]
        self.copies = [
            move(partner, source, target, sent.at[index], came.at[index])
            for index, (partner, source, target) in enumerate(routes)
        ]

    def send(self):
        for q in (FAR, BY_X, BY_Y, OWN):
            self.odd[q].start()
            self.loads[q].start()

    def join(self, q):
        self.loads[q].wait()
        self.odd[q].wait_recv()
        self.held[q] = (self.held[q].astype(f32) + self.got[q].astype(f32)).astype(bf16)

    def send_far(self):
        self.join(FAR)
        self.copies[0].start()
        self.copies[1].start()

    def send_first(self):
        self.join(BY_X)
        self.copies[2].start()
        self.join(BY_Y)
        self.copies[3].start()
        self.join(OWN)

    def send_last(self):
        for arrived, q, part, copy in ((1, BY_X, self.high, 4), (0, BY_Y, self.low, 5)):
            self.copies[arrived].wait_recv()
            added = self.held[q, part].astype(f32) + self.far[part].astype(f32)
            self.held[q, part] = added.astype(bf16)
            self.copies[copy].start()

    def finish(self):
        for copy in self.copies[2:]:
            copy.wait_recv()
        for copy in (*self.copies, *self.odd):
            copy.wait_send()
        total = self.held[OWN].astype(f32) + self.from_x[...].astype(f32) + self.from_y[...].astype(f32)
        self.out[...] = total

    def ride(self, step, steps):
        turns = (0, self.send), (steps // 8, self.send_far), (steps // 4, self.send_first)
        for turn, phase in (*turns, (steps // 2, self.send_last)):
            pl.when(step == turn)(phase)


def only(values, head, heads):
    if heads == 1:
        return values
    lane = lax.broadcasted_iota(jnp.int32, values.shape, 1)
    inside = (lane >= head * HEAD_SIZE) & (lane < (head + 1) * HEAD_SIZE)
    return jnp.where(inside, values, jnp.zeros_like(values))


def forward_kernel(heads, q_spot, k_spot, q_ref, k_ref, v_ref, *refs):
    if len(refs) > 2:
        own_ref, line_ref, low_ref, total_ref, all_ref, line_all_ref = refs[:6]
        gather = Gather(own_ref, all_ref, *refs[6:9])
        line = LineGather(line_ref, line_all_ref, *refs[9:])
        steps = pl.num_programs(0) * pl.num_programs(1) * pl.num_programs(2)
        step = (pl.program_id(0) * pl.num_programs(1) + pl.program_id(1)) * pl.num_programs(2)
        step += pl.program_id(2)
        pl.when(step == 0)(lambda: greet(line=True))
        gather.ride(step, steps)
        line.ride(step, steps)
    else:
        low_ref, total_ref = refs
    lanes = q_ref.shape[-1]
    queries = q_ref[0, 0] * bf16(HEAD_SIZE**-0.5)
    keys = k_ref[:, 0].reshape(-1, lanes)
    values = v_ref[:, 0].reshape(-1, lanes)
    allowed = k_spot[0] <= q_spot[0, 0]
    attended = jnp.zeros(queries.shape, f32)
    for head in range(heads):
        scores = dot_rows(keys, only(queries, head, heads))
        scores = jnp.where(allowed, scores, -1e30)
        highest = jnp.max(scores, axis=0, keepdims=True)
        raised = jnp.exp(scores - highest)
        summed = jnp.sum(raised, axis=0, keepdims=True)
        probs = (raised * (1.0 / summed)).astype(bf16)
        total_ref[0, 0, head : head + 1, :] = highest + jnp.log(summed)
        attended += dot_tokens(probs, only(values, head, heads))
    low_ref[0, 0] = attended.astype(bf16)
    if len(refs) > 2:
        pl.when(step == steps - 1)(line.finish)
        pl.when(step == steps - 1)(gather.finish)


def backward_kernel(
    heads, q_spot, k_spot, q_ref, k_ref, v_ref, grad_ref, total_ref, qc_ref, qs_ref, kc_ref, ks_ref, *refs
):
    if len(refs) > 5:
        parts, laid, dq_ref, dk_ref, dv_ref, out_ref, line_ref, dk_sum, dv_sum = refs[:9]
        summing = PlaneSum(parts, out_ref, *refs[9:-4])
        line = LineSum(laid, 2 * (laid.shape[-1] // 3), line_ref, *refs[-4:])
    else:
        dq_ref, dk_ref, dv_ref, dk_sum, dv_sum = refs
    lanes = q_ref.shape[-1]
    scale = HEAD_SIZE**-0.5
    step = pl.program_id(1) * pl.num_programs(2) + pl.program_id(2)
    if len(refs) > 5:
        turn = pl.program_id(0) * pl.num_programs(1) * pl.num_programs(2) + step
        turns = pl.num_programs(0) * pl.num_programs(1) * pl.num_programs(2)
        pl.when(turn == 0)(lambda: greet(line=True))
        summing.ride(turn, turns)
        pl.when(turn == 0)(line.send)
        pl.when(turn == turns // 2)(line.pass_on)

    @pl.when(step == 0)
    def _():
        dk_sum[...] = jnp.zeros_like(dk_sum)
        dv_sum[...] = jnp.zeros_like(dv_sum)

    queries = q_ref[0, 0] * bf16(scale)
    grads = grad_ref[0, 0]
    keys = k_ref[:, 0].reshape(-1, lanes)
    values = v_ref[:, 0].reshape(-1, lanes)
    allowed = k_spot[0] <= q_spot[0, 0]
    grad_q = jnp.zeros(queries.shape, f32)
    for head in range(heads):
        query = only(queries, head, heads)
        grad = only(grads, head, heads)
        scores = jnp.where(allowed, dot_rows(keys, query), -1e30)
        probs = jnp.exp(scores - total_ref[0, 0, head : head + 1, :])
        dv_sum[...] += dot(probs.astype(bf16), grad)
        weighted = probs * dot_rows(values, grad)
        delta = jnp.sum(weighted, axis=0, keepdims=True)
        grad_scores = (weighted - probs * delta).astype(bf16)
        dk_sum[...] += dot(grad_scores, query)
        grad_q += dot_tokens(grad_scores, only(keys, head, heads))
    dq_ref[0, 0] = rotate_back(grad_q * scale, qc_ref[0, 0], qs_ref[0, 0]).astype(bf16)

    @pl.when(step == pl.num_programs(1) * pl.num_programs(2) - 1)
    def _():
        shape = (dk_ref.shape[0],) + dk_ref.shape[2:]
        cosine = kc_ref[:, 0].reshape(-1, lanes)
        sine = ks_ref[:, 0].reshape(-1, lanes)
        dk_ref[:, 0] = rotate_back(dk_sum[...], cosine, sine).astype(bf16).reshape(shape)
        dv_ref[:, 0] = dv_sum[...].astype(bf16).reshape(shape)

    if len(refs) > 5:
        pl.when(turn == turns - 1)(summing.finish)
        pl.when(turn == turns - 1)(line.finish)


def attention_specs(shape, heads):
    p, s, rows, lanes = shape
    tile = min(256, rows)
    one = pl.BlockSpec((1, 1, tile, lanes), lambda i, j, t: (j, i, t, 0))
    side = pl.BlockSpec((p, 1, rows, lanes), lambda i, j, t: (0, i, 0, 0))
    stat = pl.BlockSpec((1, 1, heads, tile), lambda i, j, t: (j, i, 0, t))
    q_spot = pl.BlockSpec((1, 1, 1, tile), lambda i, j, t: (j, i, 0, t))
    k_spot = pl.BlockSpec((1, p * rows, 1), lambda i, j, t: (i, 0, 0))
    return (s, p, rows // tile), one, side, stat, q_spot, k_spot


def attend(q_spot, k_spot, queries, keys, values, own=None, line=None, identity=None):
    p, s, rows, lanes = queries.shape
    heads = lanes // HEAD_SIZE
    grid, one, side, stat, q_spec, k_spec = attention_specs(queries.shape, heads)
    pairs = p * rows * s * p * rows
    out_shape = [
        jax.ShapeDtypeStruct(queries.shape, bf16),
        jax.ShapeDtypeStruct((p, s, heads, rows), f32),
    ]
    riding = own is not None
    return pl.pallas_call(
        functools.partial(forward_kernel, heads),
        grid=grid,
        in_specs=[q_spec, k_spec, one, side, side] + [STAGED] * (2 * riding),
        out_specs=[one, stat] + [ANYWHERE] * (2 * riding),
        out_shape=out_shape + ([gathered_shape(own), line_shape(line)] if riding else []),
        scratch_shapes=[*Gather.SEMAPHORES, *LineGather.SEMAPHORES] if riding else [],
        compiler_params=talking(identity) if riding else PARAMS,
        cost_estimate=pl.CostEstimate(
            flops=pairs * heads * 2048, bytes_accessed=queries.size * 14, transcendentals=pairs * heads
        ),
    )(q_spot, k_spot, queries, keys, values, *([own, line] if riding else []))


def attend_back(
    q_spot, k_spot, queries, keys, values, grads, totals, cosine, sine, parts=None, laid=None, identity=None
):
    p, s, rows, lanes = queries.shape
    heads = lanes // HEAD_SIZE
    grid, one, side, stat, q_spec, k_spec = attention_specs(queries.shape, heads)
    pairs = p * rows * s * p * rows
    in_specs = [q_spec, k_spec, one, side, side, one, stat, one, one, side, side]
    out_specs = [one, side, side]
    out_shape = [jax.ShapeDtypeStruct(queries.shape, bf16)] * 3
    scratch = [pltpu.VMEM((p * rows, lanes), f32)] * 2
    operands = [q_spot, k_spot, queries, keys, values, grads, totals, cosine, sine, cosine, sine]
    if parts is not None:
        own = (parts.shape[1], *parts.shape[3:])
        part = (*laid.shape[1:3], laid.shape[3] // 3)
        operands += [parts, laid]
        in_specs += [ANYWHERE] * 2
        for shape, kind in ((own, f32), (part, bf16)):
            out_specs.append(pl.BlockSpec(shape, lambda i, j, t: (0, 0, 0), pipeline_mode=pl.Buffered(1)))
            out_shape.append(jax.ShapeDtypeStruct(shape, kind))
        scratch += [*PlaneSum.scratch(parts.shape), *LineSum.scratch(laid.shape, part[2])]
    return pl.pallas_call(
        functools.partial(backward_kernel, heads),
        grid=grid,
        in_specs=in_specs,
        out_specs=out_specs,
        out_shape=out_shape,
        scratch_shapes=scratch,
        compiler_params=PARAMS if parts is None else talking(identity),
        cost_estimate=pl.CostEstimate(
            flops=pairs * heads * 5120, bytes_accessed=queries.size * 20, transcendentals=pairs * heads
        ),
    )(*operands)


def on_device(
    plane,
    inputs,
    positions,
    first_gain,
    attention_weight,
    output_weight,
    second_gain,
    gate_up_weight,
    down_weight,
    cotangent,
):
    s, r, d = inputs.shape
    n = plane.size
    ff = down_weight.shape[1]
    me = lax.axis_index("ctx")
    lanes = d // n
    mine = ff // n
    step = mine // CHUNKS
    tokens = s * r * n
    rows = d // (n * lax.axis_size("fsdp"))
    half = tokens // 2
    group = (2, s, n // 2 * r)
    blocks = (s, n // 2, r, d)

    def columns(weight, start, width):
        return lax.dynamic_slice_in_dim(weight, start, width, 1)

    qkv = jnp.concatenate(
        [columns(attention_weight, part * d + me * lanes, lanes) for part in range(3)], axis=1
    )
    out_own = columns(output_weight, me * lanes, lanes)
    if plane.relative:
        whole_inputs, cot, qkv, out_own = gather_in_plane([inputs, cotangent], [qkv, out_own], 1)
    else:
        whole_inputs, cot = plane.gather([inputs, cotangent])
        qkv, out_own = gather_rows(qkv), gather_rows(out_own)

    def chunk_parts(chunk, earlier):
        start = (me + zero_of(earlier)) * mine + chunk * step
        return [
            columns(gate_up_weight, start, step),
            columns(gate_up_weight, ff + start, step),
            columns(down_weight, start, step),
        ]

    ffn = {}
    for chunk in range(CHUNKS):
        if chunk != RIDING or not plane.relative:
            whole = gather_rows(jnp.concatenate(chunk_parts(chunk, qkv), axis=1))
            ffn[chunk] = [(whole, step, part) for part in range(3)]

    places = plane.order(positions.reshape(s, n, r)).reshape(group)
    q_spot = places[:, :, None, :]
    k_spot = places.transpose(1, 0, 2).reshape(s, n * r, 1)
    cosine, sine = rope_tables(places.reshape(tokens), lanes, whole_inputs)
    normed_low, queries, keys, values = project(
        whole_inputs.reshape(tokens, d), first_gain, cosine, sine, qkv
    )
    queries, keys, values, cosine, sine = (
        part.reshape(*group, lanes) for part in (queries, keys, values, cosine, sine)
    )
    if plane.relative:
        riders = chunk_parts(RIDING, qkv)
        attended_low, totals, out_blocks, gate = attend(
            q_spot, k_spot, queries, keys, values, out_own.reshape(2, d // 2, lanes), riders[0], 2
        )
        attended_whole, upward = gather_in_plane(
            [attended_low.reshape(2, half, lanes)], riders[1:2], 3
        )
        second_low, residual, down = gathered_residuals(
            whole_inputs,
            attended_whole.reshape(2, 2, 4, s, 4, r, lanes),
            second_gain,
            out_blocks,
            riders[2],
            4,
        )
        ffn[RIDING] = [(whole, step, 0) for whole in (gate, upward, down)]
        second_low = second_low.reshape(tokens, d)
        residual = residual[0, :, 0]
    else:
        attended_low, totals = attend(q_spot, k_spot, queries, keys, values)
        out_blocks = lax.all_gather(out_own, "ctx", axis=0, tiled=False)
        attended_whole = lax.all_gather(
            attended_low.reshape(tokens, lanes), "ctx", axis=1, tiled=True
        )
        second_low, residual = residuals(
            whole_inputs.reshape(tokens, d), attended_whole, second_gain, out_blocks
        )
        residual = lax.dynamic_index_in_dim(residual.reshape(2, *blocks), me % 2, 0, keepdims=False)
        residual = lax.dynamic_index_in_dim(residual, me // 2, 1, keepdims=False)
    cot = cot.reshape(tokens, d)
    attended_low = attended_low.reshape(tokens, lanes)

    if plane.relative:
        out_rows = lax.dynamic_slice(
            out_blocks, (0, me // 4, 0, (me % 4) * lanes, 0), (2, 1, 4, lanes, lanes)
        ).reshape(2, 2, 2, lanes, lanes)
        for axis, bit in ((0, 1), (1, 4), (2, 2)):
            out_rows = jnp.where((me & bit) != 0, jnp.flip(out_rows, axis), out_rows)
        out_rows = out_rows.transpose(3, 1, 2, 0, 4).reshape(lanes, d)
    else:
        out_rows = lax.dynamic_slice_in_dim(out_blocks, me * lanes, lanes, 1)
        out_rows = out_rows.transpose(1, 0, 2).reshape(lanes, d)

    def summed(pairs, earlier=(), weight=None):
        if plane.relative:
            return token_sums(pairs, n, rows, earlier, weight)
        partial = [dot_tokens(left, right) for left, rights in pairs for right in rights]
        partial = jnp.concatenate(partial, axis=1)
        laid = [by_owners(partial, n, rows)]
        return laid if weight is None else [*laid, jnp.sum(partial * weight, axis=1)]

    hiddens, grads, partials, sums = [], [], [], []
    for chunk in ORDER:
        hidden, *grad_gate_up = hidden_part(
            second_low, cot, taken(ffn[chunk]), partials[-1:] or [out_rows]
        )
        hiddens.append(hidden)
        grads.append(grad_gate_up)
        if len(hiddens) < CHUNKS or not plane.relative:
            partials += summed([(second_low, grad_gate_up), (cot, [hidden])])
            if len(hiddens) < CHUNKS - 1 or not plane.relative:
                sums.append(sum_rows(partials[-1]))

    def apart(lefts, weights):
        odd, even = back(lefts, weights, half, half), back(lefts, weights, 0, half)
        return plane.scatter(odd.reshape(blocks), even.reshape(blocks))

    def norm_step(identity, lefts, weights, x, base, gain, earlier, last=False, laid=None):
        if plane.relative:
            return back_scatter(lefts, weights, blocks, identity, x, base, gain, earlier, last, laid)
        base = 0.0 if base is None else base.astype(f32)
        grad, terms = norm_back(apart(lefts, weights), x.astype(f32), base, gain)
        return grad, grad.astype(bf16), jnp.sum(terms, axis=(0, 1))

    grad_residual, grad_residual_low, second_gain_part, *gate_sums = norm_step(
        5,
        [grad for pair in grads for grad in pair],
        [weight for chunk in ORDER for weight in ffn[chunk][:2]],
        residual,
        cotangent,
        second_gain,
        partials[-1:],
        laid=partials[-1] if plane.relative else None,
    )
    downs = [ffn[chunk][2] for chunk in ORDER]
    if plane.relative:
        last, output_parts, grad_low, up_sums = gather_and_sum(
            grad_residual_low,
            partials[-1],
            second_low,
            grads[-1],
            cot,
            hiddens,
            downs,
            rows,
            6,
            sums[:1],
        )
        sums += [*gate_sums, up_sums]
    else:
        last = partials[-1]
        sums.pop()
        (grad_low,) = plane.gather([grad_residual_low])
    grad_low = grad_low.reshape(tokens, d)

    grad_attended, out_part = output_back(
        grad_low, attended_low, out_rows, n, rows
    )
    last = sum_rows(last)
    early = to_owners(after(jnp.concatenate(sums, axis=2), grad_attended))
    operands = (q_spot, k_spot, queries, keys, values, grad_attended.reshape(*group, lanes))
    operands += (totals, cosine, sine)
    if plane.relative:
        *grad_projected, output, down_sums = attend_back(
            *operands, output_parts.reshape(2, *blocks), partials[-1], 8
        )
        output = residual + output
        left = [down_sums]
    else:
        left = []
        grad_projected = attend_back(*operands)
        output = residual + apart(hiddens, downs)
    grad_projected = [part.reshape(tokens, lanes) for part in grad_projected]
    attention_parts, first_gain_part = summed([(normed_low, grad_projected)], [early], qkv)
    first_gain_part = first_gain_part.reshape(d) / first_gain
    attention_sums = sum_rows(attention_parts)
    grad_output_weight = sum_rows(after(out_part, attention_parts))
    grad_input, *_ = norm_step(
        7,
        grad_projected,
        [(qkv, lanes, part) for part in range(3)],
        inputs,
        None,
        first_gain,
        [attention_parts],
        True,
    )
    grad_input = grad_residual + grad_input
    gains = jnp.stack([first_gain_part, second_gain_part.reshape(d)]).astype(bf16)
    gains = gains.reshape(2, n, -1, rows).transpose(1, 3, 0, 2).reshape(n, rows, -1)
    count = gains.shape[-1]
    gains = jnp.pad(gains, ((0, 0), (0, 0), (0, 128 - count)))
    late = to_owners(jnp.concatenate([*left, last, gains], axis=2))
    gains = jnp.sum(late[:, :, -128 : count - 128].astype(f32), axis=0).reshape(rows, 2, -1)
    gains = line_total(after(gains, grad_input))
    attention_sums = to_owners(after(attention_sums, grad_input))
    parts = [[(early, 3 * turn + part) for part in range(3)] for turn in range(CHUNKS - 1)]
    parts.append([(late, len(left) + part) for part in range(3)])
    if plane.relative:
        parts[CHUNKS - 2][2] = (late, 0)
    parts = [parts[ORDER.index(chunk)] for chunk in range(CHUNKS)]
    if plane.relative:
        grad_gate_up, grad_down = spread(parts, step)
        grad_attention = spread_all(attention_sums, lanes, grad_down)
    else:
        whole = [
            [array[:, :, step * place : step * (place + 1)] for array, place in part] for part in parts
        ]
        whole = jnp.stack([jnp.stack(part, axis=2) for part in whole], axis=3)
        whole = whole.transpose(1, 2, 0, 3, 4).reshape(rows, 3, ff).astype(f32)
        grad_gate_up, grad_down = whole[:, :2].reshape(rows, 2 * ff), whole[:, 2]
        grad_attention = attention_sums.reshape(n, rows, 3, lanes).transpose(1, 2, 0, 3)
        grad_attention = grad_attention.reshape(rows, 3 * d).astype(f32)
    return (
        output,
        grad_input,
        grad_attention,
        after(grad_output_weight, grad_attention).transpose(1, 0, 2).reshape(rows, d).astype(f32),
        grad_gate_up,
        grad_down,
        gains[:, 0],
        gains[:, 1],
    )


def solution(mesh):
    plane = Plane(mesh.shape["ctx"])
    return jax.shard_map(
        functools.partial(on_device, plane),
        mesh=mesh,
        in_specs=(
            P("fsdp", "ctx", None),
            P("fsdp", None),
            P(),
            P("fsdp", None),
            P("fsdp", None),
            P(),
            P("fsdp", None),
            P("fsdp", None),
            P("fsdp", "ctx", None),
        ),
        out_specs=(
            P("fsdp", "ctx", None),
            P("fsdp", "ctx", None),
            P(("ctx", "fsdp"), None),
            P(("ctx", "fsdp"), None),
            P(("ctx", "fsdp"), None),
            P(("ctx", "fsdp"), None),
            P(("ctx", "fsdp")),
            P(("ctx", "fsdp")),
        ),
        check_vma=False,
    )
```
